32 devices in a mesh: section: 2 (over x), dp: 16 (over z, y, core).
Axes of the slice: x: 2, y: 2, z: 4, core: 2. Of those that a mesh axis runs over, the one named last changes fastest.
Arguments:
- layer_ends: bfloat16 [2, 32768, 768], P('section', 'dp'), may hold values from -6 to 6
- doc_lengths: int32 [32, 4], P('dp'), may hold values from 1 to 512, 1024 in all within a row
- wide_master: float32 [2, 768, 3072], P('section', None, 'dp'), may hold values from -0.21875 to 0.21875
- wide_moment: float32 [2, 768, 3072], P('section', None, 'dp'), may hold values from -0.00024414062 to 0.00024414062
- wide_square: float32 [2, 768, 3072], P('section', None, 'dp'), may hold values from 7.047431e-10 to 1.12758896e-08
- down_master: float32 [3072, 768], P(('section', 'dp')), may hold values from -0.109375 to 0.109375
- down_moment: float32 [3072, 768], P(('section', 'dp')), may hold values from -0.00024414062 to 0.00024414062
- down_square: float32 [3072, 768], P(('section', 'dp')), may hold values from 7.047431e-10 to 1.12758896e-08
- small_master: float32 [16896], replicated, as said below
- small_moment: float32 [16896], replicated, may hold values from -0.00024414062 to 0.00024414062
- small_square: float32 [16896], replicated, may hold values from 7.047431e-10 to 1.12758896e-08
Outputs:
- layer_results: float32 [2, 32768, 768], P('section', 'dp')
- wide_momenta: float32 [2, 768, 3072], P('section', None, 'dp')
- wide_squares: float32 [2, 768, 3072], P('section', None, 'dp')
- wide_updated: float32 [2, 768, 3072], P('section', None, 'dp')
- down_momenta: float32 [3072, 768], P(('section', 'dp'))
- down_squares: float32 [3072, 768], P(('section', 'dp'))
- down_updated: float32 [3072, 768], P(('section', 'dp'))
- small_momenta: float32 [16896], replicated
- small_squares: float32 [16896], replicated
- small_updated: float32 [16896], replicated
- grad_norm: float32 [], replicated
The draws below stay inside these ranges and needn't reach their ends.
Inputs may be any that keep to these rules, and one draw needn't show every extreme that they name: `doc_lengths`: each sequence's 4 lengths sum to 1024; its longest document has exactly 512 tokens. `small_master`: gains of order one, biases of both signs.
All inputs are finite; a program needn't handle non-finite values.
Results may differ from the reference program's by a relative error of at most 0.009.
Values may be sent and summed in bfloat16 or wider, within the bound.
No kernel may reach another device: no remote copies, remote signals or barrier semaphores. Data moves between devices by JAX's collectives and lax.ppermute only.
A program may use at most 256 MiB of HBM per device.

```python
import math
import jax
import jax.numpy as jnp
import numpy as np
from jax import lax

D = 768
FF = 3072
HEADS = 12
HEAD_DIM = 64
L = 1024
DOCS = 4
STEP = 8
ROWS = 32
TOKENS = 32768
SMALL = 16896
PARAMS = 7094784


def rising_gains(subkey, count, low_end, high_end):
    fraction = jnp.arange(count, dtype=jnp.float32) / (count - 1)
    baseline = low_end * (high_end / low_end) ** fraction
    return baseline * jax.random.uniform(subkey, (count,), jnp.float32, 0.75, 1.33)


def draw_small_master(key, part):
    key = jax.random.fold_in(key, 11)
    subkeys = jax.random.split(key, 13)
    low_end, high_end = (0.6, 1.8)
    gain_flags = [1, 0, 0, 0, 1, 0, 0, 1, 0, 0, 1, 0, 0]
    widths = [D] * 9 + [FF] * 3 + [D]
    pieces = []
    for piece_index in range(13):
        subkey = subkeys[piece_index]
        if gain_flags[piece_index] == 1:
            pieces.append(rising_gains(subkey, widths[piece_index], low_end, high_end))
        else:
            pieces.append(0.3 * jax.random.normal(subkey, (widths[piece_index],), jnp.float32))
    return jnp.concatenate(pieces).astype(jnp.float32)


def block_scale(rng, dims, shards, smallest, high):
    level, own = 1.0, jax.random.fold_in(rng, 6)
    for dim, shards_of in shards:
        draws = jnp.exp(jax.random.uniform(jax.random.fold_in(own, dim), (shards_of,), jnp.float32, smallest / len(shards), high / len(shards)))
        level = level * jnp.repeat(draws, dims[dim] // shards_of).reshape([-1 if axis == dim else 1 for axis in range(len(dims))])
    return level


def profile(number_of, total, reach, lean):
    loads = [(1 << 20) // math.isqrt(rank ** lean) + 1 for rank in range(2, number_of + 1)]
    rest, holding = total - reach - (number_of - 1), [1] * (number_of - 1)
    while rest > 0:
        movable = [i for i in range(number_of - 1) if holding[i] < reach]
        whole, budget = sum([loads[i] for i in movable]), rest
        for i in movable:
            extra = min(reach - holding[i], max(1, budget * loads[i] // whole), rest)
            holding[i] = holding[i] + extra
            rest = rest - extra
    return np.array([reach] + holding)


def uneven_parts(own_key, count, total, limit, lean):
    if count == 2:
        one = jax.random.randint(own_key, (), max(1, total - limit), min(limit, total - 1) + 1)
        return jnp.stack([one, total - one])
    tallies = jnp.asarray(profile(count, total, limit, lean), jnp.int32)
    pairs = (count - 1) // 2
    giver, taker = tallies[1:1 + 2 * pairs:2], tallies[2:2 + 2 * pairs:2]
    room = jnp.minimum(giver - 1, limit - taker)
    passed = jax.random.randint(jax.random.fold_in(own_key, 1), (pairs,), 0, 1 << 20) % (room + 1)
    tallies = tallies.at[1:1 + 2 * pairs:2].set(giver - passed).at[2:2 + 2 * pairs:2].set(taker + passed)
    return tallies[jax.random.permutation(jax.random.fold_in(own_key, 2), count)]


def gaussian(key, dims, scale, bound, cuts=(), kind=jnp.bfloat16):
    drawn = jax.random.normal(key, dims, jnp.float32) * scale
    if len(cuts) > 0:
        drawn = block_scale(key, dims, cuts, -0.22, 0.18) * drawn
    return jnp.clip(drawn, min=-bound, max=bound).astype(kind)


def setup_inputs(seed: int = 0) -> dict:
    splits = jax.random.split(jax.random.key(seed), 12)
    return {
        "layer_ends": gaussian(splits[0], (2, TOKENS, D), 1.0, 6.0, ((0, 2), (1, 16))),
        "doc_lengths": jax.vmap(lambda own: uneven_parts(own, DOCS, L, L // 2, 2))(jax.random.split(splits[1], ROWS)).reshape((ROWS, DOCS)).astype(jnp.int32),
        "wide_master": gaussian(splits[2], (2, D, 4 * D), D ** -0.5, 0.21875, ((0, 2), (2, 16)), jnp.float32),
        "wide_moment": gaussian(splits[3], (2, D, 4 * D), (0.111 * PARAMS ** -0.5), 0.00024414062, ((0, 2), (2, 16)), jnp.float32),
        "wide_square": jnp.clip(jnp.exp(math.log(1.1275889555406593e-08) - 2.7725887 * jax.random.uniform(splits[4], (2, D, 4 * D), jnp.float32) ** block_scale(splits[4], (2, D, 4 * D), ((0, 2), (2, 16)), -0.2, 0.2)), 7.047430972129121e-10, 1.1275889555406593e-08),
        "down_master": gaussian(splits[5], (FF, D), FF ** -0.5, 0.109375, ((0, 32),), jnp.float32),
        "down_moment": gaussian(splits[6], (FF, D), (0.111 * PARAMS ** -0.5), 0.00024414062, ((0, 32),), jnp.float32),
        "down_square": jnp.clip(jnp.exp(math.log(1.1275889555406593e-08) - 2.7725887 * jax.random.uniform(splits[7], (FF, D), jnp.float32) ** block_scale(splits[7], (FF, D), ((0, 32),), -0.2, 0.2)), 7.047430972129121e-10, 1.1275889555406593e-08),
        "small_master": draw_small_master(jax.random.fold_in(splits[11], 71), 0),
        "small_moment": gaussian(splits[9], (SMALL,), (0.111 * PARAMS ** -0.5), 0.00024414062, (), jnp.float32),
        "small_square": jnp.clip(jnp.exp(jax.random.uniform(splits[10], (SMALL,), jnp.float32, math.log(7.047430972129121e-10), math.log(1.1275889555406593e-08))), 7.047430972129121e-10, 1.1275889555406593e-08),
    }


@jax.custom_vjp
def low(v):
    return lax.optimization_barrier(v.astype(jnp.bfloat16)).astype(jnp.float32)

@jax.custom_vjp
def low_back(v):
    return v

def low_keep(v):
    return (low(v), None)

def low_pass(kept, grad):
    return (grad,)

def back_keep(v):
    return (v, None)

def back_low(kept, grad):
    return (low(grad),)
low.defvjp(low_keep, low_pass)
low_back.defvjp(back_keep, back_low)
eps_norm = 1e-05
clip_limit = 1.0
beta_one = 0.9
beta_two = 0.99
adam_eps = 1e-08
decay_weight = 0.1
rate_wide = 0.05
rate_down = 0.025
rate_small = 0.6
masked_score = -1e+30
highest = lax.Precision.HIGHEST

def matmul(left, right):
    return jnp.dot(left, right, precision=highest, preferred_element_type=jnp.float32)

def layer_norm(values, norm_gain, norm_bias):
    row_mean = lax.optimization_barrier(jnp.mean(values, axis=-1, keepdims=True))
    centred = values - row_mean
    spread = lax.optimization_barrier(jnp.mean(centred * centred, axis=-1, keepdims=True))
    return centred * lax.rsqrt(spread + eps_norm) * norm_gain + norm_bias

def split_small(small_vector):
    piece_sizes = [D] * 9 + [FF] * 3 + [D]
    pieces = []
    offset = 0
    for piece_width in piece_sizes:
        pieces.append(small_vector[offset:offset + piece_width])
        offset = offset + piece_width
    return pieces

def segment_rows(lengths):
    doc_ends = jnp.cumsum(lengths, axis=-1)
    places = jnp.arange(L, dtype=jnp.int32)
    return lax.optimization_barrier(jnp.sum((places[None, :, None] >= doc_ends[:, None, :]).astype(jnp.int32), axis=-1)).astype(jnp.int32)

def row_attention(row_args):
    query_heads, key_heads, value_heads, segments = row_args
    scores = jnp.einsum('qhd,khd->hqk', query_heads, key_heads, precision=highest) * HEAD_DIM ** (-0.5)
    scores = low_back(scores)
    positions = jnp.arange(L)
    allowed = (segments[:, None] == segments[None, :]) & (positions[:, None] >= positions[None, :])
    masked = jnp.where(allowed[None], scores, masked_score)
    probs = low(jax.nn.softmax(masked, axis=-1))
    return jnp.einsum('hqk,khd->qhd', probs, value_heads, precision=highest).reshape(L, D)

def forward(inputs, wide_weights, down_weights, small_vector, lengths):
    gain_one, bias_one, bias_query, bias_value, inner_gain, inner_bias, bias_out, gain_two, bias_two, bias_hidden, hidden_gain, hidden_bias, bias_down = split_small(small_vector)
    group_rows = inputs.shape[0]
    attn_weights = low(wide_weights[0])
    first_weights = low(wide_weights[1])
    second_weights = low(down_weights)
    flat_inputs = inputs.reshape(-1, D)
    normed = low(layer_norm(flat_inputs, gain_one, bias_one))
    qkv_bias = jnp.concatenate([bias_query, jnp.zeros((D,), jnp.float32), bias_value])
    qkv_rows = low(low_back(matmul(normed, attn_weights[:, :3 * D]) + qkv_bias))
    qkv_rows = qkv_rows.reshape(group_rows, L, 3, HEADS, HEAD_DIM)
    segments = segment_rows(lengths)
    attended = lax.map(jax.checkpoint(row_attention), (qkv_rows[:, :, 0], qkv_rows[:, :, 1], qkv_rows[:, :, 2], segments))
    attended = low_back(attended.reshape(-1, D))
    inner_low = low(layer_norm(attended, inner_gain, inner_bias))
    residual = flat_inputs + matmul(inner_low, attn_weights[:, 3 * D:]) + bias_out
    residual = low(low_back(residual))
    second_normed = low(layer_norm(residual, gain_two, bias_two))
    hidden_pre = low_back(matmul(second_normed, first_weights) + bias_hidden)
    hidden_norm = low(layer_norm(jax.nn.gelu(hidden_pre, approximate=False), hidden_gain, hidden_bias))
    outputs = residual + matmul(hidden_norm, second_weights) + bias_down
    return outputs.reshape(group_rows, L, D)

def adamw(master, moment, square, clipped, step_rate, decay):
    moment_new = beta_one * moment + (1.0 - beta_one) * clipped
    square_new = beta_two * square + (1.0 - beta_two) * clipped * clipped
    moment_hat = moment_new / (1.0 - beta_one ** STEP)
    square_hat = square_new / (1.0 - beta_two ** STEP)
    master_new = master - step_rate * (moment_hat / (jnp.sqrt(square_hat) + adam_eps) + decay * master)
    return (moment_new, square_new, master_new)

def reference(layer_ends, doc_lengths, wide_master, wide_moment, wide_square, down_master, down_moment, down_square, small_master, small_moment, small_square):
    inputs = layer_ends[0].astype(jnp.float32)
    cotangent = layer_ends[1].astype(jnp.float32)
    group_rows = math.gcd(ROWS, max(1, 4096 // L))
    group_count = ROWS // group_rows

    def scan_step(grad_sums, group_item):
        input_rows, cotan_rows, length_rows = group_item

        def layer_fn(input_values, wide_values, down_values, small_values):
            return forward(input_values, wide_values, down_values, small_values, length_rows)
        output_rows, pullback = jax.vjp(layer_fn, input_rows, wide_master, down_master, small_master)
        grad_inputs, grad_wide, grad_down, grad_small = pullback(cotan_rows)
        grad_sums = (grad_sums[0] + grad_wide, grad_sums[1] + grad_down, grad_sums[2] + grad_small)
        return (grad_sums, (output_rows, grad_inputs))
    zero_grads = (jnp.zeros_like(wide_master), jnp.zeros_like(down_master), jnp.zeros_like(small_master))
    grad_sums, (output_rows, grad_rows) = lax.scan(scan_step, zero_grads, (inputs.reshape(group_count, group_rows, L, D), cotangent.reshape(group_count, group_rows, L, D), doc_lengths.reshape(group_count, group_rows, DOCS)))
    layer_results = jnp.stack([grad_rows.reshape(TOKENS, D), output_rows.reshape(TOKENS, D)])
    grad_wide, grad_down, grad_small = grad_sums
    squared = jnp.sum(grad_wide * grad_wide) + jnp.sum(grad_down * grad_down) + jnp.sum(grad_small * grad_small)
    grad_norm = jnp.sqrt(squared)
    factor = clip_limit / jnp.maximum(grad_norm, clip_limit)
    wide_momenta, wide_squares, wide_updated = adamw(wide_master, wide_moment, wide_square, grad_wide * factor, rate_wide, decay_weight)
    down_momenta, down_squares, down_updated = adamw(down_master, down_moment, down_square, grad_down * factor, rate_down, decay_weight)
    small_momenta, small_squares, small_updated = adamw(small_master, small_moment, small_square, grad_small * factor, rate_small, 0.0)
    return (layer_results, wide_momenta, wide_squares, wide_updated, down_momenta, down_squares, down_updated, small_momenta, small_squares, small_updated, grad_norm)
```

```python
import functools

import jax
import jax.numpy as jnp
import numpy as np
from jax import lax
from jax.experimental import pallas as pl
from jax.experimental.pallas import tpu as pltpu
from jax.sharding import PartitionSpec as P

D = 768
FF = 3072
HEADS = 12
HEAD_DIM = 64
PAIRS = HEADS // 2
L = 1024
BLOCK = 256
TILES = L // BLOCK
STEP = 8
CHUNK = 512
WIDE_TILE = 512
FFN_TILE = 256
SMALL_AT = {}
offset = 0
for name, width in (
    ("g1", D), ("b1", D), ("bq", D), ("bv", D), ("gi", D), ("bi", D), ("bo", D), ("g2", D), ("b2", D),
    ("c1", FF), ("gh", FF), ("bh", FF), ("c2", D),
):
    SMALL_AT[name] = (offset, width)
    offset += width
SMALL = offset

eps_norm = 1e-05
clip_limit = 1.0
beta_one = 0.9
beta_two = 0.99
adam_eps = 1e-08
decay_weight = 0.1
rate_wide = 0.05
rate_down = 0.025
rate_small = 0.6
masked_score = -1e30

BOTH = ("section", "dp")
F32 = jnp.float32
BF16 = jnp.bfloat16
NN = ((1,), (0,))
NT = ((1,), (1,))
TN = ((0,), (0,))
VMEM_BYTES = 58 * 2**20


def dot(a, b, dims):
    return lax.dot_general(a, b, (dims, ((), ())), preferred_element_type=F32)


def small_row(small_ref, name, start=0, width=None):
    at, full = SMALL_AT[name]
    return small_ref[:, at + start : at + start + (full if width is None else width)]


def normalise(values):
    row_mean = jnp.mean(values, axis=-1, keepdims=True)
    centred = values - row_mean
    spread = jnp.mean(centred * centred, axis=-1, keepdims=True)
    inverse = lax.rsqrt(spread + eps_norm)
    return centred * inverse, inverse


def normalise_back(grad, gain, unit, inverse):
    scaled = grad * gain
    first = jnp.mean(scaled, axis=-1, keepdims=True)
    second = jnp.mean(scaled * unit, axis=-1, keepdims=True)
    return inverse * (scaled - first - unit * second)


def column_sum(values):
    return jnp.sum(values, axis=0, keepdims=True)


def visible_bias(ends_ref, query_start, key_start, keys):
    key = key_start + lax.broadcasted_iota(jnp.int32, (keys, BLOCK), 0)
    query = query_start + lax.broadcasted_iota(jnp.int32, (1, BLOCK), 1)
    begin = jnp.zeros((1, BLOCK), jnp.int32)
    for i in range(3):
        end = ends_ref[i]
        begin = jnp.where(query >= end, end, begin)
    return jnp.where((key >= begin) & (key <= query), 0.0, masked_score).astype(F32)


def halves(pair):
    lane = lax.broadcasted_iota(jnp.int32, pair.shape, 1)
    zero = jnp.zeros_like(pair)
    return jnp.where(lane < HEAD_DIM, pair, zero), jnp.where(lane < HEAD_DIM, zero, pair)


def first_key(tile):
    return max(0, tile - 2) * BLOCK


def attention_kernel(groups, first_ref, ends_ref, table_ref, own_ref, swapped_ref, small_ref, *refs):
    slots, refs = refs[: len(groups)], refs[len(groups) :]
    qkv_ref, o_ref, stats_ref, hs_ref, pair_ref, held_ref, *refs = refs
    bias_ref, vt_ref, weights_ref, x_ref, a_ref, sem, x_sem, out_sem = refs

    @pl.when(first_ref[0] == 1)
    def _():
        pltpu.make_async_copy(own_ref.at[pl.ds(0, L)], x_ref, x_sem).start()

    @pl.when(first_ref[0] == 0)
    def _():
        pltpu.make_async_copy(swapped_ref, x_ref, x_sem).start()

    copies = []
    for at, (group, rows, count) in enumerate(groups):
        for slot in range(count):
            target = pl.multiple_of(table_ref[at, slot], 16)
            copies.append(
                pltpu.make_async_copy(
                    slots[at].at[slot], weights_ref.at[pl.ds(target, rows)], sem
                )
            )
    for copy in copies:
        copy.start()
    for copy in copies:
        copy.wait()
    hold = pltpu.make_async_copy(weights_ref, held_ref, out_sem.at[0])
    hold.start()
    pltpu.make_async_copy(swapped_ref, x_ref, x_sem).wait()

    def project(tile, carry):
        rows = pl.ds(pl.multiple_of(tile * WIDE_TILE, WIDE_TILE), WIDE_TILE)
        unit, _ = normalise(x_ref[rows, :].astype(F32))
        a = (unit * small_row(small_ref, "g1") + small_row(small_ref, "b1")).astype(BF16)
        a_ref[rows, :] = a
        q = (dot(a, weights_ref[:D, :], NT) + small_row(small_ref, "bq")).astype(BF16)
        qkv_ref[rows, :D] = q * jnp.asarray(0.125, BF16)
        qkv_ref[rows, D : 2 * D] = dot(a, weights_ref[D : 2 * D, :], NT).astype(BF16)
        v = (dot(a, weights_ref[2 * D : 3 * D, :], NT) + small_row(small_ref, "bv")).astype(BF16)
        qkv_ref[rows, 2 * D :] = v
        vt_ref[:, rows] = v.T
        return carry

    lax.fori_loop(0, L // WIDE_TILE, project, 0)
    hold_a = pltpu.make_async_copy(a_ref, pair_ref.at[0], out_sem.at[1])
    hold_a.start()

    for tile in range(TILES):
        start = first_key(tile)
        keys = (tile + 1) * BLOCK - start
        rows = slice(tile * BLOCK, (tile + 1) * BLOCK)
        window = slice(start, start + keys)
        bias_ref[:keys, :] = visible_bias(ends_ref, tile * BLOCK, start, keys)

        def one_pair(pair, carry, rows=rows, window=window, keys=keys):
            at = pl.multiple_of(pair * 128, 128)
            q_parts = halves(qkv_ref[rows, pl.ds(at, 128)])
            k = qkv_ref[window, pl.ds(D + at, 128)]
            vt = vt_ref[pl.ds(at, 128), window]
            weights, tops = [], []
            for q_part in q_parts:
                scores = dot(k, q_part, NT) + bias_ref[:keys, :]
                top = jnp.max(scores, axis=0, keepdims=True)
                weights.append(jnp.exp(scores - top).astype(BF16))
                tops.append(top)
            ones = jnp.ones((16, keys), BF16)
            outs = []
            for i in range(2):
                left = jnp.concatenate([vt[i * HEAD_DIM : (i + 1) * HEAD_DIM], ones], axis=0)
                mixed = dot(left, weights[i], NN)
                total = mixed[HEAD_DIM : HEAD_DIM + 1, :]
                outs.append(mixed[:HEAD_DIM, :] / total)
                stats_ref[pair, i : i + 1, rows] = tops[i] + jnp.log(total)
            o_ref[rows, pl.ds(at, 128)] = jnp.concatenate(outs, axis=0).T
            return carry

        lax.fori_loop(0, PAIRS, one_pair, 0, unroll=2)

    def finish(tile, carry):
        rows = pl.ds(pl.multiple_of(tile * WIDE_TILE, WIDE_TILE), WIDE_TILE)
        unit, _ = normalise(o_ref[rows, :])
        u = (unit * small_row(small_ref, "gi") + small_row(small_ref, "bi")).astype(BF16)
        h = x_ref[rows, :].astype(F32) + dot(u, weights_ref[3 * D :, :], NT)
        hs_ref[rows, :] = (h + small_row(small_ref, "bo")).astype(BF16)
        return carry

    lax.fori_loop(0, L // WIDE_TILE, finish, 0)
    hold.wait()
    hold_a.wait()


def whole(memory_space=pltpu.VMEM):
    return pl.BlockSpec(memory_space=memory_space)


def beside(kernel, inputs, outputs, waits, carried):
    def body(*refs):
        passed = len(waits) + len(carried)
        after_inputs = refs[inputs + passed :]
        kernel(*refs[:inputs], *after_inputs[:outputs], *after_inputs[outputs + len(carried) :])

    return body


def shapes_of(arrays):
    return tuple(jax.ShapeDtypeStruct(a.shape, a.dtype) for a in arrays)


def attention_forward(first, ends, table, ends_in, swapped, small, slots, groups):
    return pl.pallas_call(
        functools.partial(attention_kernel, groups),
        out_shape=(
            jax.ShapeDtypeStruct((L, 3 * D), BF16),
            jax.ShapeDtypeStruct((L, D), F32),
            jax.ShapeDtypeStruct((PAIRS, 2, L), F32),
            jax.ShapeDtypeStruct((L, D), BF16),
            jax.ShapeDtypeStruct((2, L, D), BF16),
            jax.ShapeDtypeStruct((FF, D), BF16),
        ),
        in_specs=[whole(pltpu.SMEM)] * 3 + [whole(pl.ANY)] * 2 + [whole()]
        + [whole(pl.ANY)] * len(slots),
        out_specs=(whole(),) * 4 + (whole(pl.ANY),) * 2,
        scratch_shapes=[
            pltpu.VMEM((3 * BLOCK, BLOCK), F32),
            pltpu.VMEM((D, L), BF16),
            pltpu.VMEM((FF, D), BF16),
            pltpu.VMEM((L, D), BF16),
            pltpu.VMEM((L, D), BF16),
            pltpu.SemaphoreType.DMA,
            pltpu.SemaphoreType.DMA,
            pltpu.SemaphoreType.DMA((2,)),
        ],
        compiler_params=pltpu.CompilerParams(vmem_limit_bytes=VMEM_BYTES),
        cost_estimate=pl.CostEstimate(flops=14 * 10**9, bytes_accessed=20 * 10**6, transcendentals=0),
        name="attention_forward",
    )(first, ends, table, ends_in, swapped, small, *slots)


def gelu_parts(x):
    size = jnp.abs(x)
    bell = jnp.exp(x * x * -0.5)
    t = 1.0 / (1.0 + size * (0.3275911 * 0.5**0.5))
    tail = t * (0.5 * 0.254829592 + t * (0.5 * -0.284496736 + t * (
        0.5 * 1.421413741 + t * (0.5 * -1.453152027 + t * (0.5 * 1.061405429)))))
    tail = tail * bell
    phi = jnp.where(x > 0, 1.0 - tail, tail)
    return x * phi, phi + x * bell * 0.3989422804014327


def ffn_kernel(
    places, chosen_ref, hs_ref, lower_ref, swapped_ref, small_ref, slots_ref,
    y_ref, sent_ref, pair_ref, turned_ref, dhs_ref, wide_ref,
    g_ref, slope_ref, t_ref, held_ref, first_ref, second_ref, sems,
):
    first_rows, second_rows, rows = places

    def weight_copies(into_ref, rows_of, start, sem):
        return [
            pltpu.make_async_copy(
                slots_ref.at[block, pl.ds(start, rows)], into_ref.at[pl.ds(row, rows)], sem
            )
            for block, row in enumerate(rows_of)
        ]

    @pl.when(pl.program_id(0) == 0)
    def _():
        wide_ref[...] = jnp.zeros_like(wide_ref)
        copies = weight_copies(first_ref, first_rows, 0, sems.at[0])
        for copy in copies + weight_copies(second_ref, second_rows, rows, sems.at[1]):
            copy.start()
        for copy in copies:
            copy.wait()

    hs = hs_ref[...].astype(F32)
    unit, inverse = normalise(hs)
    e = (unit * small_row(small_ref, "g2") + small_row(small_ref, "b2")).astype(BF16)
    pair_ref[0] = e
    dy = jnp.where(chosen_ref[0] == 1, swapped_ref[...], lower_ref[...])
    pair_ref[1] = dy
    chunks = [slice(j, j + CHUNK) for j in range(0, FF, CHUNK)]

    total = jnp.zeros((FFN_TILE, 1), F32)
    for cut in chunks:
        f = dot(e, first_ref[cut, :], NT) + small_row(small_ref, "c1", cut.start, CHUNK)
        g, slope = gelu_parts(f)
        g_ref[:, cut] = g
        slope_ref[:, cut] = slope
        total = total + jnp.sum(g, axis=1, keepdims=True)
    mean = total / FF
    total = jnp.zeros((FFN_TILE, 1), F32)
    for cut in chunks:
        centred = g_ref[:, cut] - mean
        total = total + jnp.sum(centred * centred, axis=1, keepdims=True)
    inner_inverse = lax.rsqrt(total / FF + eps_norm)

    step = pl.program_id(0)
    columns = pl.ds(pl.multiple_of(step * FFN_TILE, FFN_TILE), FFN_TILE)
    flush = pltpu.make_async_copy(held_ref, turned_ref.at[:, :, columns], sems.at[2])

    @pl.when(step == 0)
    def _():
        for copy in weight_copies(second_ref, second_rows, rows, sems.at[1]):
            copy.wait()

    @pl.when(step > 0)
    def _():
        flush.wait()

    y = hs + small_row(small_ref, "c2")
    first_sum = jnp.zeros((FFN_TILE, 1), F32)
    second_sum = jnp.zeros((FFN_TILE, 1), F32)
    for cut in chunks:
        gain = small_row(small_ref, "gh", cut.start, CHUNK)
        ghat = (g_ref[:, cut] - mean) * inner_inverse
        g_ref[:, cut] = ghat
        n = (ghat * gain + small_row(small_ref, "bh", cut.start, CHUNK)).astype(BF16)
        held_ref[1, cut, :] = n.T
        y = y + dot(n, second_ref[cut, :], NN)
        dn = dot(dy, second_ref[cut, :], NT)
        wide_ref[0:1, cut] += column_sum(dn * ghat)
        wide_ref[1:2, cut] += column_sum(dn)
        scaled = dn * gain
        t_ref[:, cut] = scaled
        first_sum = first_sum + jnp.sum(scaled, axis=1, keepdims=True)
        second_sum = second_sum + jnp.sum(scaled * ghat, axis=1, keepdims=True)
    y_ref[...] = y
    sent_ref[...] = y.astype(BF16)
    first_sum = first_sum / FF
    second_sum = second_sum / FF

    de = jnp.zeros((FFN_TILE, D), F32)
    for cut in chunks:
        back = t_ref[:, cut] - first_sum - g_ref[:, cut] * second_sum
        df = (inner_inverse * back * slope_ref[:, cut]).astype(BF16)
        held_ref[0, cut, :] = df.T
        wide_ref[2:3, cut] += column_sum(df.astype(F32))
        de = de + dot(df, first_ref[cut, :], NN)
    flush.start()

    dyf = dy.astype(F32)
    wide_ref[3:4, :D] += column_sum(de * unit)
    wide_ref[3:4, D : 2 * D] += column_sum(de)
    wide_ref[3:4, 2 * D : 3 * D] += column_sum(dyf)
    dhp = normalise_back(de, small_row(small_ref, "g2"), unit, inverse)
    dhs_ref[...] = (dyf + dhp).astype(BF16)

    @pl.when(step == pl.num_programs(0) - 1)
    def _():
        flush.wait()


def feed_forward(chosen, hs, ends_in, swapped, small, slots, places):
    at = L // FFN_TILE
    tile = lambda shift=0: pl.BlockSpec((FFN_TILE, D), lambda i: (i + shift, 0))
    keep = lambda shape: pl.BlockSpec(shape, lambda i: (0, 0), pipeline_mode=pl.Buffered(1))
    return pl.pallas_call(
        functools.partial(ffn_kernel, places),
        grid=(at,),
        out_shape=(
            jax.ShapeDtypeStruct((2 * L, D), F32),
            jax.ShapeDtypeStruct((L, D), BF16),
            jax.ShapeDtypeStruct((2, L, D), BF16),
            jax.ShapeDtypeStruct((2, FF, L), BF16),
            jax.ShapeDtypeStruct((L, D), BF16),
            jax.ShapeDtypeStruct((4, FF), F32),
        ),
        in_specs=[whole(pltpu.SMEM), tile(), tile(at), tile(), keep((1, SMALL)), whole(pl.ANY)],
        out_specs=(
            tile(at), tile(),
            pl.BlockSpec((2, FFN_TILE, D), lambda i: (0, i, 0)),
            whole(pl.ANY),
            tile(),
            pl.BlockSpec((4, FF), lambda i: (0, 0)),
        ),
        scratch_shapes=[pltpu.VMEM((FFN_TILE, FF), F32)] * 3
        + [pltpu.VMEM((2, FF, FFN_TILE), BF16)]
        + [pltpu.VMEM((FF, D), BF16)] * 2
        + [pltpu.SemaphoreType.DMA((3,))],
        compiler_params=pltpu.CompilerParams(vmem_limit_bytes=VMEM_BYTES),
        cost_estimate=pl.CostEstimate(flops=40 * 10**9, bytes_accessed=30 * 10**6, transcendentals=0),
        name="feed_forward",
    )(chosen, hs, ends_in, swapped, small, slots)


TOKEN = jax.ShapeDtypeStruct((8, 128), F32)


def weight_grad_kernel(plan, me_ref, *refs):
    lefts, right_ref = refs[: plan["lefts"]], refs[plan["lefts"]]
    refs = refs[plan["lefts"] + 1 :]
    moved, outs, token_ref = refs[: plan["moved"]], refs[plan["moved"] : -1], refs[-1]
    rows = lefts[0].shape[1]
    blocks = [ref[0] for ref in lefts]
    token_ref[...] = jnp.zeros_like(token_ref)
    if rows % 16 == 0:
        value = dot(jnp.concatenate(blocks, axis=0), right_ref[0], NN)
        parts = [value[at * rows : (at + 1) * rows] for at in range(len(blocks))]
    else:
        parts = [dot(block, right_ref[0], NN) for block in blocks]
    split = plan["split"]
    step = pl.program_id(0) % 2**split
    kind = pl.program_id(0) // 2**split

    def store(group, parts):
        views = plan["views"][group]
        for at, part in enumerate(parts):
            place = tuple(int(p) for p in np.unravel_index(at, views))
            if not moved:
                outs[group][place] = part.astype(BF16)
                continue
            total = part + moved[group][place].astype(F32)
            low_ref, high_ref = outs[2 * group : 2 * group + 2]
            first_bit = plan["first"][group]
            if first_bit is None:
                if place[0] == 0:
                    low_ref[place[1:]] = total
                else:
                    high_ref[place[1:]] = total.astype(BF16)
                continue

            @pl.when((step >> first_bit) & 1 == 0)
            def _():
                low_ref[place[1:]] = total

            @pl.when((step >> first_bit) & 1 == 1)
            def _():
                high_ref[place[1:]] = total.astype(BF16)

    if plan["joint"]:
        count = len(parts) // 2
        for group in range(2):
            store(group, parts[group * count : (group + 1) * count])
    else:
        for group in range(2):

            @pl.when(kind == group)
            def _():
                store(group, parts)


def weight_grad(me, left, count, right, groups, split, joint, right_of, moved, name, waits=()):
    bits = count.bit_length() - 1
    rows = left.shape[1]
    steps = 2**split
    top = [("dp", bits - 1 - i) for i in range(split)]
    shift = bits - split
    in_specs, outs, out_specs, views, firsts, combos = [], [], [], [], [], []
    moved_specs = []

    def row_of(group, combo, step, me_ref):
        order, row_block = groups[group]
        free = [pair for pair in order[1:] if pair not in top]
        apart, across = (0 if moved else 1), 0
        for at, (axis, bit) in enumerate(free):
            on = (combo >> (len(free) - 1 - at)) & 1
            if axis == "dp":
                apart |= on << bit
            else:
                across = on
        return row_block((apart + (step << shift)) ^ me_ref[0], across ^ me_ref[1])

    def local_step(i, group):
        if joint:
            return i
        return jnp.clip(i - group * steps, 0, steps - 1)

    free_count = 2 ** (len(groups[0][0]) - 1 - split)
    if joint:
        for group in range(2):
            for combo in range(free_count):
                in_specs.append(
                    pl.BlockSpec(
                        (1, rows, L),
                        lambda i, m, g=group, c=combo: (row_of(g, c, i, m), 0, 0),
                    )
                )
    else:
        for combo in range(free_count):

            def place(i, m, c=combo):
                step = i % steps
                return jnp.where(i < steps, row_of(0, c, step, m), row_of(1, c, step, m)), 0, 0

            in_specs.append(pl.BlockSpec((1, rows, L), place))
    lefts = len(in_specs)
    in_specs.append(pl.BlockSpec((1, L, D), lambda i, m: (right_of(i, m), 0, 0)))

    for group, (order, _) in enumerate(groups):
        order = order[1:]

        def spots(i, m, pairs=order, group=group):
            step = local_step(i, group)
            return (*[(step >> (p[1] - shift)) & 1 if p in top else 0 for p in pairs], 0, 0)

        view = tuple(1 if pair in top else 2 for pair in order)
        views.append(view)
        firsts.append(order[0][1] - shift if order[0] in top else None)
        full = pl.BlockSpec((*view, rows, D), spots)
        if moved:
            moved_specs.append(full)
            half = pl.BlockSpec(
                (*view[1:], rows, D), lambda i, m, spots=spots: spots(i, m)[1:]
            )
            out_specs += [half, half]
            shape = (2,) * (len(order) - 1) + (rows, D)
            outs += [jax.ShapeDtypeStruct(shape, F32), jax.ShapeDtypeStruct(shape, BF16)]
        else:
            out_specs.append(full)
            outs.append(jax.ShapeDtypeStruct((2,) * len(order) + (rows, D), BF16))
    plan = dict(
        lefts=lefts, moved=len(moved), split=split, views=views, first=firsts, joint=joint
    )
    moved = [m.reshape((2,) * (len(groups[0][0]) - 1) + (rows, D)) for m in moved]
    inputs = len(in_specs) + len(moved) + 1
    *results, token = pl.pallas_call(
        beside(functools.partial(weight_grad_kernel, plan), inputs, len(outs) + 1, waits, ()),
        grid_spec=pltpu.PrefetchScalarGridSpec(
            num_scalar_prefetch=1,
            grid=(steps if joint else 2 * steps,),
            in_specs=in_specs + moved_specs + [whole(pl.ANY)] * len(waits),
            out_specs=tuple(out_specs) + (pl.BlockSpec((8, 128), lambda i, m: (0, 0)),),
        ),
        out_shape=tuple(outs) + (TOKEN,),
        compiler_params=pltpu.CompilerParams(vmem_limit_bytes=VMEM_BYTES),
        cost_estimate=pl.CostEstimate(flops=6 * 10**9, bytes_accessed=9 * 10**6, transcendentals=0),
        name=name,
    )(me, *[left] * lefts, right, *moved, *waits)
    return [r.reshape(-1, rows, D) for r in results], token


def inner_back_kernel(
    dhs_ref, o_ref, small_ref, weights_ref, pair_ref, do_ref, delta_ref, turned_ref, u_ref, low_ref
):
    @pl.when(pl.program_id(0) == 0)
    def _():
        low_ref[...] = jnp.zeros_like(low_ref)

    o = o_ref[...]
    unit, inverse = normalise(o)
    gain = small_row(small_ref, "gi")
    u_ref[0] = (unit * gain + small_row(small_ref, "bi")).astype(BF16)
    dhs = dhs_ref[...]
    turned_ref[0] = dhs.T
    du = dot(dhs, weights_ref[...], NN)
    low_ref[4:5, :] += column_sum(du * unit)
    low_ref[5:6, :] += column_sum(du)
    low_ref[6:7, :] += column_sum(dhs.astype(F32))
    do = normalise_back(du, gain, unit, inverse).astype(BF16)
    do_ref[...] = do
    product = (do.astype(F32) * o).T
    for head in range(HEADS):
        delta_ref[head // 2, head % 2 : head % 2 + 1, :] = column_sum(
            product[head * HEAD_DIM : (head + 1) * HEAD_DIM, :]
        )


def inner_back(dhs, o, small, weights, pair, waits=()):
    tile = lambda width: pl.BlockSpec((BLOCK, width), lambda i: (i, 0))
    return pl.pallas_call(
        beside(inner_back_kernel, 5, 5, waits, ()),
        grid=(TILES,),
        out_shape=(
            jax.ShapeDtypeStruct((L, D), BF16),
            jax.ShapeDtypeStruct((PAIRS, 2, L), F32),
            jax.ShapeDtypeStruct((4, D, L), BF16),
            jax.ShapeDtypeStruct((2, L, D), BF16),
            jax.ShapeDtypeStruct((8, D), F32),
        ),
        in_specs=[
            tile(D),
            tile(D),
            pl.BlockSpec((1, SMALL), lambda i: (0, 0), pipeline_mode=pl.Buffered(1)),
            pl.BlockSpec((D, D), lambda i: (3, 0), pipeline_mode=pl.Buffered(1)),
            whole(pl.ANY),
        ]
        + [whole(pl.ANY)] * len(waits),
        out_specs=(
            tile(D),
            pl.BlockSpec((PAIRS, 2, BLOCK), lambda i: (0, 0, i)),
            pl.BlockSpec((1, D, BLOCK), lambda i: (3, 0, i)),
            pl.BlockSpec((1, BLOCK, D), lambda i: (1, i, 0)),
            pl.BlockSpec((8, D), lambda i: (0, 0)),
        ),
        input_output_aliases={4: 3},
        compiler_params=pltpu.CompilerParams(vmem_limit_bytes=VMEM_BYTES),
        cost_estimate=pl.CostEstimate(flops=6 * 10**9, bytes_accessed=15 * 10**6, transcendentals=0),
        name="inner_back",
    )(dhs, o, small, weights, pair, *waits)


GROUP = 3


def pair_back_kernel(
    ends_ref, q_ref, k_ref, v_ref, do_ref, stats_ref, delta_ref, earlier_ref,
    dq_ref, dk_ref, dv_ref, turned_ref, token_ref, bias_ref, dk_sum, dv_sum,
):
    token_ref[...] = jnp.zeros_like(token_ref)

    @pl.when(pl.program_id(0) == 0)
    def _():
        for tile in range(TILES):
            start = first_key(tile)
            keys = (tile + 1) * BLOCK - start
            bias_ref[tile, :keys, :] = visible_bias(ends_ref, tile * BLOCK, start, keys)

    dk_sum[...] = jnp.zeros_like(dk_sum)
    dv_sum[...] = jnp.zeros_like(dv_sum)
    for tile in range(TILES):
        start = first_key(tile)
        keys = (tile + 1) * BLOCK - start
        rows = slice(tile * BLOCK, (tile + 1) * BLOCK)
        window = slice(start, start + keys)
        q_parts = halves(q_ref[rows, :])
        do_parts = halves(do_ref[rows, :])
        k = k_ref[window, :]
        v = v_ref[window, :]
        kt = k.T
        dqs = []
        for i in range(2):
            scores = dot(k, q_parts[i], NT) + bias_ref[tile, :keys, :]
            probs = jnp.exp(scores - stats_ref[0, i : i + 1, rows])
            dprobs = dot(v, do_parts[i], NT)
            ds = (probs * (dprobs - delta_ref[0, i : i + 1, rows])).astype(BF16)
            dv_sum[window, :] += dot(probs.astype(BF16), do_parts[i], NN)
            dk_sum[window, :] += dot(ds, q_parts[i], NN)
            dqs.append(dot(kt[i * HEAD_DIM : (i + 1) * HEAD_DIM], ds, NN))
        dq = (jnp.concatenate(dqs, axis=0) * 0.125).astype(BF16)
        turned_ref[0, :, rows] = dq
        dq_ref[rows, :] = dq.T
    for part, sum_ref, out_ref in ((1, dk_sum, dk_ref), (2, dv_sum, dv_ref)):
        grad = sum_ref[...].astype(BF16)
        out_ref[...] = grad
        turned_ref[part] = grad.T


def pair_back(part, ends, qkv, do, stats, delta, turned, waits=()):
    first = part * GROUP
    column = lambda base: pl.BlockSpec((L, 128), lambda i: (0, base + first + i))
    rows = pl.BlockSpec((1, 2, L), lambda i: (first + i, 0, 0))
    out = pl.BlockSpec((L, 128), lambda i: (0, i))
    width = GROUP * 128
    return pl.pallas_call(
        beside(pair_back_kernel, 8, 5, waits, ()),
        grid=(GROUP,),
        out_shape=(jax.ShapeDtypeStruct((L, width), BF16),) * 3
        + (jax.ShapeDtypeStruct((4, D, L), BF16), TOKEN),
        in_specs=[
            whole(pltpu.SMEM), column(0), column(PAIRS), column(2 * PAIRS), column(0), rows, rows,
            whole(pl.ANY),
        ]
        + [whole(pl.ANY)] * len(waits),
        out_specs=(out,) * 3 + (
            pl.BlockSpec((3, 128, L), lambda i: (0, first + i, 0)),
            pl.BlockSpec((8, 128), lambda i: (0, 0)),
        ),
        input_output_aliases={7: 3},
        scratch_shapes=[
            pltpu.VMEM((TILES, 3 * BLOCK, BLOCK), F32),
            pltpu.VMEM((L, 128), F32),
            pltpu.VMEM((L, 128), F32),
        ],
        compiler_params=pltpu.CompilerParams(vmem_limit_bytes=VMEM_BYTES),
        cost_estimate=pl.CostEstimate(flops=13 * 10**9, bytes_accessed=15 * 10**6, transcendentals=0),
        name="pair_back",
    )(ends, qkv, qkv, qkv, do, stats, delta, turned, *waits)


def input_grad_kernel(
    first_ref, dq0, dk0, dv0, dq1, dk1, dv1, own_ref, swapped_ref, dhs_ref, small_ref, weights_ref,
    results_ref, earlier_ref, dx_ref, sent_ref, low_ref,
):
    @pl.when(pl.program_id(0) == 0)
    def _():
        low_ref[...] = earlier_ref[...]

    x = jnp.where(first_ref[0] == 1, own_ref[...], swapped_ref[...])
    unit, inverse = normalise(x.astype(F32))
    gain = small_row(small_ref, "g1")
    grads = [ref[...] for ref in (dq0, dq1, dk0, dk1, dv0, dv1)]
    width = GROUP * 128
    da = dot(jnp.concatenate(grads, axis=1), weights_ref[...], NN)
    for at, grad in enumerate(grads):
        if at < 2 or at > 3:
            row = 2 if at < 2 else 3
            cut = slice((at % 2) * width, (at % 2 + 1) * width)
            low_ref[row : row + 1, cut] += column_sum(grad.astype(F32))
    low_ref[0:1, :] += column_sum(da * unit)
    low_ref[1:2, :] += column_sum(da)
    dx = normalise_back(da, gain, unit, inverse) + dhs_ref[...].astype(F32)
    dx_ref[...] = dx
    sent_ref[...] = dx.astype(BF16)


def input_grad(part, first, grads, ends_in, swapped, dhs, small, weights, results, earlier, waits=()):
    tile = lambda width: pl.BlockSpec((BLOCK, width), lambda i: (i + 2 * part, 0))
    keep = lambda shape: pl.BlockSpec(shape, lambda i: (0, 0), pipeline_mode=pl.Buffered(1))
    return pl.pallas_call(
        beside(input_grad_kernel, 14, 3, waits, ()),
        grid=(TILES // 2,),
        out_shape=(
            jax.ShapeDtypeStruct((2 * L, D), F32),
            jax.ShapeDtypeStruct((L // 2, D), BF16),
            jax.ShapeDtypeStruct((8, D), F32),
        ),
        in_specs=[whole(pltpu.SMEM)] + [tile(GROUP * 128)] * 6
        + [tile(D)] * 3 + [keep((1, SMALL)), keep((3 * D, D))]
        + [whole(pl.ANY), keep((8, D))]
        + [whole(pl.ANY)] * len(waits),
        out_specs=(
            tile(D),
            pl.BlockSpec((BLOCK, D), lambda i: (i, 0)),
            pl.BlockSpec((8, D), lambda i: (0, 0)),
        ),
        input_output_aliases={12: 0},
        compiler_params=pltpu.CompilerParams(vmem_limit_bytes=VMEM_BYTES),
        cost_estimate=pl.CostEstimate(flops=4 * 10**9, bytes_accessed=10 * 10**6, transcendentals=0),
        name="input_grad",
    )(first, *grads, ends_in, swapped, dhs, small, weights, results, earlier, *waits)


def place_kernel(first_ref, y_ref, dx0_ref, dx1_ref, results_ref, out_ref, token_ref):
    token_ref[...] = jnp.zeros_like(token_ref)
    dx = jnp.where(pl.program_id(0) == 0, dx0_ref[...], dx1_ref[...])
    out_ref[...] = jnp.where(first_ref[0] == 1, dx, y_ref[...]).astype(F32)


def place_results(first, y, dx, results):
    tile = pl.BlockSpec((WIDE_TILE, D), lambda i, f: (i, 0))
    fixed = pl.BlockSpec((WIDE_TILE, D), lambda i, f: (0, 0))
    return pl.pallas_call(
        place_kernel,
        grid_spec=pltpu.PrefetchScalarGridSpec(
            num_scalar_prefetch=1,
            grid=(L // WIDE_TILE,),
            in_specs=[tile, fixed, fixed, whole(pl.ANY)],
            out_specs=(
                pl.BlockSpec((WIDE_TILE, D), lambda i, f: (i + f[0] * (L // WIDE_TILE), 0)),
                pl.BlockSpec((8, 128), lambda i, f: (0, 0)),
            ),
        ),
        out_shape=(jax.ShapeDtypeStruct((2 * L, D), F32), TOKEN),
        input_output_aliases={4: 0},
        cost_estimate=pl.CostEstimate(flops=10**6, bytes_accessed=8 * 10**6, transcendentals=0),
        name="place_results",
    )(first, y, *dx, results)


def combine_kernel(groups, *refs):
    inputs, outputs = refs[: 4 * groups], refs[4 * groups :]
    for g in range(groups):
        low, high, low_in, high_in = inputs[4 * g : 4 * g + 4]
        kept_ref, sent_ref = outputs[2 * g : 2 * g + 2]
        kept_ref[...] = low[...] + low_in[...].astype(F32)
        sent_ref[...] = (high[...] + high_in[...].astype(F32)).astype(BF16)


def combine(states, bits, waits=()):
    moved = [swap_bit(sent, *bit) for (_, sent), bit in zip(states, bits)]
    half = states[0][0].shape[0] // 2
    steps = min(half, 2)
    block = (half // steps,) + states[0][0].shape[1:]
    operands, in_specs, out_shape, out_specs = [], [], [], []
    lower = pl.BlockSpec(block, lambda i: (i, 0, 0))
    upper = pl.BlockSpec(block, lambda i: (i + steps, 0, 0))
    for (kept, _), other in zip(states, moved):
        operands += [kept, kept, other, other]
        in_specs += [lower, upper, lower, upper]
        shape = (half,) + kept.shape[1:]
        out_shape += [jax.ShapeDtypeStruct(shape, F32), jax.ShapeDtypeStruct(shape, BF16)]
        out_specs += [lower, lower]
    outs = pl.pallas_call(
        beside(
            functools.partial(combine_kernel, len(states)), len(operands), len(out_shape), waits, ()
        ),
        grid=(steps,),
        in_specs=in_specs + [whole(pl.ANY)] * len(waits),
        out_specs=tuple(out_specs),
        out_shape=tuple(out_shape),
        compiler_params=pltpu.CompilerParams(vmem_limit_bytes=VMEM_BYTES),
        cost_estimate=pl.CostEstimate(flops=10**6, bytes_accessed=8 * 10**6, transcendentals=0),
        name="combine",
    )(*operands, *waits)
    return [(outs[2 * g], outs[2 * g + 1]) for g in range(len(states))]


def owned_kernel(attn_ref, first_ref, down_ref, low_ref, early_ref, late_ref):
    total = jnp.zeros((1, 1), F32)
    for ref in (attn_ref, first_ref, down_ref):
        total = total + jnp.sum(column_sum(ref[...] * ref[...]), axis=1, keepdims=True)
    late_ref[...] = jnp.zeros_like(late_ref)
    late_ref[:7, :] = low_ref[:7, :]
    order = [(3, 0), (3, 1)] + [(row, part) for row in (2, 0, 1) for part in range(4)] + [(3, 2)]
    for at, (row, part) in enumerate(order):
        late_ref[7 + at : 8 + at, :] = early_ref[row : row + 1, part * D : (part + 1) * D]
    late_ref[22:23, :] = jnp.broadcast_to(total, (1, D))


def owned_grads(attn, first, down, low, early, waits):
    return pl.pallas_call(
        beside(owned_kernel, 5, 1, waits, ()),
        in_specs=[whole()] * 5 + [whole(pl.ANY)] * len(waits),
        out_specs=whole(),
        out_shape=jax.ShapeDtypeStruct((24, D), F32),
        name="owned_grads",
    )(attn, first, down, low, early, *waits)


def update_kernel(first_ref, late_ref, own_ref, other_ref, down_ref, *refs):
    states, norm_ref, factor_ref, outs = refs[:6], refs[6], refs[7], refs[8:]
    grads = late_ref[:22, :]
    norm = jnp.sqrt(late_ref[22:23, 0:1] + jnp.sum(column_sum(grads * grads), axis=1, keepdims=True))
    factor = clip_limit / jnp.maximum(norm, clip_limit)
    norm_ref[...] = norm
    factor_ref[...] = factor
    half = own_ref.shape[0]
    upper = jnp.where(first_ref[0] == 1, own_ref[...], other_ref[...])
    lower = jnp.where(first_ref[0] == 1, other_ref[...], own_ref[...])
    jobs = (
        (0, slice(0, half), upper, rate_wide),
        (0, slice(half, 2 * half), lower, rate_wide),
        (1, slice(0, half), down_ref[...], rate_down),
    )
    for kind, rows, grad, rate in jobs:
        master, moment, square = [ref[rows, :] for ref in states[3 * kind : 3 * kind + 3]]
        news = adamw(master, moment, square, grad * factor, rate, decay_weight)
        for new, out_ref in zip(news, outs[3 * kind : 3 * kind + 3]):
            out_ref[rows, :] = new


def update_all(first, late, own, other, down, states):
    scalar = jax.ShapeDtypeStruct((1, 1), F32)
    return pl.pallas_call(
        update_kernel,
        in_specs=[whole(pltpu.SMEM)] + [whole()] * 10,
        out_specs=(whole(),) * 8,
        out_shape=(scalar, scalar) + shapes_of(states),
        compiler_params=pltpu.CompilerParams(vmem_limit_bytes=VMEM_BYTES),
        name="update_all",
    )(first, late, own, other, down, *states)


SECTION = ("section", 0)


def swap_bit(value, axis, bit):
    mask = 2**bit
    return lax.ppermute(value, axis, [(i, i ^ mask) for i in range(lax.axis_size(axis))])


def axis_bits():
    return [("dp", b) for b in range(lax.axis_size("dp").bit_length() - 1)]


def plane_slots(order):
    apart = jnp.arange(lax.axis_size("dp"), dtype=jnp.int32) ^ lax.axis_index("dp")
    slot = jnp.zeros_like(apart)
    for at, (_, bit) in enumerate(order):
        slot = slot | (((apart >> bit) & 1) << at)
    return slot


def plane_devices(order):
    slot = np.arange(lax.axis_size("dp"), dtype=np.int32)
    apart = np.zeros_like(slot)
    for at, (_, bit) in enumerate(order):
        apart |= ((slot >> at) & 1) << bit
    return jnp.asarray(apart) ^ lax.axis_index("dp")


def gather_steps(own, order):
    held = own
    for axis, bit in order:
        held = jnp.concatenate([held, swap_bit(held, axis, bit)], axis=0)
    return held


def reduce_step(state, bit):
    kept, sent = state
    moved = swap_bit(sent, *bit).astype(F32)
    half = kept.shape[0] // 2
    if half == 0:
        return kept[0] + moved[0], None
    return kept[:half] + moved[:half], (kept[half:] + moved[half:]).astype(BF16)


def after(values, *others):
    return lax.optimization_barrier((values, others))[0]


def adamw(master, moment, square, clipped, step_rate, decay):
    moment_new = beta_one * moment + (1.0 - beta_one) * clipped
    square_new = beta_two * square + (1.0 - beta_two) * clipped * clipped
    moment_hat = moment_new / (1.0 - beta_one**STEP)
    square_hat = square_new / (1.0 - beta_two**STEP)
    master_new = master - step_rate * (
        moment_hat / (jnp.sqrt(square_hat) + adam_eps) + decay * master
    )
    return (moment_new, square_new, master_new)


def shards(
    layer_ends,
    doc_lengths,
    wide_master,
    wide_moment,
    wide_square,
    down_master,
    down_moment,
    down_square,
    small_master,
    small_moment,
    small_square,
):
    is_first = lax.axis_index("section") == 0
    count = lax.axis_size("dp")
    devices = 2 * count
    wide_rows = FF // count
    half_rows = wide_rows // 2
    small = small_master.reshape(1, SMALL)
    bits = axis_bits()
    reduce_orders = (bits, [bits[0], bits[2], bits[1]] + bits[3:])
    gather_orders = tuple(order[::-1] for order in reduce_orders)
    device = np.arange(count)
    half = half_rows

    own = wide_master[0].T.astype(BF16)
    other = swap_bit(own, "section", 0)
    attn_own = jnp.where(is_first, own, other)
    first_own = jnp.where(is_first, other[:half], own[half:])
    gathered = lax.all_gather(
        jnp.concatenate([first_own, down_master.astype(BF16)], axis=0), BOTH, axis=0, tiled=False
    )

    first = is_first.astype(jnp.int32)[None]
    me = jnp.stack([lax.axis_index("dp"), lax.axis_index("section")]).astype(jnp.int32)
    ends = layer_ends[0]
    to_swap = after(jnp.where(is_first, ends[L:], ends[:L]), other)
    swapped = swap_bit(to_swap, "section", 0)
    doc_ends = jnp.cumsum(jnp.where(is_first, doc_lengths[0], doc_lengths[1]))

    shared = 0
    while gather_orders[0][shared] == gather_orders[1][shared]:
        shared += 1
    held = gather_steps(attn_own[None], gather_orders[0][:shared])
    parts = [
        gather_steps(held[:, g * half : (g + 1) * half], gather_orders[g][shared:-1])
        for g in range(2)
    ]
    parts[1] = after(parts[1], swapped)
    slots, tables, groups = [], [], []
    for g, order in enumerate(gather_orders):
        device = plane_devices(order[:-1])[: count // 2]
        for part, bit in ((parts[g], 0), (swap_bit(parts[g], *order[-1]), 1)):
            slots.append(part)
            tables.append((device ^ bit) * wide_rows + g * half)
            groups.append((g, half, count // 2))
    block = np.arange(devices)
    first_rows = (block % count) * wide_rows + (block // count) * half
    ffn_places = (tuple(int(r) for r in first_rows), tuple(int(b) * half for b in block), half)
    if half % 16 != 0:
        whole_attn = jnp.zeros((FF, D), BF16)
        for part, rows in zip(slots, tables):
            for slot in range(count // 2):
                whole_attn = lax.dynamic_update_slice(whole_attn, part[slot], (rows[slot], 0))
        slots, tables, groups = [whole_attn[None]], [jnp.zeros((1,), jnp.int32)], [(0, FF, 1)]
        first_all = gathered[:, :half].reshape(2, count, half, D).transpose(1, 0, 2, 3)
        second_all = gathered[:, half:].reshape(FF, D)
        gathered = jnp.concatenate([first_all.reshape(FF, D), second_all], axis=0)[None]
        ffn_places = ((0,), (0,), FF)

    qkv, attended, stats, residual, inner_pair, attn_t = attention_forward(
        first, doc_ends, jnp.stack(tables), ends, swapped, small, slots, tuple(groups)
    )
    results, y_low, ffn_pair, ffn_turned, dhs, early = feed_forward(
        first, residual, ends, swapped, small, gathered, ffn_places
    )
    returned_y = lax.ppermute(y_low, "section", [(0, 1)])

    wide_block = lambda device, section: 2 * device + section
    down_block = lambda device, section: section * count + device
    ffn_orders = (
        [bits[0], bits[1], SECTION] + bits[2:],
        [bits[0], bits[2], bits[1], SECTION] + bits[3:],
    )
    attn_orders = (
        [bits[0], bits[1], bits[2], SECTION] + bits[3:],
        [bits[0], bits[2], bits[1], SECTION] + bits[3:],
    )
    groups = [(ffn_orders[0], wide_block), (ffn_orders[1], lambda d, s: down_block(d, s) + devices)]
    of_kind = lambda i, m: i // 2
    lefts = ffn_turned.reshape(2 * devices, half, L)
    sent, _ = weight_grad(
        me, lefts, count, ffn_pair, groups, 1, False, of_kind, [], "ffn_grad_sent"
    )
    do, delta, turned, inner_pair, out_low = inner_back(
        dhs, attended, small, attn_t, inner_pair, sent
    )
    moved = [swap_bit(s, *o[0]) for s, o in zip(sent, ffn_orders)]
    (low_a, high_a, low_b, high_b), _ = weight_grad(
        me, lefts, count, ffn_pair, groups, 1, False, of_kind, moved, "ffn_grad_kept", [do]
    )
    states = [(low_a, high_a), (low_b, high_b)]
    dq0, dk0, dv0, turned, _ = pair_back(
        0, doc_ends, qkv, do, stats, delta, turned, [high_a, high_b]
    )
    dq1, dk1, dv1, turned, _ = pair_back(
        1, doc_ends, qkv, do, stats, delta, turned, [returned_y]
    )
    states = combine(states, [o[1] for o in ffn_orders], [dq1])
    groups = [(order, lambda d, s, g=g: 4 * d + 2 * s + g) for g, order in enumerate(attn_orders)]

    def last_quarter(step, me_ref):
        return jnp.where((step ^ (me_ref[0] >> (len(bits) - 2))) == 3, 1, 0)

    lefts = turned.reshape(2 * devices, half // 2, L)
    attn_sent, token = weight_grad(
        me, lefts, count, inner_pair, groups, 2, True, last_quarter, [],
        "attention_grad_sent", [s for _, s in states],
    )
    grads = (dq0, dk0, dv0, dq1, dk1, dv1)
    results, dx0, low = input_grad(
        0, first, grads, ends, swapped, dhs, small, attn_t, results, out_low, [token]
    )
    returned_x = [lax.ppermute(dx0, "section", [(1, 0)])]
    moved = [swap_bit(s, *o[0]) for s, o in zip(attn_sent, attn_orders)]
    states = combine(states, [o[2] for o in ffn_orders], [dx0])
    (low_a, high_a, low_b, high_b), token = weight_grad(
        me, lefts, count, inner_pair, groups, 2, True, last_quarter, moved,
        "attention_grad_kept", [dx0] + [s for _, s in states],
    )
    attn_states = [(low_a, high_a), (low_b, high_b)]
    states = combine(states, [o[3] for o in ffn_orders], [token])
    results, dx1, low = input_grad(
        1, first, grads, ends, swapped, dhs, small, attn_t, results, low,
        [high_a, high_b] + [s for _, s in states],
    )
    returned_x.append(lax.ppermute(dx1, "section", [(1, 0)]))
    attn_states = combine(
        attn_states, [o[1] for o in attn_orders], [dx1, returned_x[0]]
    )
    for at in range(4, len(ffn_orders[0])):
        states = [reduce_step(s, o[at]) for s, o in zip(states, ffn_orders)]
    first_half, down_grad = states[0][0], states[1][0]
    attn_states = combine(attn_states, [o[2] for o in attn_orders])
    attn_state = tuple(jnp.concatenate(both, axis=1) for both in zip(*attn_states))
    for pair in attn_orders[0][3:]:
        attn_state = reduce_step(attn_state, pair)
    attn_half = attn_state[0]
    results, token = place_results(first, returned_y, returned_x, results)
    late = owned_grads(attn_half, first_half, down_grad, low, early, [token])
    own_half = jnp.where(is_first, attn_half, first_half)
    other_half = swap_bit(jnp.where(is_first, first_half, attn_half), "section", 0)
    for pair in [SECTION] + bits:
        late = late + swap_bit(late, *pair)
    turned_wide = [a[0].T for a in (wide_master, wide_moment, wide_square)]
    norm, factor, *news = update_all(
        first, late, own_half, other_half, down_grad, turned_wide + [down_master, down_moment, down_square]
    )
    small_news = adamw(
        small_master, small_moment, small_square,
        late[:22].reshape(SMALL) * factor[0, 0], rate_small, 0.0,
    )
    return (
        results[None],
        *[a.T[None] for a in news[:3]],
        *news[3:6],
        *small_news,
        norm[0, 0],
    )


def solution(mesh):
    wide = P("section", None, "dp")
    down = P(("section", "dp"), None)
    ends = P("section", "dp", None)
    return jax.shard_map(
        shards,
        mesh=mesh,
        in_specs=(ends, P("dp", None), wide, wide, wide, down, down, down, P(), P(), P()),
        out_specs=(ends, wide, wide, wide, down, down, down, P(), P(), P(), P()),
        check_vma=False,
    )
```

```python
import functools

import jax
import jax.numpy as jnp
import numpy as np
from jax import lax
from jax.experimental import pallas as pl
from jax.experimental.pallas import tpu as pltpu
from jax.sharding import PartitionSpec as P

D = 768
FF = 3072
HEADS = 12
HEAD_DIM = 64
PAIRS = HEADS // 2
L = 1024
BLOCK = 256
TILES = L // BLOCK
STEP = 8
CHUNK = 512
WIDE_TILE = 512
FFN_TILE = 256
SMALL_AT = {}
offset = 0
for name, width in (
    ("g1", D), ("b1", D), ("bq", D), ("bv", D), ("gi", D), ("bi", D), ("bo", D), ("g2", D), ("b2", D),
    ("c1", FF), ("gh", FF), ("bh", FF), ("c2", D),
):
    SMALL_AT[name] = (offset, width)
    offset += width
SMALL = offset

eps_norm = 1e-05
clip_limit = 1.0
beta_one = 0.9
beta_two = 0.99
adam_eps = 1e-08
decay_weight = 0.1
rate_wide = 0.05
rate_down = 0.025
rate_small = 0.6
masked_score = -1e30

BOTH = ("section", "dp")
F32 = jnp.float32
BF16 = jnp.bfloat16
NN = ((1,), (0,))
NT = ((1,), (1,))
TN = ((0,), (0,))
VMEM_BYTES = 58 * 2**20


def dot(a, b, dims):
    return lax.dot_general(a, b, (dims, ((), ())), preferred_element_type=F32)


def small_row(small_ref, name, start=0, width=None):
    at, full = SMALL_AT[name]
    return small_ref[:, at + start : at + start + (full if width is None else width)]


def normalise(values):
    row_mean = jnp.mean(values, axis=-1, keepdims=True)
    centred = values - row_mean
    spread = jnp.mean(centred * centred, axis=-1, keepdims=True)
    inverse = lax.rsqrt(spread + eps_norm)
    return centred * inverse, inverse


def normalise_back(grad, gain, unit, inverse):
    scaled = grad * gain
    first = jnp.mean(scaled, axis=-1, keepdims=True)
    second = jnp.mean(scaled * unit, axis=-1, keepdims=True)
    return inverse * (scaled - first - unit * second)


def column_sum(values):
    return jnp.sum(values, axis=0, keepdims=True)


def document_ends(lengths_ref, first_ref):
    row = 1 - first_ref[0]
    ends = [lengths_ref[row, 0]]
    for i in (1, 2):
        ends.append(ends[-1] + lengths_ref[row, i])
    return ends


def visible_bias(ends, query_start, key_start, keys):
    key = key_start + lax.broadcasted_iota(jnp.int32, (keys, BLOCK), 0)
    query = query_start + lax.broadcasted_iota(jnp.int32, (1, BLOCK), 1)
    begin = jnp.zeros((1, BLOCK), jnp.int32)
    for end in ends:
        begin = jnp.where(query >= end, end, begin)
    return jnp.where((key >= begin) & (key <= query), 0.0, masked_score).astype(F32)


def halves(pair):
    lane = lax.broadcasted_iota(jnp.int32, pair.shape, 1)
    zero = jnp.zeros_like(pair)
    return jnp.where(lane < HEAD_DIM, pair, zero), jnp.where(lane < HEAD_DIM, zero, pair)


def first_key(tile):
    return max(0, tile - 2) * BLOCK


def attention_kernel(groups, first_ref, lengths_ref, me_ref, own_ref, swapped_ref, small_ref, *refs):
    slots, refs = refs[: len(groups)], refs[len(groups) :]
    qkv_ref, o_ref, stats_ref, hs_ref, pair_ref, held_ref, *refs = refs
    bias_ref, vt_ref, weights_ref, x_ref, a_ref, sem, x_sem, out_sem = refs

    @pl.when(first_ref[0] == 1)
    def _():
        pltpu.make_async_copy(own_ref.at[pl.ds(0, L)], x_ref, x_sem).start()

    @pl.when(first_ref[0] == 0)
    def _():
        pltpu.make_async_copy(swapped_ref, x_ref, x_sem).start()

    copies = []
    for at, (scale, shift, rows, apart) in enumerate(groups):
        for slot, bits in enumerate(apart):
            target = pl.multiple_of((me_ref[0] ^ bits) * scale + shift, 16)
            copies.append(
                pltpu.make_async_copy(
                    slots[at].at[slot], weights_ref.at[pl.ds(target, rows)], sem
                )
            )
    for copy in copies:
        copy.start()
    for copy in copies:
        copy.wait()
    hold = pltpu.make_async_copy(weights_ref, held_ref, out_sem.at[0])
    hold.start()
    pltpu.make_async_copy(swapped_ref, x_ref, x_sem).wait()

    def project(tile, carry):
        rows = pl.ds(pl.multiple_of(tile * WIDE_TILE, WIDE_TILE), WIDE_TILE)
        unit, _ = normalise(x_ref[rows, :].astype(F32))
        a = (unit * small_row(small_ref, "g1") + small_row(small_ref, "b1")).astype(BF16)
        a_ref[rows, :] = a
        q = (dot(a, weights_ref[:D, :], NT) + small_row(small_ref, "bq")).astype(BF16)
        qkv_ref[rows, :D] = q * jnp.asarray(0.125, BF16)
        qkv_ref[rows, D : 2 * D] = dot(a, weights_ref[D : 2 * D, :], NT).astype(BF16)
        v = (dot(a, weights_ref[2 * D : 3 * D, :], NT) + small_row(small_ref, "bv")).astype(BF16)
        qkv_ref[rows, 2 * D :] = v
        vt_ref[:, rows] = v.T
        return carry

    lax.fori_loop(0, L // WIDE_TILE, project, 0)
    hold_a = pltpu.make_async_copy(a_ref, pair_ref.at[0], out_sem.at[1])
    hold_a.start()
    ends = document_ends(lengths_ref, first_ref)

    for tile in range(TILES):
        start = first_key(tile)
        keys = (tile + 1) * BLOCK - start
        rows = slice(tile * BLOCK, (tile + 1) * BLOCK)
        window = slice(start, start + keys)
        bias_ref[:keys, :] = visible_bias(ends, tile * BLOCK, start, keys)

        def one_pair(pair, carry, rows=rows, window=window, keys=keys):
            at = pl.multiple_of(pair * 128, 128)
            q_parts = halves(qkv_ref[rows, pl.ds(at, 128)])
            k = qkv_ref[window, pl.ds(D + at, 128)]
            vt = vt_ref[pl.ds(at, 128), window]
            weights, tops = [], []
            for q_part in q_parts:
                scores = dot(k, q_part, NT) + bias_ref[:keys, :]
                top = jnp.max(scores, axis=0, keepdims=True)
                weights.append(jnp.exp(scores - top).astype(BF16))
                tops.append(top)
            ones = jnp.ones((16, keys), BF16)
            outs = []
            for i in range(2):
                left = jnp.concatenate([vt[i * HEAD_DIM : (i + 1) * HEAD_DIM], ones], axis=0)
                mixed = dot(left, weights[i], NN)
                total = mixed[HEAD_DIM : HEAD_DIM + 1, :]
                outs.append(mixed[:HEAD_DIM, :] / total)
                stats_ref[pair, i : i + 1, rows] = tops[i] + jnp.log(total)
            o_ref[rows, pl.ds(at, 128)] = jnp.concatenate(outs, axis=0).T
            return carry

        lax.fori_loop(0, PAIRS, one_pair, 0, unroll=2)

    def finish(tile, carry):
        rows = pl.ds(pl.multiple_of(tile * WIDE_TILE, WIDE_TILE), WIDE_TILE)
        unit, _ = normalise(o_ref[rows, :])
        u = (unit * small_row(small_ref, "gi") + small_row(small_ref, "bi")).astype(BF16)
        h = x_ref[rows, :].astype(F32) + dot(u, weights_ref[3 * D :, :], NT)
        hs_ref[rows, :] = (h + small_row(small_ref, "bo")).astype(BF16)
        return carry

    lax.fori_loop(0, L // WIDE_TILE, finish, 0)
    hold.wait()
    hold_a.wait()


def whole(memory_space=pltpu.VMEM):
    return pl.BlockSpec(memory_space=memory_space)


def beside(kernel, inputs, outputs, waits, carried):
    def body(*refs):
        passed = len(waits) + len(carried)
        after_inputs = refs[inputs + passed :]
        kernel(*refs[:inputs], *after_inputs[:outputs], *after_inputs[outputs + len(carried) :])

    return body


def shapes_of(arrays):
    return tuple(jax.ShapeDtypeStruct(a.shape, a.dtype) for a in arrays)


def attention_forward(first, lengths, me, ends_in, swapped, small, slots, groups):
    return pl.pallas_call(
        functools.partial(attention_kernel, groups),
        out_shape=(
            jax.ShapeDtypeStruct((L, 3 * D), BF16),
            jax.ShapeDtypeStruct((L, D), F32),
            jax.ShapeDtypeStruct((PAIRS, 2, L), F32),
            jax.ShapeDtypeStruct((L, D), BF16),
            jax.ShapeDtypeStruct((2, L, D), BF16),
            jax.ShapeDtypeStruct((FF, D), BF16),
        ),
        in_specs=[whole(pltpu.SMEM)] * 3 + [whole(pl.ANY)] * 2 + [whole()]
        + [whole(pl.ANY)] * len(slots),
        out_specs=(whole(),) * 4 + (whole(pl.ANY),) * 2,
        scratch_shapes=[
            pltpu.VMEM((3 * BLOCK, BLOCK), F32),
            pltpu.VMEM((D, L), BF16),
            pltpu.VMEM((FF, D), BF16),
            pltpu.VMEM((L, D), BF16),
            pltpu.VMEM((L, D), BF16),
            pltpu.SemaphoreType.DMA,
            pltpu.SemaphoreType.DMA,
            pltpu.SemaphoreType.DMA((2,)),
        ],
        compiler_params=pltpu.CompilerParams(vmem_limit_bytes=VMEM_BYTES),
        cost_estimate=pl.CostEstimate(flops=14 * 10**9, bytes_accessed=20 * 10**6, transcendentals=0),
        name="attention_forward",
    )(first, lengths, me, ends_in, swapped, small, *slots)


def gelu_parts(x):
    size = jnp.abs(x)
    bell = jnp.exp(x * x * -0.5)
    t = 1.0 / (1.0 + size * (0.3275911 * 0.5**0.5))
    tail = t * (0.5 * 0.254829592 + t * (0.5 * -0.284496736 + t * (
        0.5 * 1.421413741 + t * (0.5 * -1.453152027 + t * (0.5 * 1.061405429)))))
    tail = tail * bell
    phi = jnp.where(x > 0, 1.0 - tail, tail)
    return x * phi, phi + x * bell * 0.3989422804014327


def ffn_kernel(
    places, chosen_ref, hs_ref, lower_ref, swapped_ref, small_ref, slots_ref,
    y_ref, sent_ref, pair_ref, turned_ref, dhs_ref, wide_ref,
    g_ref, slope_ref, t_ref, held_ref, first_ref, second_ref, sems,
):
    first_rows, second_rows, rows = places

    def weight_copies(into_ref, rows_of, start, sem):
        return [
            pltpu.make_async_copy(
                slots_ref.at[block, pl.ds(start, rows)], into_ref.at[pl.ds(row, rows)], sem
            )
            for block, row in enumerate(rows_of)
        ]

    @pl.when(pl.program_id(0) == 0)
    def _():
        wide_ref[...] = jnp.zeros_like(wide_ref)
        copies = weight_copies(first_ref, first_rows, 0, sems.at[0])
        for copy in copies + weight_copies(second_ref, second_rows, rows, sems.at[1]):
            copy.start()
        for copy in copies:
            copy.wait()

    hs = hs_ref[...].astype(F32)
    unit, inverse = normalise(hs)
    e = (unit * small_row(small_ref, "g2") + small_row(small_ref, "b2")).astype(BF16)
    pair_ref[0] = e
    dy = jnp.where(chosen_ref[0] == 1, swapped_ref[...], lower_ref[...])
    pair_ref[1] = dy
    chunks = [slice(j, j + CHUNK) for j in range(0, FF, CHUNK)]

    total = jnp.zeros((FFN_TILE, 1), F32)
    for cut in chunks:
        f = dot(e, first_ref[cut, :], NT) + small_row(small_ref, "c1", cut.start, CHUNK)
        g, slope = gelu_parts(f)
        g_ref[:, cut] = g
        slope_ref[:, cut] = slope
        total = total + jnp.sum(g, axis=1, keepdims=True)
    mean = total / FF
    total = jnp.zeros((FFN_TILE, 1), F32)
    for cut in chunks:
        centred = g_ref[:, cut] - mean
        total = total + jnp.sum(centred * centred, axis=1, keepdims=True)
    inner_inverse = lax.rsqrt(total / FF + eps_norm)

    step = pl.program_id(0)
    columns = pl.ds(pl.multiple_of(step * FFN_TILE, FFN_TILE), FFN_TILE)
    flush = pltpu.make_async_copy(held_ref, turned_ref.at[:, :, columns], sems.at[2])

    @pl.when(step == 0)
    def _():
        for copy in weight_copies(second_ref, second_rows, rows, sems.at[1]):
            copy.wait()

    @pl.when(step > 0)
    def _():
        flush.wait()

    y = hs + small_row(small_ref, "c2")
    first_sum = jnp.zeros((FFN_TILE, 1), F32)
    second_sum = jnp.zeros((FFN_TILE, 1), F32)
    for cut in chunks:
        gain = small_row(small_ref, "gh", cut.start, CHUNK)
        ghat = (g_ref[:, cut] - mean) * inner_inverse
        g_ref[:, cut] = ghat
        n = (ghat * gain + small_row(small_ref, "bh", cut.start, CHUNK)).astype(BF16)
        held_ref[1, cut, :] = n.T
        y = y + dot(n, second_ref[cut, :], NN)
        dn = dot(dy, second_ref[cut, :], NT)
        wide_ref[0:1, cut] += column_sum(dn * ghat)
        wide_ref[1:2, cut] += column_sum(dn)
        scaled = dn * gain
        t_ref[:, cut] = scaled
        first_sum = first_sum + jnp.sum(scaled, axis=1, keepdims=True)
        second_sum = second_sum + jnp.sum(scaled * ghat, axis=1, keepdims=True)
    y_ref[...] = y
    sent_ref[...] = y.astype(BF16)
    first_sum = first_sum / FF
    second_sum = second_sum / FF

    de = jnp.zeros((FFN_TILE, D), F32)
    for cut in chunks:
        back = t_ref[:, cut] - first_sum - g_ref[:, cut] * second_sum
        df = (inner_inverse * back * slope_ref[:, cut]).astype(BF16)
        held_ref[0, cut, :] = df.T
        wide_ref[2:3, cut] += column_sum(df.astype(F32))
        de = de + dot(df, first_ref[cut, :], NN)
    flush.start()

    dyf = dy.astype(F32)
    wide_ref[3:4, :D] += column_sum(de * unit)
    wide_ref[3:4, D : 2 * D] += column_sum(de)
    wide_ref[3:4, 2 * D : 3 * D] += column_sum(dyf)
    dhp = normalise_back(de, small_row(small_ref, "g2"), unit, inverse)
    dhs_ref[...] = (dyf + dhp).astype(BF16)

    @pl.when(step == pl.num_programs(0) - 1)
    def _():
        flush.wait()


def feed_forward(chosen, hs, ends_in, swapped, small, slots, places):
    at = L // FFN_TILE
    tile = lambda shift=0: pl.BlockSpec((FFN_TILE, D), lambda i: (i + shift, 0))
    keep = lambda shape: pl.BlockSpec(shape, lambda i: (0, 0), pipeline_mode=pl.Buffered(1))
    return pl.pallas_call(
        functools.partial(ffn_kernel, places),
        grid=(at,),
        out_shape=(
            jax.ShapeDtypeStruct((2 * L, D), F32),
            jax.ShapeDtypeStruct((L, D), BF16),
            jax.ShapeDtypeStruct((2, L, D), BF16),
            jax.ShapeDtypeStruct((2, FF, L), BF16),
            jax.ShapeDtypeStruct((L, D), BF16),
            jax.ShapeDtypeStruct((4, FF), F32),
        ),
        in_specs=[whole(pltpu.SMEM), tile(), tile(at), tile(), keep((1, SMALL)), whole(pl.ANY)],
        out_specs=(
            tile(at), tile(),
            pl.BlockSpec((2, FFN_TILE, D), lambda i: (0, i, 0)),
            whole(pl.ANY),
            tile(),
            pl.BlockSpec((4, FF), lambda i: (0, 0)),
        ),
        scratch_shapes=[pltpu.VMEM((FFN_TILE, FF), F32)] * 3
        + [pltpu.VMEM((2, FF, FFN_TILE), BF16)]
        + [pltpu.VMEM((FF, D), BF16)] * 2
        + [pltpu.SemaphoreType.DMA((3,))],
        compiler_params=pltpu.CompilerParams(vmem_limit_bytes=VMEM_BYTES),
        cost_estimate=pl.CostEstimate(flops=40 * 10**9, bytes_accessed=30 * 10**6, transcendentals=0),
        name="feed_forward",
    )(chosen, hs, ends_in, swapped, small, slots)


TOKEN = jax.ShapeDtypeStruct((8, 128), F32)


def weight_grad_kernel(plan, me_ref, *refs):
    lefts, right_ref = refs[: plan["lefts"]], refs[plan["lefts"]]
    refs = refs[plan["lefts"] + 1 :]
    moved, outs, token_ref = refs[: plan["moved"]], refs[plan["moved"] : -1], refs[-1]
    rows = lefts[0].shape[1]
    blocks = [ref[0] for ref in lefts]
    token_ref[...] = jnp.zeros_like(token_ref)
    if rows % 16 == 0:
        value = dot(jnp.concatenate(blocks, axis=0), right_ref[0], NN)
        parts = [value[at * rows : (at + 1) * rows] for at in range(len(blocks))]
    else:
        parts = [dot(block, right_ref[0], NN) for block in blocks]
    split = plan["split"]
    step = pl.program_id(0) % 2**split
    kind = pl.program_id(0) // 2**split

    def store(group, parts):
        views = plan["views"][group]
        for at, part in enumerate(parts):
            place = tuple(int(p) for p in np.unravel_index(at, views))
            if not moved:
                outs[group][place] = part.astype(BF16)
                continue
            total = part + moved[group][place].astype(F32)
            low_ref, high_ref = outs[2 * group : 2 * group + 2]
            first_bit = plan["first"][group]
            if first_bit is None:
                if place[0] == 0:
                    low_ref[place[1:]] = total
                else:
                    high_ref[place[1:]] = total.astype(BF16)
                continue

            @pl.when((step >> first_bit) & 1 == 0)
            def _():
                low_ref[place[1:]] = total

            @pl.when((step >> first_bit) & 1 == 1)
            def _():
                high_ref[place[1:]] = total.astype(BF16)

    if plan["joint"]:
        count = len(parts) // 2
        for group in range(2):
            store(group, parts[group * count : (group + 1) * count])
    else:
        for group in range(2):

            @pl.when(kind == group)
            def _():
                store(group, parts)


def weight_grad(me, left, count, right, groups, split, joint, right_of, moved, name, waits=()):
    bits = count.bit_length() - 1
    rows = left.shape[1]
    steps = 2**split
    top = [("dp", bits - 1 - i) for i in range(split)]
    shift = bits - split
    in_specs, outs, out_specs, views, firsts, combos = [], [], [], [], [], []
    moved_specs = []

    def row_of(group, combo, step, me_ref):
        order, row_block = groups[group]
        free = [pair for pair in order[1:] if pair not in top]
        apart, across = (0 if moved else 1), 0
        for at, (axis, bit) in enumerate(free):
            on = (combo >> (len(free) - 1 - at)) & 1
            if axis == "dp":
                apart |= on << bit
            else:
                across = on
        return row_block((apart + (step << shift)) ^ me_ref[0], across ^ me_ref[1])

    def local_step(i, group):
        if joint:
            return i
        return jnp.clip(i - group * steps, 0, steps - 1)

    free_count = 2 ** (len(groups[0][0]) - 1 - split)
    if joint:
        for group in range(2):
            for combo in range(free_count):
                in_specs.append(
                    pl.BlockSpec(
                        (1, rows, L),
                        lambda i, m, g=group, c=combo: (row_of(g, c, i, m), 0, 0),
                    )
                )
    else:
        for combo in range(free_count):

            def place(i, m, c=combo):
                step = i % steps
                return jnp.where(i < steps, row_of(0, c, step, m), row_of(1, c, step, m)), 0, 0

            in_specs.append(pl.BlockSpec((1, rows, L), place))
    lefts = len(in_specs)
    in_specs.append(pl.BlockSpec((1, L, D), lambda i, m: (right_of(i, m), 0, 0)))

    for group, (order, _) in enumerate(groups):
        order = order[1:]

        def spots(i, m, pairs=order, group=group):
            step = local_step(i, group)
            return (*[(step >> (p[1] - shift)) & 1 if p in top else 0 for p in pairs], 0, 0)

        view = tuple(1 if pair in top else 2 for pair in order)
        views.append(view)
        firsts.append(order[0][1] - shift if order[0] in top else None)
        full = pl.BlockSpec((*view, rows, D), spots)
        if moved:
            moved_specs.append(full)
            half = pl.BlockSpec(
                (*view[1:], rows, D), lambda i, m, spots=spots: spots(i, m)[1:]
            )
            out_specs += [half, half]
            shape = (2,) * (len(order) - 1) + (rows, D)
            outs += [jax.ShapeDtypeStruct(shape, F32), jax.ShapeDtypeStruct(shape, BF16)]
        else:
            out_specs.append(full)
            outs.append(jax.ShapeDtypeStruct((2,) * len(order) + (rows, D), BF16))
    plan = dict(
        lefts=lefts, moved=len(moved), split=split, views=views, first=firsts, joint=joint
    )
    moved = [m.reshape((2,) * (len(groups[0][0]) - 1) + (rows, D)) for m in moved]
    inputs = len(in_specs) + len(moved) + 1
    *results, token = pl.pallas_call(
        beside(functools.partial(weight_grad_kernel, plan), inputs, len(outs) + 1, waits, ()),
        grid_spec=pltpu.PrefetchScalarGridSpec(
            num_scalar_prefetch=1,
            grid=(steps if joint else 2 * steps,),
            in_specs=in_specs + moved_specs + [whole(pl.ANY)] * len(waits),
            out_specs=tuple(out_specs) + (pl.BlockSpec((8, 128), lambda i, m: (0, 0)),),
        ),
        out_shape=tuple(outs) + (TOKEN,),
        compiler_params=pltpu.CompilerParams(vmem_limit_bytes=VMEM_BYTES),
        cost_estimate=pl.CostEstimate(flops=6 * 10**9, bytes_accessed=9 * 10**6, transcendentals=0),
        name=name,
    )(me, *[left] * lefts, right, *moved, *waits)
    return [r.reshape(-1, rows, D) for r in results], token


def inner_back_kernel(
    dhs_ref, o_ref, small_ref, weights_ref, pair_ref, do_ref, delta_ref, turned_ref, u_ref, low_ref
):
    @pl.when(pl.program_id(0) == 0)
    def _():
        low_ref[...] = jnp.zeros_like(low_ref)

    o = o_ref[...]
    unit, inverse = normalise(o)
    gain = small_row(small_ref, "gi")
    u_ref[0] = (unit * gain + small_row(small_ref, "bi")).astype(BF16)
    dhs = dhs_ref[...]
    turned_ref[0] = dhs.T
    du = dot(dhs, weights_ref[...], NN)
    low_ref[4:5, :] += column_sum(du * unit)
    low_ref[5:6, :] += column_sum(du)
    low_ref[6:7, :] += column_sum(dhs.astype(F32))
    do = normalise_back(du, gain, unit, inverse).astype(BF16)
    do_ref[...] = do
    product = (do.astype(F32) * o).T
    for head in range(HEADS):
        delta_ref[head // 2, head % 2 : head % 2 + 1, :] = column_sum(
            product[head * HEAD_DIM : (head + 1) * HEAD_DIM, :]
        )


def inner_back(dhs, o, small, weights, pair, waits=()):
    tile = lambda width: pl.BlockSpec((BLOCK, width), lambda i: (i, 0))
    return pl.pallas_call(
        beside(inner_back_kernel, 5, 5, waits, ()),
        grid=(TILES,),
        out_shape=(
            jax.ShapeDtypeStruct((L, D), BF16),
            jax.ShapeDtypeStruct((PAIRS, 2, L), F32),
            jax.ShapeDtypeStruct((4, D, L), BF16),
            jax.ShapeDtypeStruct((2, L, D), BF16),
            jax.ShapeDtypeStruct((8, D), F32),
        ),
        in_specs=[
            tile(D),
            tile(D),
            pl.BlockSpec((1, SMALL), lambda i: (0, 0), pipeline_mode=pl.Buffered(1)),
            pl.BlockSpec((D, D), lambda i: (3, 0), pipeline_mode=pl.Buffered(1)),
            whole(pl.ANY),
        ]
        + [whole(pl.ANY)] * len(waits),
        out_specs=(
            tile(D),
            pl.BlockSpec((PAIRS, 2, BLOCK), lambda i: (0, 0, i)),
            pl.BlockSpec((1, D, BLOCK), lambda i: (3, 0, i)),
            pl.BlockSpec((1, BLOCK, D), lambda i: (1, i, 0)),
            pl.BlockSpec((8, D), lambda i: (0, 0)),
        ),
        input_output_aliases={4: 3},
        compiler_params=pltpu.CompilerParams(vmem_limit_bytes=VMEM_BYTES),
        cost_estimate=pl.CostEstimate(flops=6 * 10**9, bytes_accessed=15 * 10**6, transcendentals=0),
        name="inner_back",
    )(dhs, o, small, weights, pair, *waits)


GROUP = 3


def pair_back_kernel(
    first_ref, lengths_ref, q_ref, k_ref, v_ref, do_ref, stats_ref, delta_ref, earlier_ref,
    dq_ref, dk_ref, dv_ref, turned_ref, token_ref, bias_ref, dk_sum, dv_sum,
):
    token_ref[...] = jnp.zeros_like(token_ref)

    @pl.when(pl.program_id(0) == 0)
    def _():
        ends = document_ends(lengths_ref, first_ref)
        for tile in range(TILES):
            start = first_key(tile)
            keys = (tile + 1) * BLOCK - start
            bias_ref[tile, :keys, :] = visible_bias(ends, tile * BLOCK, start, keys)

    dk_sum[...] = jnp.zeros_like(dk_sum)
    dv_sum[...] = jnp.zeros_like(dv_sum)
    for tile in range(TILES):
        start = first_key(tile)
        keys = (tile + 1) * BLOCK - start
        rows = slice(tile * BLOCK, (tile + 1) * BLOCK)
        window = slice(start, start + keys)
        q_parts = halves(q_ref[rows, :])
        do_parts = halves(do_ref[rows, :])
        k = k_ref[window, :]
        v = v_ref[window, :]
        kt = k.T
        dqs = []
        for i in range(2):
            scores = dot(k, q_parts[i], NT) + bias_ref[tile, :keys, :]
            probs = jnp.exp(scores - stats_ref[0, i : i + 1, rows])
            dprobs = dot(v, do_parts[i], NT)
            ds = (probs * (dprobs - delta_ref[0, i : i + 1, rows])).astype(BF16)
            dv_sum[window, :] += dot(probs.astype(BF16), do_parts[i], NN)
            dk_sum[window, :] += dot(ds, q_parts[i], NN)
            dqs.append(dot(kt[i * HEAD_DIM : (i + 1) * HEAD_DIM], ds, NN))
        dq = (jnp.concatenate(dqs, axis=0) * 0.125).astype(BF16)
        turned_ref[0, :, rows] = dq
        dq_ref[rows, :] = dq.T
    for part, sum_ref, out_ref in ((1, dk_sum, dk_ref), (2, dv_sum, dv_ref)):
        grad = sum_ref[...].astype(BF16)
        out_ref[...] = grad
        turned_ref[part] = grad.T


def pair_back(part, first_flag, lengths, qkv, do, stats, delta, turned, waits=()):
    first = part * GROUP
    column = lambda base: pl.BlockSpec((L, 128), lambda i: (0, base + first + i))
    rows = pl.BlockSpec((1, 2, L), lambda i: (first + i, 0, 0))
    out = pl.BlockSpec((L, 128), lambda i: (0, i))
    width = GROUP * 128
    return pl.pallas_call(
        beside(pair_back_kernel, 9, 5, waits, ()),
        grid=(GROUP,),
        out_shape=(jax.ShapeDtypeStruct((L, width), BF16),) * 3
        + (jax.ShapeDtypeStruct((4, D, L), BF16), TOKEN),
        in_specs=[
            whole(pltpu.SMEM), whole(pltpu.SMEM), column(0), column(PAIRS), column(2 * PAIRS), column(0), rows, rows,
            whole(pl.ANY),
        ]
        + [whole(pl.ANY)] * len(waits),
        out_specs=(out,) * 3 + (
            pl.BlockSpec((3, 128, L), lambda i: (0, first + i, 0)),
            pl.BlockSpec((8, 128), lambda i: (0, 0)),
        ),
        input_output_aliases={8: 3},
        scratch_shapes=[
            pltpu.VMEM((TILES, 3 * BLOCK, BLOCK), F32),
            pltpu.VMEM((L, 128), F32),
            pltpu.VMEM((L, 128), F32),
        ],
        compiler_params=pltpu.CompilerParams(vmem_limit_bytes=VMEM_BYTES),
        cost_estimate=pl.CostEstimate(flops=13 * 10**9, bytes_accessed=15 * 10**6, transcendentals=0),
        name="pair_back",
    )(first_flag, lengths, qkv, qkv, qkv, do, stats, delta, turned, *waits)


def input_grad_kernel(
    first_ref, dq0, dk0, dv0, dq1, dk1, dv1, own_ref, swapped_ref, dhs_ref, small_ref, weights_ref,
    results_ref, earlier_ref, dx_ref, sent_ref, low_ref,
):
    @pl.when(pl.program_id(0) == 0)
    def _():
        low_ref[...] = earlier_ref[...]

    x = jnp.where(first_ref[0] == 1, own_ref[...], swapped_ref[...])
    unit, inverse = normalise(x.astype(F32))
    gain = small_row(small_ref, "g1")
    grads = [ref[...] for ref in (dq0, dq1, dk0, dk1, dv0, dv1)]
    width = GROUP * 128
    da = dot(jnp.concatenate(grads, axis=1), weights_ref[...], NN)
    for at, grad in enumerate(grads):
        if at < 2 or at > 3:
            row = 2 if at < 2 else 3
            cut = slice((at % 2) * width, (at % 2 + 1) * width)
            low_ref[row : row + 1, cut] += column_sum(grad.astype(F32))
    low_ref[0:1, :] += column_sum(da * unit)
    low_ref[1:2, :] += column_sum(da)
    dx = normalise_back(da, gain, unit, inverse) + dhs_ref[...].astype(F32)
    dx_ref[...] = dx
    sent_ref[...] = dx.astype(BF16)


def input_grad(start, tiles, first, grads, ends_in, swapped, dhs, small, weights, results, earlier, waits=(), carried=()):
    tile = lambda width: pl.BlockSpec((BLOCK, width), lambda i: (i + start, 0))
    keep = lambda shape: pl.BlockSpec(shape, lambda i: (0, 0), pipeline_mode=pl.Buffered(1))
    return pl.pallas_call(
        beside(input_grad_kernel, 14, 3, waits, carried),
        grid=(tiles,),
        out_shape=(
            jax.ShapeDtypeStruct((2 * L, D), F32),
            jax.ShapeDtypeStruct((tiles * BLOCK, D), BF16),
            jax.ShapeDtypeStruct((8, D), F32),
        )
        + shapes_of(carried),
        in_specs=[whole(pltpu.SMEM)] + [tile(GROUP * 128)] * 6
        + [tile(D)] * 3 + [keep((1, SMALL)), keep((3 * D, D))]
        + [whole(pl.ANY), keep((8, D))]
        + [whole(pl.ANY)] * (len(waits) + len(carried)),
        out_specs=(
            tile(D),
            pl.BlockSpec((BLOCK, D), lambda i: (i, 0)),
            pl.BlockSpec((8, D), lambda i: (0, 0)),
        )
        + (whole(pl.ANY),) * len(carried),
        input_output_aliases={12: 0} | {14 + len(waits) + i: 3 + i for i in range(len(carried))},
        compiler_params=pltpu.CompilerParams(vmem_limit_bytes=VMEM_BYTES),
        cost_estimate=pl.CostEstimate(flops=4 * 10**9, bytes_accessed=10 * 10**6, transcendentals=0),
        name="input_grad",
    )(first, *grads, ends_in, swapped, dhs, small, weights, results, earlier, *waits, *carried)


def place_kernel(first_ref, y_ref, dx0_ref, dx1_ref, results_ref, out_ref, token_ref):
    token_ref[...] = jnp.zeros_like(token_ref)
    is_dx = first_ref[0] == 1
    step = pl.program_id(0)

    @pl.when(step == 0)
    def _():
        out_ref[...] = jnp.where(is_dx, dx0_ref[:WIDE_TILE, :], y_ref[...]).astype(F32)

    @pl.when(step == 1)
    def _():
        dx = jnp.concatenate([dx0_ref[WIDE_TILE:, :], dx1_ref[...]], axis=0)
        out_ref[...] = jnp.where(is_dx, dx, y_ref[...]).astype(F32)


def place_results(first, y, dx, results):
    tile = pl.BlockSpec((WIDE_TILE, D), lambda i, f: (i, 0))
    return pl.pallas_call(
        place_kernel,
        grid_spec=pltpu.PrefetchScalarGridSpec(
            num_scalar_prefetch=1,
            grid=(L // WIDE_TILE,),
            in_specs=[tile] + [pl.BlockSpec(d.shape, lambda i, f: (0, 0)) for d in dx]
            + [whole(pl.ANY)],
            out_specs=(
                pl.BlockSpec((WIDE_TILE, D), lambda i, f: (i + f[0] * (L // WIDE_TILE), 0)),
                pl.BlockSpec((8, 128), lambda i, f: (0, 0)),
            ),
        ),
        out_shape=(jax.ShapeDtypeStruct((2 * L, D), F32), TOKEN),
        input_output_aliases={4: 0},
        cost_estimate=pl.CostEstimate(flops=10**6, bytes_accessed=8 * 10**6, transcendentals=0),
        name="place_results",
    )(first, y, *dx, results)


def combine_kernel(groups, *refs):
    inputs, outputs = refs[: 4 * groups], refs[4 * groups :]
    for g in range(groups):
        low, high, low_in, high_in = inputs[4 * g : 4 * g + 4]
        kept_ref, sent_ref = outputs[2 * g : 2 * g + 2]
        kept_ref[...] = low[...] + low_in[...].astype(F32)
        sent_ref[...] = (high[...] + high_in[...].astype(F32)).astype(BF16)


def combine(states, bits, waits=()):
    moved = [swap_bit(sent, *bit) for (_, sent), bit in zip(states, bits)]
    half = states[0][0].shape[0] // 2
    steps = min(half, 2)
    block = (half // steps,) + states[0][0].shape[1:]
    operands, in_specs, out_shape, out_specs = [], [], [], []
    lower = pl.BlockSpec(block, lambda i: (i, 0, 0))
    upper = pl.BlockSpec(block, lambda i: (i + steps, 0, 0))
    for (kept, _), other in zip(states, moved):
        operands += [kept, kept, other, other]
        in_specs += [lower, upper, lower, upper]
        shape = (half,) + kept.shape[1:]
        out_shape += [jax.ShapeDtypeStruct(shape, F32), jax.ShapeDtypeStruct(shape, BF16)]
        out_specs += [lower, lower]
    outs = pl.pallas_call(
        beside(
            functools.partial(combine_kernel, len(states)), len(operands), len(out_shape), waits, ()
        ),
        grid=(steps,),
        in_specs=in_specs + [whole(pl.ANY)] * len(waits),
        out_specs=tuple(out_specs),
        out_shape=tuple(out_shape),
        compiler_params=pltpu.CompilerParams(vmem_limit_bytes=VMEM_BYTES),
        cost_estimate=pl.CostEstimate(flops=10**6, bytes_accessed=8 * 10**6, transcendentals=0),
        name="combine",
    )(*operands, *waits)
    return [(outs[2 * g], outs[2 * g + 1]) for g in range(len(states))]


def owned_kernel(attn_ref, first_ref, down_ref, low_ref, early_ref, late_ref):
    total = jnp.zeros((1, 1), F32)
    for ref in (attn_ref, first_ref, down_ref):
        total = total + jnp.sum(column_sum(ref[...] * ref[...]), axis=1, keepdims=True)
    late_ref[...] = jnp.zeros_like(late_ref)
    late_ref[:7, :] = low_ref[:7, :]
    order = [(3, 0), (3, 1)] + [(row, part) for row in (2, 0, 1) for part in range(4)] + [(3, 2)]
    for at, (row, part) in enumerate(order):
        late_ref[7 + at : 8 + at, :] = early_ref[row : row + 1, part * D : (part + 1) * D]
    late_ref[22:23, :] = jnp.broadcast_to(total, (1, D))


def owned_grads(attn, first, down, low, early, waits):
    return pl.pallas_call(
        beside(owned_kernel, 5, 1, waits, ()),
        in_specs=[whole()] * 5 + [whole(pl.ANY)] * len(waits),
        out_specs=whole(),
        out_shape=jax.ShapeDtypeStruct((24, D), F32),
        name="owned_grads",
    )(attn, first, down, low, early, *waits)


def update_kernel(first_ref, late_ref, own_ref, other_ref, down_ref, *refs):
    states, norm_ref, factor_ref, outs = refs[:6], refs[6], refs[7], refs[8:]
    grads = late_ref[:22, :]
    norm = jnp.sqrt(late_ref[22:23, 0:1] + jnp.sum(column_sum(grads * grads), axis=1, keepdims=True))
    factor = clip_limit / jnp.maximum(norm, clip_limit)
    norm_ref[...] = norm
    factor_ref[...] = factor
    half = own_ref.shape[0]
    upper = jnp.where(first_ref[0] == 1, own_ref[...], other_ref[...])
    lower = jnp.where(first_ref[0] == 1, other_ref[...], own_ref[...])
    jobs = (
        (0, slice(0, half), upper, rate_wide),
        (0, slice(half, 2 * half), lower, rate_wide),
        (1, slice(0, half), down_ref[...], rate_down),
    )
    for kind, rows, grad, rate in jobs:
        master, moment, square = [ref[rows, :] for ref in states[3 * kind : 3 * kind + 3]]
        news = adamw(master, moment, square, grad * factor, rate, decay_weight)
        for new, out_ref in zip(news, outs[3 * kind : 3 * kind + 3]):
            out_ref[rows, :] = new


def update_all(first, late, own, other, down, states):
    scalar = jax.ShapeDtypeStruct((1, 1), F32)
    return pl.pallas_call(
        update_kernel,
        in_specs=[whole(pltpu.SMEM)] + [whole()] * 10,
        out_specs=(whole(),) * 8,
        out_shape=(scalar, scalar) + shapes_of(states),
        compiler_params=pltpu.CompilerParams(vmem_limit_bytes=VMEM_BYTES),
        name="update_all",
    )(first, late, own, other, down, *states)


SECTION = ("section", 0)


def swap_bit(value, axis, bit):
    mask = 2**bit
    return lax.ppermute(value, axis, [(i, i ^ mask) for i in range(lax.axis_size(axis))])


def swap_mask(value, mask):
    pairs = [(i, i ^ mask) for i in range(2 * lax.axis_size("dp"))]
    return lax.ppermute(value, BOTH, pairs)


def sum_everywhere(value):
    size = lax.axis_size("dp")
    masks = [1, size] + [2**b for b in range(1, size.bit_length() - 1)]
    while masks:
        if len(masks) % 2 == 1:
            value = value + swap_mask(value, masks.pop(0))
            continue
        one, two = masks.pop(0), masks.pop(0)
        across = [swap_mask(value, mask) for mask in (one, two, one | two)]
        value = (value + across[0]) + (across[1] + across[2])
    return value


def axis_bits():
    return [("dp", b) for b in range(lax.axis_size("dp").bit_length() - 1)]


def plane_patterns(order):
    slot = np.arange(2 ** len(order), dtype=np.int32)
    apart = np.zeros_like(slot)
    for at, (_, bit) in enumerate(order):
        apart |= ((slot >> at) & 1) << bit
    return tuple(int(a) for a in apart)


def gather_steps(own, order):
    held = own
    for axis, bit in order:
        held = jnp.concatenate([held, swap_bit(held, axis, bit)], axis=0)
    return held


def reduce_step(state, bit):
    kept, sent = state
    moved = swap_bit(sent, *bit).astype(F32)
    half = kept.shape[0] // 2
    if half == 0:
        return kept[0] + moved[0], None
    return kept[:half] + moved[:half], (kept[half:] + moved[half:]).astype(BF16)


def after(values, *others):
    return lax.optimization_barrier((values, others))[0]


def adamw(master, moment, square, clipped, step_rate, decay):
    moment_new = beta_one * moment + (1.0 - beta_one) * clipped
    square_new = beta_two * square + (1.0 - beta_two) * clipped * clipped
    moment_hat = moment_new / (1.0 - beta_one**STEP)
    square_hat = square_new / (1.0 - beta_two**STEP)
    master_new = master - step_rate * (
        moment_hat / (jnp.sqrt(square_hat) + adam_eps) + decay * master
    )
    return (moment_new, square_new, master_new)


def shards(
    layer_ends,
    doc_lengths,
    wide_master,
    wide_moment,
    wide_square,
    down_master,
    down_moment,
    down_square,
    small_master,
    small_moment,
    small_square,
):
    is_first = lax.axis_index("section") == 0
    count = lax.axis_size("dp")
    devices = 2 * count
    wide_rows = FF // count
    half_rows = wide_rows // 2
    small = small_master.reshape(1, SMALL)
    bits = axis_bits()
    reduce_orders = (bits, [bits[0], bits[2], bits[1]] + bits[3:])
    gather_orders = tuple(order[::-1] for order in reduce_orders)
    device = np.arange(count)
    half = half_rows

    own = wide_master[0].T.astype(BF16)
    other = swap_bit(own, "section", 0)
    attn_own = jnp.where(is_first, own, other)
    first_own = jnp.where(is_first, other[:half], own[half:])
    gathered = lax.all_gather(
        jnp.concatenate([first_own, down_master.astype(BF16)], axis=0), BOTH, axis=0, tiled=False
    )

    first = is_first.astype(jnp.int32)[None]
    me = jnp.stack([lax.axis_index("dp"), lax.axis_index("section")]).astype(jnp.int32)
    ends = layer_ends[0]
    to_swap = after(jnp.where(is_first, ends[L:], ends[:L]), other)
    swapped = swap_bit(to_swap, "section", 0)

    shared = 0
    while gather_orders[0][shared] == gather_orders[1][shared]:
        shared += 1
    held = gather_steps(attn_own[None], gather_orders[0][:shared])
    parts = [
        gather_steps(held[:, g * half : (g + 1) * half], gather_orders[g][shared:-1])
        for g in range(2)
    ]
    parts[1] = after(parts[1], swapped)
    slots, groups = [], []
    for g, order in enumerate(gather_orders):
        patterns = plane_patterns(order[:-1])
        for part, bit in ((parts[g], 0), (swap_bit(parts[g], *order[-1]), 1)):
            slots.append(part)
            groups.append((wide_rows, g * half, half, tuple(p ^ bit for p in patterns)))
    block = np.arange(devices)
    first_rows = (block % count) * wide_rows + (block // count) * half
    ffn_places = (tuple(int(r) for r in first_rows), tuple(int(b) * half for b in block), half)
    if half % 16 != 0:
        whole_attn = jnp.zeros((FF, D), BF16)
        for part, (scale, shift, _, apart) in zip(slots, groups):
            for slot, bits_apart in enumerate(apart):
                row = (lax.axis_index("dp") ^ bits_apart) * scale + shift
                whole_attn = lax.dynamic_update_slice(whole_attn, part[slot], (row, 0))
        slots, groups = [whole_attn[None]], [(0, 0, FF, (0,))]
        first_all = gathered[:, :half].reshape(2, count, half, D).transpose(1, 0, 2, 3)
        second_all = gathered[:, half:].reshape(FF, D)
        gathered = jnp.concatenate([first_all.reshape(FF, D), second_all], axis=0)[None]
        ffn_places = ((0,), (0,), FF)

    qkv, attended, stats, residual, inner_pair, attn_t = attention_forward(
        first, doc_lengths, me, ends, swapped, small, slots, tuple(groups)
    )
    results, y_low, ffn_pair, ffn_turned, dhs, early = feed_forward(
        first, residual, ends, swapped, small, gathered, ffn_places
    )

    wide_block = lambda device, section: 2 * device + section
    down_block = lambda device, section: section * count + device
    ffn_orders = (
        [bits[0], bits[1], SECTION] + bits[2:],
        [bits[0], SECTION, bits[2], bits[1]] + bits[3:],
    )
    attn_orders = (
        [bits[0], bits[1], bits[2], SECTION] + bits[3:],
        [bits[0], bits[2], bits[1], SECTION] + bits[3:],
    )
    groups = [(ffn_orders[0], wide_block), (ffn_orders[1], lambda d, s: down_block(d, s) + devices)]
    of_kind = lambda i, m: i // 2
    lefts = ffn_turned.reshape(2 * devices, half, L)
    sent, _ = weight_grad(
        me, lefts, count, ffn_pair, groups, 1, False, of_kind, [], "ffn_grad_sent"
    )
    do, delta, turned, inner_pair, out_low = inner_back(
        dhs, attended, small, attn_t, inner_pair, sent
    )
    moved = [swap_bit(s, *o[0]) for s, o in zip(sent, ffn_orders)]
    (low_a, high_a, low_b, high_b), _ = weight_grad(
        me, lefts, count, ffn_pair, groups, 1, False, of_kind, moved, "ffn_grad_kept", [do]
    )
    states = [(low_a, high_a), (low_b, high_b)]
    dq0, dk0, dv0, turned, _ = pair_back(
        0, first, doc_lengths, qkv, do, stats, delta, turned, [high_a, high_b]
    )
    dq1, dk1, dv1, turned, _ = pair_back(
        1, first, doc_lengths, qkv, do, stats, delta, turned
    )
    states = combine(states, [o[1] for o in ffn_orders], [dq1])
    groups = [(order, lambda d, s, g=g: 4 * d + 2 * s + g) for g, order in enumerate(attn_orders)]

    def last_quarter(step, me_ref):
        return jnp.where((step ^ (me_ref[0] >> (len(bits) - 2))) == 3, 1, 0)

    lefts = turned.reshape(2 * devices, half // 2, L)
    attn_sent, token = weight_grad(
        me, lefts, count, inner_pair, groups, 2, True, last_quarter, [],
        "attention_grad_sent", [s for _, s in states],
    )
    grads = (dq0, dk0, dv0, dq1, dk1, dv1)
    results, dx0, low, y_low = input_grad(
        0, 3, first, grads, ends, swapped, dhs, small, attn_t, results, out_low, [token], [y_low]
    )
    returned_x = [lax.ppermute(dx0, "section", [(1, 0)])]
    returned_y = lax.ppermute(y_low, "section", [(0, 1)])
    moved = [swap_bit(s, *o[0]) for s, o in zip(attn_sent, attn_orders)]
    states = combine(states, [o[2] for o in ffn_orders], [dx0])
    (low_a, high_a, low_b, high_b), token = weight_grad(
        me, lefts, count, inner_pair, groups, 2, True, last_quarter, moved,
        "attention_grad_kept", [dx0] + [s for _, s in states],
    )
    attn_states = [(low_a, high_a), (low_b, high_b)]
    states = combine(states, [o[3] for o in ffn_orders], [token])
    results, dx1, low = input_grad(
        3, 1, first, grads, ends, swapped, dhs, small, attn_t, results, low,
        [high_a, high_b] + [s for _, s in states],
    )
    returned_x.append(lax.ppermute(dx1, "section", [(1, 0)]))
    attn_states = combine(
        attn_states, [o[1] for o in attn_orders], [dx1, returned_x[0]]
    )
    for at in range(4, len(ffn_orders[0])):
        states = [reduce_step(s, o[at]) for s, o in zip(states, ffn_orders)]
    first_half, down_grad = states[0][0], states[1][0]
    attn_states = combine(attn_states, [o[2] for o in attn_orders], returned_x[1:] + [returned_y])
    attn_state = tuple(jnp.concatenate(both, axis=1) for both in zip(*attn_states))
    for pair in attn_orders[0][3:]:
        attn_state = reduce_step(attn_state, pair)
    attn_half = attn_state[0]
    results, token = place_results(first, returned_y, returned_x, results)
    late = owned_grads(attn_half, first_half, down_grad, low, early, [token])
    own_half = jnp.where(is_first, attn_half, first_half)
    other_half = swap_bit(jnp.where(is_first, first_half, attn_half), "section", 0)
    late = sum_everywhere(late)
    turned_wide = [a[0].T for a in (wide_master, wide_moment, wide_square)]
    norm, factor, *news = update_all(
        first, late, own_half, other_half, down_grad, turned_wide + [down_master, down_moment, down_square]
    )
    small_news = adamw(
        small_master, small_moment, small_square,
        late[:22].reshape(SMALL) * factor[0, 0], rate_small, 0.0,
    )
    return (
        results[None],
        *[a.T[None] for a in news[:3]],
        *news[3:6],
        *small_news,
        norm[0, 0],
    )


def solution(mesh):
    wide = P("section", None, "dp")
    down = P(("section", "dp"), None)
    ends = P("section", "dp", None)
    return jax.shard_map(
        shards,
        mesh=mesh,
        in_specs=(ends, P("dp", None), wide, wide, wide, down, down, down, P(), P(), P()),
        out_specs=(ends, wide, wide, wide, down, down, down, P(), P(), P(), P()),
        check_vma=False,
    )
```

```python
import functools

import jax
import jax.numpy as jnp
import numpy as np
from jax import lax
from jax.experimental import pallas as pl
from jax.experimental.pallas import tpu as pltpu
from jax.sharding import PartitionSpec as P

D = 768
FF = 3072
HEADS = 12
HEAD_DIM = 64
PAIRS = HEADS // 2
L = 1024
BLOCK = 256
TILES = L // BLOCK
STEP = 8
CHUNK = 512
WIDE_TILE = 512
FFN_TILE = 256
SMALL_AT = {}
offset = 0
for name, width in (
    ("g1", D), ("b1", D), ("bq", D), ("bv", D), ("gi", D), ("bi", D), ("bo", D), ("g2", D), ("b2", D),
    ("c1", FF), ("gh", FF), ("bh", FF), ("c2", D),
):
    SMALL_AT[name] = (offset, width)
    offset += width
SMALL = offset

eps_norm = 1e-05
clip_limit = 1.0
beta_one = 0.9
beta_two = 0.99
adam_eps = 1e-08
decay_weight = 0.1
rate_wide = 0.05
rate_down = 0.025
rate_small = 0.6
masked_score = -1e30

BOTH = ("section", "dp")
F32 = jnp.float32
BF16 = jnp.bfloat16
NN = ((1,), (0,))
NT = ((1,), (1,))
TN = ((0,), (0,))
VMEM_BYTES = 58 * 2**20


def dot(a, b, dims):
    return lax.dot_general(a, b, (dims, ((), ())), preferred_element_type=F32)


def small_row(small_ref, name, start=0, width=None):
    at, full = SMALL_AT[name]
    return small_ref[:, at + start : at + start + (full if width is None else width)]


def normalise(values):
    row_mean = jnp.mean(values, axis=-1, keepdims=True)
    centred = values - row_mean
    spread = jnp.mean(centred * centred, axis=-1, keepdims=True)
    inverse = lax.rsqrt(spread + eps_norm)
    return centred * inverse, inverse


def normalise_back(grad, gain, unit, inverse):
    scaled = grad * gain
    first = jnp.mean(scaled, axis=-1, keepdims=True)
    second = jnp.mean(scaled * unit, axis=-1, keepdims=True)
    return inverse * (scaled - first - unit * second)


def column_sum(values):
    return jnp.sum(values, axis=0, keepdims=True)


def document_ends(lengths_ref, first_ref):
    row = 1 - first_ref[0]
    ends = [lengths_ref[row, 0]]
    for i in (1, 2):
        ends.append(ends[-1] + lengths_ref[row, i])
    return ends


def visible_bias(ends, query_start, key_start, keys):
    key = key_start + lax.broadcasted_iota(jnp.int32, (keys, BLOCK), 0)
    query = query_start + lax.broadcasted_iota(jnp.int32, (1, BLOCK), 1)
    begin = jnp.zeros((1, BLOCK), jnp.int32)
    for end in ends:
        begin = jnp.where(query >= end, end, begin)
    return jnp.where((key >= begin) & (key <= query), 0.0, masked_score).astype(F32)


def halves(pair):
    lane = lax.broadcasted_iota(jnp.int32, pair.shape, 1)
    zero = jnp.zeros_like(pair)
    return jnp.where(lane < HEAD_DIM, pair, zero), jnp.where(lane < HEAD_DIM, zero, pair)


def first_key(tile):
    return max(0, tile - 2) * BLOCK


def attention_kernel(groups, first_ref, lengths_ref, me_ref, own_ref, swapped_ref, small_ref, *refs):
    slots, refs = refs[: len(groups)], refs[len(groups) :]
    qkv_ref, o_ref, stats_ref, hs_ref, pair_ref, held_ref, *refs = refs
    bias_ref, vt_ref, weights_ref, x_ref, a_ref, sem, x_sem, out_sem = refs

    @pl.when(first_ref[0] == 1)
    def _():
        pltpu.make_async_copy(own_ref.at[pl.ds(0, L)], x_ref, x_sem).start()

    @pl.when(first_ref[0] == 0)
    def _():
        pltpu.make_async_copy(swapped_ref, x_ref, x_sem).start()

    copies = []
    for at, (scale, shift, rows, apart) in enumerate(groups):
        for slot, bits in enumerate(apart):
            target = pl.multiple_of((me_ref[0] ^ bits) * scale + shift, 16)
            copies.append(
                pltpu.make_async_copy(
                    slots[at].at[slot], weights_ref.at[pl.ds(target, rows)], sem
                )
            )
    for copy in copies:
        copy.start()
    for copy in copies:
        copy.wait()
    hold = pltpu.make_async_copy(weights_ref, held_ref, out_sem.at[0])
    hold.start()
    pltpu.make_async_copy(swapped_ref, x_ref, x_sem).wait()

    def project(tile, carry):
        rows = pl.ds(pl.multiple_of(tile * WIDE_TILE, WIDE_TILE), WIDE_TILE)
        unit, _ = normalise(x_ref[rows, :].astype(F32))
        a = (unit * small_row(small_ref, "g1") + small_row(small_ref, "b1")).astype(BF16)
        a_ref[rows, :] = a
        q = (dot(a, weights_ref[:D, :], NT) + small_row(small_ref, "bq")).astype(BF16)
        qkv_ref[rows, :D] = q * jnp.asarray(0.125, BF16)
        qkv_ref[rows, D : 2 * D] = dot(a, weights_ref[D : 2 * D, :], NT).astype(BF16)
        v = (dot(a, weights_ref[2 * D : 3 * D, :], NT) + small_row(small_ref, "bv")).astype(BF16)
        qkv_ref[rows, 2 * D :] = v
        vt_ref[:, rows] = v.T
        return carry

    lax.fori_loop(0, L // WIDE_TILE, project, 0)
    hold_a = pltpu.make_async_copy(a_ref, pair_ref.at[0], out_sem.at[1])
    hold_a.start()
    ends = document_ends(lengths_ref, first_ref)

    for tile in range(TILES):
        start = first_key(tile)
        keys = (tile + 1) * BLOCK - start
        rows = slice(tile * BLOCK, (tile + 1) * BLOCK)
        window = slice(start, start + keys)
        bias_ref[:keys, :] = visible_bias(ends, tile * BLOCK, start, keys)

        def one_pair(pair, carry, rows=rows, window=window, keys=keys):
            at = pl.multiple_of(pair * 128, 128)
            q_parts = halves(qkv_ref[rows, pl.ds(at, 128)])
            k = qkv_ref[window, pl.ds(D + at, 128)]
            vt = vt_ref[pl.ds(at, 128), window]
            weights, tops = [], []
            for q_part in q_parts:
                scores = dot(k, q_part, NT) + bias_ref[:keys, :]
                top = jnp.max(scores, axis=0, keepdims=True)
                weights.append(jnp.exp(scores - top).astype(BF16))
                tops.append(top)
            ones = jnp.ones((16, keys), BF16)
            outs = []
            for i in range(2):
                left = jnp.concatenate([vt[i * HEAD_DIM : (i + 1) * HEAD_DIM], ones], axis=0)
                mixed = dot(left, weights[i], NN)
                total = mixed[HEAD_DIM : HEAD_DIM + 1, :]
                outs.append(mixed[:HEAD_DIM, :] / total)
                stats_ref[pair, i : i + 1, rows] = tops[i] + jnp.log(total)
            o_ref[rows, pl.ds(at, 128)] = jnp.concatenate(outs, axis=0).T
            return carry

        lax.fori_loop(0, PAIRS, one_pair, 0, unroll=2)

    def finish(tile, carry):
        rows = pl.ds(pl.multiple_of(tile * WIDE_TILE, WIDE_TILE), WIDE_TILE)
        unit, _ = normalise(o_ref[rows, :])
        u = (unit * small_row(small_ref, "gi") + small_row(small_ref, "bi")).astype(BF16)
        h = x_ref[rows, :].astype(F32) + dot(u, weights_ref[3 * D :, :], NT)
        hs_ref[rows, :] = (h + small_row(small_ref, "bo")).astype(BF16)
        return carry

    lax.fori_loop(0, L // WIDE_TILE, finish, 0)
    hold.wait()
    hold_a.wait()


def whole(memory_space=pltpu.VMEM):
    return pl.BlockSpec(memory_space=memory_space)


def beside(kernel, inputs, outputs, waits, carried):
    def body(*refs):
        passed = len(waits) + len(carried)
        after_inputs = refs[inputs + passed :]
        kernel(*refs[:inputs], *after_inputs[:outputs], *after_inputs[outputs + len(carried) :])

    return body


def shapes_of(arrays):
    return tuple(jax.ShapeDtypeStruct(a.shape, a.dtype) for a in arrays)


def attention_forward(first, lengths, me, ends_in, swapped, small, slots, groups):
    return pl.pallas_call(
        functools.partial(attention_kernel, groups),
        out_shape=(
            jax.ShapeDtypeStruct((L, 3 * D), BF16),
            jax.ShapeDtypeStruct((L, D), F32),
            jax.ShapeDtypeStruct((PAIRS, 2, L), F32),
            jax.ShapeDtypeStruct((L, D), BF16),
            jax.ShapeDtypeStruct((2, L, D), BF16),
            jax.ShapeDtypeStruct((FF, D), BF16),
        ),
        in_specs=[whole(pltpu.SMEM)] * 3 + [whole(pl.ANY)] * 2 + [whole()]
        + [whole(pl.ANY)] * len(slots),
        out_specs=(whole(),) * 4 + (whole(pl.ANY),) * 2,
        scratch_shapes=[
            pltpu.VMEM((3 * BLOCK, BLOCK), F32),
            pltpu.VMEM((D, L), BF16),
            pltpu.VMEM((FF, D), BF16),
            pltpu.VMEM((L, D), BF16),
            pltpu.VMEM((L, D), BF16),
            pltpu.SemaphoreType.DMA,
            pltpu.SemaphoreType.DMA,
            pltpu.SemaphoreType.DMA((2,)),
        ],
        compiler_params=pltpu.CompilerParams(vmem_limit_bytes=VMEM_BYTES),
        cost_estimate=pl.CostEstimate(flops=14 * 10**9, bytes_accessed=20 * 10**6, transcendentals=0),
        name="attention_forward",
    )(first, lengths, me, ends_in, swapped, small, *slots)


def gelu_parts(x):
    size = jnp.abs(x)
    bell = jnp.exp(x * x * -0.5)
    t = 1.0 / (1.0 + size * (0.3275911 * 0.5**0.5))
    tail = t * (0.5 * 0.254829592 + t * (0.5 * -0.284496736 + t * (
        0.5 * 1.421413741 + t * (0.5 * -1.453152027 + t * (0.5 * 1.061405429)))))
    tail = tail * bell
    phi = jnp.where(x > 0, 1.0 - tail, tail)
    return x * phi, phi + x * bell * 0.3989422804014327


def ffn_kernel(
    places, chosen_ref, hs_ref, lower_ref, swapped_ref, small_ref, slots_ref,
    y_ref, sent_ref, pair_ref, turned_ref, dhs_ref, wide_ref,
    g_ref, slope_ref, t_ref, held_ref, first_ref, second_ref, sems,
):
    first_rows, second_rows, rows = places

    def weight_copies(into_ref, rows_of, start, sem):
        return [
            pltpu.make_async_copy(
                slots_ref.at[block, pl.ds(start, rows)], into_ref.at[pl.ds(row, rows)], sem
            )
            for block, row in enumerate(rows_of)
        ]

    @pl.when(pl.program_id(0) == 0)
    def _():
        wide_ref[...] = jnp.zeros_like(wide_ref)
        copies = weight_copies(first_ref, first_rows, 0, sems.at[0])
        for copy in copies + weight_copies(second_ref, second_rows, rows, sems.at[1]):
            copy.start()
        for copy in copies:
            copy.wait()

    hs = hs_ref[...].astype(F32)
    unit, inverse = normalise(hs)
    e = (unit * small_row(small_ref, "g2") + small_row(small_ref, "b2")).astype(BF16)
    pair_ref[0] = e
    dy = jnp.where(chosen_ref[0] == 1, swapped_ref[...], lower_ref[...])
    pair_ref[1] = dy
    chunks = [slice(j, j + CHUNK) for j in range(0, FF, CHUNK)]

    total = jnp.zeros((FFN_TILE, 1), F32)
    for cut in chunks:
        f = dot(e, first_ref[cut, :], NT) + small_row(small_ref, "c1", cut.start, CHUNK)
        g, slope = gelu_parts(f)
        g_ref[:, cut] = g
        slope_ref[:, cut] = slope
        total = total + jnp.sum(g, axis=1, keepdims=True)
    mean = total / FF
    total = jnp.zeros((FFN_TILE, 1), F32)
    for cut in chunks:
        centred = g_ref[:, cut] - mean
        total = total + jnp.sum(centred * centred, axis=1, keepdims=True)
    inner_inverse = lax.rsqrt(total / FF + eps_norm)

    step = pl.program_id(0)
    columns = pl.ds(pl.multiple_of(step * FFN_TILE, FFN_TILE), FFN_TILE)
    flush = pltpu.make_async_copy(held_ref, turned_ref.at[:, :, columns], sems.at[2])

    @pl.when(step == 0)
    def _():
        for copy in weight_copies(second_ref, second_rows, rows, sems.at[1]):
            copy.wait()

    @pl.when(step > 0)
    def _():
        flush.wait()

    y = hs + small_row(small_ref, "c2")
    first_sum = jnp.zeros((FFN_TILE, 1), F32)
    second_sum = jnp.zeros((FFN_TILE, 1), F32)
    for cut in chunks:
        gain = small_row(small_ref, "gh", cut.start, CHUNK)
        ghat = (g_ref[:, cut] - mean) * inner_inverse
        g_ref[:, cut] = ghat
        n = (ghat * gain + small_row(small_ref, "bh", cut.start, CHUNK)).astype(BF16)
        held_ref[1, cut, :] = n.T
        y = y + dot(n, second_ref[cut, :], NN)
        dn = dot(dy, second_ref[cut, :], NT)
        wide_ref[0:1, cut] += column_sum(dn * ghat)
        wide_ref[1:2, cut] += column_sum(dn)
        scaled = dn * gain
        t_ref[:, cut] = scaled
        first_sum = first_sum + jnp.sum(scaled, axis=1, keepdims=True)
        second_sum = second_sum + jnp.sum(scaled * ghat, axis=1, keepdims=True)
    y_ref[...] = y
    sent_ref[...] = y.astype(BF16)
    first_sum = first_sum / FF
    second_sum = second_sum / FF

    de = jnp.zeros((FFN_TILE, D), F32)
    for cut in chunks:
        back = t_ref[:, cut] - first_sum - g_ref[:, cut] * second_sum
        df = (inner_inverse * back * slope_ref[:, cut]).astype(BF16)
        held_ref[0, cut, :] = df.T
        wide_ref[2:3, cut] += column_sum(df.astype(F32))
        de = de + dot(df, first_ref[cut, :], NN)
    flush.start()

    dyf = dy.astype(F32)
    wide_ref[3:4, :D] += column_sum(de * unit)
    wide_ref[3:4, D : 2 * D] += column_sum(de)
    wide_ref[3:4, 2 * D : 3 * D] += column_sum(dyf)
    dhp = normalise_back(de, small_row(small_ref, "g2"), unit, inverse)
    dhs_ref[...] = (dyf + dhp).astype(BF16)

    @pl.when(step == pl.num_programs(0) - 1)
    def _():
        flush.wait()


def feed_forward(chosen, hs, ends_in, swapped, small, slots, places):
    at = L // FFN_TILE
    tile = lambda shift=0: pl.BlockSpec((FFN_TILE, D), lambda i: (i + shift, 0))
    keep = lambda shape: pl.BlockSpec(shape, lambda i: (0, 0), pipeline_mode=pl.Buffered(1))
    return pl.pallas_call(
        functools.partial(ffn_kernel, places),
        grid=(at,),
        out_shape=(
            jax.ShapeDtypeStruct((2 * L, D), F32),
            jax.ShapeDtypeStruct((L, D), BF16),
            jax.ShapeDtypeStruct((2, L, D), BF16),
            jax.ShapeDtypeStruct((2, FF, L), BF16),
            jax.ShapeDtypeStruct((L, D), BF16),
            jax.ShapeDtypeStruct((4, FF), F32),
        ),
        in_specs=[whole(pltpu.SMEM), tile(), tile(at), tile(), keep((1, SMALL)), whole(pl.ANY)],
        out_specs=(
            tile(at), tile(),
            pl.BlockSpec((2, FFN_TILE, D), lambda i: (0, i, 0)),
            whole(pl.ANY),
            tile(),
            pl.BlockSpec((4, FF), lambda i: (0, 0)),
        ),
        scratch_shapes=[pltpu.VMEM((FFN_TILE, FF), F32)] * 3
        + [pltpu.VMEM((2, FF, FFN_TILE), BF16)]
        + [pltpu.VMEM((FF, D), BF16)] * 2
        + [pltpu.SemaphoreType.DMA((3,))],
        compiler_params=pltpu.CompilerParams(vmem_limit_bytes=VMEM_BYTES),
        cost_estimate=pl.CostEstimate(flops=40 * 10**9, bytes_accessed=30 * 10**6, transcendentals=0),
        name="feed_forward",
    )(chosen, hs, ends_in, swapped, small, slots)


TOKEN = jax.ShapeDtypeStruct((8, 128), F32)


def weight_grad_kernel(plan, me_ref, *refs):
    lefts, right_ref = refs[: plan["lefts"]], refs[plan["lefts"]]
    refs = refs[plan["lefts"] + 1 :]
    moved, outs, token_ref = refs[: plan["moved"]], refs[plan["moved"] : -1], refs[-1]
    rows = lefts[0].shape[1]
    blocks = [ref[0] for ref in lefts]
    token_ref[...] = jnp.zeros_like(token_ref)
    if rows % 16 == 0:
        value = dot(jnp.concatenate(blocks, axis=0), right_ref[0], NN)
        parts = [value[at * rows : (at + 1) * rows] for at in range(len(blocks))]
    else:
        parts = [dot(block, right_ref[0], NN) for block in blocks]
    split = plan["split"]
    step = pl.program_id(0) % 2**split
    kind = pl.program_id(0) // 2**split

    def store(group, parts):
        views = plan["views"][group]
        for at, part in enumerate(parts):
            place = tuple(int(p) for p in np.unravel_index(at, views))
            if not moved:
                outs[group][place] = part.astype(BF16)
                continue
            total = part + moved[group][place].astype(F32)
            low_ref, high_ref = outs[2 * group : 2 * group + 2]
            first_bit = plan["first"][group]
            if first_bit is None:
                if place[0] == 0:
                    low_ref[place[1:]] = total
                else:
                    high_ref[place[1:]] = total.astype(BF16)
                continue

            @pl.when((step >> first_bit) & 1 == 0)
            def _():
                low_ref[place[1:]] = total

            @pl.when((step >> first_bit) & 1 == 1)
            def _():
                high_ref[place[1:]] = total.astype(BF16)

    if plan["joint"]:
        count = len(parts) // 2
        for group in range(2):
            store(group, parts[group * count : (group + 1) * count])
    else:
        for group in range(2):

            @pl.when(kind == group)
            def _():
                store(group, parts)


def weight_grad(me, left, count, right, groups, split, joint, right_of, moved, name, waits=()):
    bits = count.bit_length() - 1
    rows = left.shape[1]
    steps = 2**split
    top = [("dp", bits - 1 - i) for i in range(split)]
    shift = bits - split
    in_specs, outs, out_specs, views, firsts, combos = [], [], [], [], [], []
    moved_specs = []

    def row_of(group, combo, step, me_ref):
        order, row_block = groups[group]
        free = [pair for pair in order[1:] if pair not in top]
        apart, across = (0 if moved else 1), 0
        for at, (axis, bit) in enumerate(free):
            on = (combo >> (len(free) - 1 - at)) & 1
            if axis == "dp":
                apart |= on << bit
            else:
                across = on
        return row_block((apart + (step << shift)) ^ me_ref[0], across ^ me_ref[1])

    def local_step(i, group):
        if joint:
            return i
        return jnp.clip(i - group * steps, 0, steps - 1)

    free_count = 2 ** (len(groups[0][0]) - 1 - split)
    if joint:
        for group in range(2):
            for combo in range(free_count):
                in_specs.append(
                    pl.BlockSpec(
                        (1, rows, L),
                        lambda i, m, g=group, c=combo: (row_of(g, c, i, m), 0, 0),
                    )
                )
    else:
        for combo in range(free_count):

            def place(i, m, c=combo):
                step = i % steps
                return jnp.where(i < steps, row_of(0, c, step, m), row_of(1, c, step, m)), 0, 0

            in_specs.append(pl.BlockSpec((1, rows, L), place))
    lefts = len(in_specs)
    in_specs.append(pl.BlockSpec((1, L, D), lambda i, m: (right_of(i, m), 0, 0)))

    for group, (order, _) in enumerate(groups):
        order = order[1:]

        def spots(i, m, pairs=order, group=group):
            step = local_step(i, group)
            return (*[(step >> (p[1] - shift)) & 1 if p in top else 0 for p in pairs], 0, 0)

        view = tuple(1 if pair in top else 2 for pair in order)
        views.append(view)
        firsts.append(order[0][1] - shift if order[0] in top else None)
        full = pl.BlockSpec((*view, rows, D), spots)
        if moved:
            moved_specs.append(full)
            half = pl.BlockSpec(
                (*view[1:], rows, D), lambda i, m, spots=spots: spots(i, m)[1:]
            )
            out_specs += [half, half]
            shape = (2,) * (len(order) - 1) + (rows, D)
            outs += [jax.ShapeDtypeStruct(shape, F32), jax.ShapeDtypeStruct(shape, BF16)]
        else:
            out_specs.append(full)
            outs.append(jax.ShapeDtypeStruct((2,) * len(order) + (rows, D), BF16))
    plan = dict(
        lefts=lefts, moved=len(moved), split=split, views=views, first=firsts, joint=joint
    )
    moved = [m.reshape((2,) * (len(groups[0][0]) - 1) + (rows, D)) for m in moved]
    inputs = len(in_specs) + len(moved) + 1
    *results, token = pl.pallas_call(
        beside(functools.partial(weight_grad_kernel, plan), inputs, len(outs) + 1, waits, ()),
        grid_spec=pltpu.PrefetchScalarGridSpec(
            num_scalar_prefetch=1,
            grid=(steps if joint else 2 * steps,),
            in_specs=in_specs + moved_specs + [whole(pl.ANY)] * len(waits),
            out_specs=tuple(out_specs) + (pl.BlockSpec((8, 128), lambda i, m: (0, 0)),),
        ),
        out_shape=tuple(outs) + (TOKEN,),
        compiler_params=pltpu.CompilerParams(vmem_limit_bytes=VMEM_BYTES),
        cost_estimate=pl.CostEstimate(flops=6 * 10**9, bytes_accessed=9 * 10**6, transcendentals=0),
        name=name,
    )(me, *[left] * lefts, right, *moved, *waits)
    return [r.reshape(-1, rows, D) for r in results], token


def inner_back_kernel(
    dhs_ref, o_ref, small_ref, weights_ref, pair_ref, do_ref, delta_ref, turned_ref, u_ref, low_ref
):
    @pl.when(pl.program_id(0) == 0)
    def _():
        low_ref[...] = jnp.zeros_like(low_ref)

    o = o_ref[...]
    unit, inverse = normalise(o)
    gain = small_row(small_ref, "gi")
    u_ref[0] = (unit * gain + small_row(small_ref, "bi")).astype(BF16)
    dhs = dhs_ref[...]
    turned_ref[0] = dhs.T
    du = dot(dhs, weights_ref[...], NN)
    low_ref[4:5, :] += column_sum(du * unit)
    low_ref[5:6, :] += column_sum(du)
    low_ref[6:7, :] += column_sum(dhs.astype(F32))
    do = normalise_back(du, gain, unit, inverse).astype(BF16)
    do_ref[...] = do
    product = (do.astype(F32) * o).T
    for head in range(HEADS):
        delta_ref[head // 2, head % 2 : head % 2 + 1, :] = column_sum(
            product[head * HEAD_DIM : (head + 1) * HEAD_DIM, :]
        )


def inner_back(dhs, o, small, weights, pair, waits=()):
    tile = lambda width: pl.BlockSpec((BLOCK, width), lambda i: (i, 0))
    return pl.pallas_call(
        beside(inner_back_kernel, 5, 5, waits, ()),
        grid=(TILES,),
        out_shape=(
            jax.ShapeDtypeStruct((L, D), BF16),
            jax.ShapeDtypeStruct((PAIRS, 2, L), F32),
            jax.ShapeDtypeStruct((4, D, L), BF16),
            jax.ShapeDtypeStruct((2, L, D), BF16),
            jax.ShapeDtypeStruct((8, D), F32),
        ),
        in_specs=[
            tile(D),
            tile(D),
            pl.BlockSpec((1, SMALL), lambda i: (0, 0), pipeline_mode=pl.Buffered(1)),
            pl.BlockSpec((D, D), lambda i: (3, 0), pipeline_mode=pl.Buffered(1)),
            whole(pl.ANY),
        ]
        + [whole(pl.ANY)] * len(waits),
        out_specs=(
            tile(D),
            pl.BlockSpec((PAIRS, 2, BLOCK), lambda i: (0, 0, i)),
            pl.BlockSpec((1, D, BLOCK), lambda i: (3, 0, i)),
            pl.BlockSpec((1, BLOCK, D), lambda i: (1, i, 0)),
            pl.BlockSpec((8, D), lambda i: (0, 0)),
        ),
        input_output_aliases={4: 3},
        compiler_params=pltpu.CompilerParams(vmem_limit_bytes=VMEM_BYTES),
        cost_estimate=pl.CostEstimate(flops=6 * 10**9, bytes_accessed=15 * 10**6, transcendentals=0),
        name="inner_back",
    )(dhs, o, small, weights, pair, *waits)


GROUP = 3


def pair_back_kernel(
    first_ref, lengths_ref, q_ref, k_ref, v_ref, do_ref, stats_ref, delta_ref, earlier_ref,
    dq_ref, dk_ref, dv_ref, turned_ref, token_ref, bias_ref, dk_sum, dv_sum,
):
    token_ref[...] = jnp.zeros_like(token_ref)

    @pl.when(pl.program_id(0) == 0)
    def _():
        ends = document_ends(lengths_ref, first_ref)
        for tile in range(TILES):
            start = first_key(tile)
            keys = (tile + 1) * BLOCK - start
            bias_ref[tile, :keys, :] = visible_bias(ends, tile * BLOCK, start, keys)

    dk_sum[...] = jnp.zeros_like(dk_sum)
    dv_sum[...] = jnp.zeros_like(dv_sum)
    for tile in range(TILES):
        start = first_key(tile)
        keys = (tile + 1) * BLOCK - start
        rows = slice(tile * BLOCK, (tile + 1) * BLOCK)
        window = slice(start, start + keys)
        q_parts = halves(q_ref[rows, :])
        do_parts = halves(do_ref[rows, :])
        q_turned, do_turned = q_ref[rows, :].T, do_ref[rows, :].T
        k = k_ref[window, :]
        v = v_ref[window, :]
        kt = k.T
        dqs = []
        for i in range(2):
            scores = dot(k, q_parts[i], NT) + bias_ref[tile, :keys, :]
            probs = jnp.exp(scores - stats_ref[0, i : i + 1, rows])
            dprobs = dot(v, do_parts[i], NT)
            ds = (probs * (dprobs - delta_ref[0, i : i + 1, rows])).astype(BF16)
            half = slice(i * HEAD_DIM, (i + 1) * HEAD_DIM)
            dv_sum[half, window] += dot(do_turned[half], probs.astype(BF16), NT)
            dk_sum[half, window] += dot(q_turned[half], ds, NT)
            dqs.append(dot(kt[i * HEAD_DIM : (i + 1) * HEAD_DIM], ds, NN))
        dq = (jnp.concatenate(dqs, axis=0) * 0.125).astype(BF16)
        turned_ref[0, :, rows] = dq
        dq_ref[rows, :] = dq.T
    for part, sum_ref, out_ref in ((1, dk_sum, dk_ref), (2, dv_sum, dv_ref)):
        grad = sum_ref[...].astype(BF16)
        turned_ref[part] = grad
        out_ref[...] = grad.T


def pair_back(part, first_flag, lengths, qkv, do, stats, delta, turned, waits=()):
    first = part * GROUP
    column = lambda base: pl.BlockSpec((L, 128), lambda i: (0, base + first + i))
    rows = pl.BlockSpec((1, 2, L), lambda i: (first + i, 0, 0))
    out = pl.BlockSpec((L, 128), lambda i: (0, i))
    width = GROUP * 128
    return pl.pallas_call(
        beside(pair_back_kernel, 9, 5, waits, ()),
        grid=(GROUP,),
        out_shape=(jax.ShapeDtypeStruct((L, width), BF16),) * 3
        + (jax.ShapeDtypeStruct((4, D, L), BF16), TOKEN),
        in_specs=[
            whole(pltpu.SMEM), whole(pltpu.SMEM), column(0), column(PAIRS), column(2 * PAIRS), column(0), rows, rows,
            whole(pl.ANY),
        ]
        + [whole(pl.ANY)] * len(waits),
        out_specs=(out,) * 3 + (
            pl.BlockSpec((3, 128, L), lambda i: (0, first + i, 0)),
            pl.BlockSpec((8, 128), lambda i: (0, 0)),
        ),
        input_output_aliases={8: 3},
        scratch_shapes=[
            pltpu.VMEM((TILES, 3 * BLOCK, BLOCK), F32),
            pltpu.VMEM((128, L), F32),
            pltpu.VMEM((128, L), F32),
        ],
        compiler_params=pltpu.CompilerParams(vmem_limit_bytes=VMEM_BYTES),
        cost_estimate=pl.CostEstimate(flops=13 * 10**9, bytes_accessed=15 * 10**6, transcendentals=0),
        name="pair_back",
    )(first_flag, lengths, qkv, qkv, qkv, do, stats, delta, turned, *waits)


def input_grad_kernel(
    first_ref, dq0, dk0, dv0, dq1, dk1, dv1, own_ref, swapped_ref, dhs_ref, small_ref, weights_ref,
    results_ref, earlier_ref, dx_ref, sent_ref, low_ref,
):
    @pl.when(pl.program_id(0) == 0)
    def _():
        low_ref[...] = earlier_ref[...]

    x = jnp.where(first_ref[0] == 1, own_ref[...], swapped_ref[...])
    unit, inverse = normalise(x.astype(F32))
    gain = small_row(small_ref, "g1")
    grads = [ref[...] for ref in (dq0, dq1, dk0, dk1, dv0, dv1)]
    width = GROUP * 128
    da = dot(jnp.concatenate(grads, axis=1), weights_ref[...], NN)
    for at, grad in enumerate(grads):
        if at < 2 or at > 3:
            row = 2 if at < 2 else 3
            cut = slice((at % 2) * width, (at % 2 + 1) * width)
            low_ref[row : row + 1, cut] += column_sum(grad.astype(F32))
    low_ref[0:1, :] += column_sum(da * unit)
    low_ref[1:2, :] += column_sum(da)
    dx = normalise_back(da, gain, unit, inverse) + dhs_ref[...].astype(F32)
    dx_ref[...] = dx
    sent_ref[...] = dx.astype(BF16)


def input_grad(start, tiles, first, grads, ends_in, swapped, dhs, small, weights, results, earlier, waits=(), carried=()):
    tile = lambda width: pl.BlockSpec((BLOCK, width), lambda i: (i + start, 0))
    keep = lambda shape: pl.BlockSpec(shape, lambda i: (0, 0), pipeline_mode=pl.Buffered(1))
    return pl.pallas_call(
        beside(input_grad_kernel, 14, 3, waits, carried),
        grid=(tiles,),
        out_shape=(
            jax.ShapeDtypeStruct((2 * L, D), F32),
            jax.ShapeDtypeStruct((tiles * BLOCK, D), BF16),
            jax.ShapeDtypeStruct((8, D), F32),
        )
        + shapes_of(carried),
        in_specs=[whole(pltpu.SMEM)] + [tile(GROUP * 128)] * 6
        + [tile(D)] * 3 + [keep((1, SMALL)), keep((3 * D, D))]
        + [whole(pl.ANY), keep((8, D))]
        + [whole(pl.ANY)] * (len(waits) + len(carried)),
        out_specs=(
            tile(D),
            pl.BlockSpec((BLOCK, D), lambda i: (i, 0)),
            pl.BlockSpec((8, D), lambda i: (0, 0)),
        )
        + (whole(pl.ANY),) * len(carried),
        input_output_aliases={12: 0} | {14 + len(waits) + i: 3 + i for i in range(len(carried))},
        compiler_params=pltpu.CompilerParams(vmem_limit_bytes=VMEM_BYTES),
        cost_estimate=pl.CostEstimate(flops=4 * 10**9, bytes_accessed=10 * 10**6, transcendentals=0),
        name="input_grad",
    )(first, *grads, ends_in, swapped, dhs, small, weights, results, earlier, *waits, *carried)


def place_kernel(first_ref, y_ref, dx0_ref, dx1_ref, results_ref, out_ref, token_ref):
    token_ref[...] = jnp.zeros_like(token_ref)
    is_dx = first_ref[0] == 1
    step = pl.program_id(0)

    @pl.when(step == 0)
    def _():
        out_ref[...] = jnp.where(is_dx, dx0_ref[:WIDE_TILE, :], y_ref[...]).astype(F32)

    @pl.when(step == 1)
    def _():
        dx = jnp.concatenate([dx0_ref[WIDE_TILE:, :], dx1_ref[...]], axis=0)
        out_ref[...] = jnp.where(is_dx, dx, y_ref[...]).astype(F32)


def place_results(first, y, dx, results):
    tile = pl.BlockSpec((WIDE_TILE, D), lambda i, f: (i, 0))
    return pl.pallas_call(
        place_kernel,
        grid_spec=pltpu.PrefetchScalarGridSpec(
            num_scalar_prefetch=1,
            grid=(L // WIDE_TILE,),
            in_specs=[tile] + [pl.BlockSpec(d.shape, lambda i, f: (0, 0)) for d in dx]
            + [whole(pl.ANY)],
            out_specs=(
                pl.BlockSpec((WIDE_TILE, D), lambda i, f: (i + f[0] * (L // WIDE_TILE), 0)),
                pl.BlockSpec((8, 128), lambda i, f: (0, 0)),
            ),
        ),
        out_shape=(jax.ShapeDtypeStruct((2 * L, D), F32), TOKEN),
        input_output_aliases={4: 0},
        cost_estimate=pl.CostEstimate(flops=10**6, bytes_accessed=8 * 10**6, transcendentals=0),
        name="place_results",
    )(first, y, *dx, results)


def combine_kernel(groups, *refs):
    inputs, outputs = refs[: 4 * groups], refs[4 * groups :]
    for g in range(groups):
        low, high, low_in, high_in = inputs[4 * g : 4 * g + 4]
        kept_ref, sent_ref = outputs[2 * g : 2 * g + 2]
        kept_ref[...] = low[...] + low_in[...].astype(F32)
        sent_ref[...] = (high[...] + high_in[...].astype(F32)).astype(BF16)


def combine(states, bits, waits=()):
    moved = [swap_bit(sent, *bit) for (_, sent), bit in zip(states, bits)]
    half = states[0][0].shape[0] // 2
    steps = min(half, 2)
    block = (half // steps,) + states[0][0].shape[1:]
    operands, in_specs, out_shape, out_specs = [], [], [], []
    lower = pl.BlockSpec(block, lambda i: (i, 0, 0))
    upper = pl.BlockSpec(block, lambda i: (i + steps, 0, 0))
    for (kept, _), other in zip(states, moved):
        operands += [kept, kept, other, other]
        in_specs += [lower, upper, lower, upper]
        shape = (half,) + kept.shape[1:]
        out_shape += [jax.ShapeDtypeStruct(shape, F32), jax.ShapeDtypeStruct(shape, BF16)]
        out_specs += [lower, lower]
    outs = pl.pallas_call(
        beside(
            functools.partial(combine_kernel, len(states)), len(operands), len(out_shape), waits, ()
        ),
        grid=(steps,),
        in_specs=in_specs + [whole(pl.ANY)] * len(waits),
        out_specs=tuple(out_specs),
        out_shape=tuple(out_shape),
        compiler_params=pltpu.CompilerParams(vmem_limit_bytes=VMEM_BYTES),
        cost_estimate=pl.CostEstimate(flops=10**6, bytes_accessed=8 * 10**6, transcendentals=0),
        name="combine",
    )(*operands, *waits)
    return [(outs[2 * g], outs[2 * g + 1]) for g in range(len(states))]


def owned_kernel(attn_ref, first_ref, down_ref, low_ref, early_ref, late_ref):
    total = jnp.zeros((1, 1), F32)
    for ref in (attn_ref, first_ref, down_ref):
        total = total + jnp.sum(column_sum(ref[...] * ref[...]), axis=1, keepdims=True)
    late_ref[...] = jnp.zeros_like(late_ref)
    late_ref[:7, :] = low_ref[:7, :]
    order = [(3, 0), (3, 1)] + [(row, part) for row in (2, 0, 1) for part in range(4)] + [(3, 2)]
    for at, (row, part) in enumerate(order):
        late_ref[7 + at : 8 + at, :] = early_ref[row : row + 1, part * D : (part + 1) * D]
    late_ref[22:23, :] = jnp.broadcast_to(total, (1, D))


def owned_grads(attn, first, down, low, early, waits):
    return pl.pallas_call(
        beside(owned_kernel, 5, 1, waits, ()),
        in_specs=[whole()] * 5 + [whole(pl.ANY)] * len(waits),
        out_specs=whole(),
        out_shape=jax.ShapeDtypeStruct((24, D), F32),
        name="owned_grads",
    )(attn, first, down, low, early, *waits)


def update_kernel(first_ref, late_ref, own_ref, other_ref, down_ref, *refs):
    states, norm_ref, factor_ref, outs = refs[:6], refs[6], refs[7], refs[8:]
    grads = late_ref[:22, :]
    norm = jnp.sqrt(late_ref[22:23, 0:1] + jnp.sum(column_sum(grads * grads), axis=1, keepdims=True))
    factor = clip_limit / jnp.maximum(norm, clip_limit)
    norm_ref[...] = norm
    factor_ref[...] = factor
    half = own_ref.shape[0]
    upper = jnp.where(first_ref[0] == 1, own_ref[...], other_ref[...])
    lower = jnp.where(first_ref[0] == 1, other_ref[...], own_ref[...])
    jobs = (
        (0, slice(0, half), upper, rate_wide),
        (0, slice(half, 2 * half), lower, rate_wide),
        (1, slice(0, half), down_ref[...], rate_down),
    )
    for kind, rows, grad, rate in jobs:
        master, moment, square = [ref[rows, :] for ref in states[3 * kind : 3 * kind + 3]]
        news = adamw(master, moment, square, grad * factor, rate, decay_weight)
        for new, out_ref in zip(news, outs[3 * kind : 3 * kind + 3]):
            out_ref[rows, :] = new


def update_all(first, late, own, other, down, states):
    scalar = jax.ShapeDtypeStruct((1, 1), F32)
    return pl.pallas_call(
        update_kernel,
        in_specs=[whole(pltpu.SMEM)] + [whole()] * 10,
        out_specs=(whole(),) * 8,
        out_shape=(scalar, scalar) + shapes_of(states),
        compiler_params=pltpu.CompilerParams(vmem_limit_bytes=VMEM_BYTES),
        name="update_all",
    )(first, late, own, other, down, *states)


SECTION = ("section", 0)


def swap_bit(value, axis, bit):
    mask = 2**bit
    return lax.ppermute(value, axis, [(i, i ^ mask) for i in range(lax.axis_size(axis))])


def swap_mask(value, mask):
    pairs = [(i, i ^ mask) for i in range(2 * lax.axis_size("dp"))]
    return lax.ppermute(value, BOTH, pairs)


def sum_everywhere(value):
    size = lax.axis_size("dp")
    masks = [1, size] + [2**b for b in range(1, size.bit_length() - 1)]
    while masks:
        if len(masks) % 2 == 1:
            value = value + swap_mask(value, masks.pop(0))
            continue
        one, two = masks.pop(0), masks.pop(0)
        across = [swap_mask(value, mask) for mask in (one, two, one | two)]
        value = (value + across[0]) + (across[1] + across[2])
    return value


def axis_bits():
    return [("dp", b) for b in range(lax.axis_size("dp").bit_length() - 1)]


def plane_patterns(order):
    slot = np.arange(2 ** len(order), dtype=np.int32)
    apart = np.zeros_like(slot)
    for at, (_, bit) in enumerate(order):
        apart |= ((slot >> at) & 1) << bit
    return tuple(int(a) for a in apart)


def gather_steps(own, order):
    held = own
    for axis, bit in order:
        held = jnp.concatenate([held, swap_bit(held, axis, bit)], axis=0)
    return held


def reduce_step(state, bit):
    kept, sent = state
    moved = swap_bit(sent, *bit).astype(F32)
    half = kept.shape[0] // 2
    if half == 0:
        return kept[0] + moved[0], None
    return kept[:half] + moved[:half], (kept[half:] + moved[half:]).astype(BF16)


def after(values, *others):
    return lax.optimization_barrier((values, others))[0]


def adamw(master, moment, square, clipped, step_rate, decay):
    moment_new = beta_one * moment + (1.0 - beta_one) * clipped
    square_new = beta_two * square + (1.0 - beta_two) * clipped * clipped
    moment_hat = moment_new / (1.0 - beta_one**STEP)
    square_hat = square_new / (1.0 - beta_two**STEP)
    master_new = master - step_rate * (
        moment_hat / (jnp.sqrt(square_hat) + adam_eps) + decay * master
    )
    return (moment_new, square_new, master_new)


def shards(
    layer_ends,
    doc_lengths,
    wide_master,
    wide_moment,
    wide_square,
    down_master,
    down_moment,
    down_square,
    small_master,
    small_moment,
    small_square,
):
    is_first = lax.axis_index("section") == 0
    count = lax.axis_size("dp")
    devices = 2 * count
    wide_rows = FF // count
    half_rows = wide_rows // 2
    small = small_master.reshape(1, SMALL)
    bits = axis_bits()
    reduce_orders = (bits, [bits[0], bits[2], bits[1]] + bits[3:])
    gather_orders = tuple(order[::-1] for order in reduce_orders)
    device = np.arange(count)
    half = half_rows

    own = wide_master[0].T.astype(BF16)
    other = swap_bit(own, "section", 0)
    attn_own = jnp.where(is_first, own, other)
    first_own = jnp.where(is_first, other[:half], own[half:])
    gathered = lax.all_gather(
        jnp.concatenate([first_own, down_master.astype(BF16)], axis=0), BOTH, axis=0, tiled=False
    )

    first = is_first.astype(jnp.int32)[None]
    me = jnp.stack([lax.axis_index("dp"), lax.axis_index("section")]).astype(jnp.int32)
    ends = layer_ends[0]
    to_swap = after(jnp.where(is_first, ends[L:], ends[:L]), other)
    swapped = swap_bit(to_swap, "section", 0)

    shared = 0
    while gather_orders[0][shared] == gather_orders[1][shared]:
        shared += 1
    held = gather_steps(attn_own[None], gather_orders[0][:shared])
    parts = [
        gather_steps(held[:, g * half : (g + 1) * half], gather_orders[g][shared:-1])
        for g in range(2)
    ]
    parts[1] = after(parts[1], swapped)
    slots, groups = [], []
    for g, order in enumerate(gather_orders):
        patterns = plane_patterns(order[:-1])
        for part, bit in ((parts[g], 0), (swap_bit(parts[g], *order[-1]), 1)):
            slots.append(part)
            groups.append((wide_rows, g * half, half, tuple(p ^ bit for p in patterns)))
    block = np.arange(devices)
    first_rows = (block % count) * wide_rows + (block // count) * half
    ffn_places = (tuple(int(r) for r in first_rows), tuple(int(b) * half for b in block), half)
    if half % 16 != 0:
        whole_attn = jnp.zeros((FF, D), BF16)
        for part, (scale, shift, _, apart) in zip(slots, groups):
            for slot, bits_apart in enumerate(apart):
                row = (lax.axis_index("dp") ^ bits_apart) * scale + shift
                whole_attn = lax.dynamic_update_slice(whole_attn, part[slot], (row, 0))
        slots, groups = [whole_attn[None]], [(0, 0, FF, (0,))]
        first_all = gathered[:, :half].reshape(2, count, half, D).transpose(1, 0, 2, 3)
        second_all = gathered[:, half:].reshape(FF, D)
        gathered = jnp.concatenate([first_all.reshape(FF, D), second_all], axis=0)[None]
        ffn_places = ((0,), (0,), FF)

    qkv, attended, stats, residual, inner_pair, attn_t = attention_forward(
        first, doc_lengths, me, ends, swapped, small, slots, tuple(groups)
    )
    results, y_low, ffn_pair, ffn_turned, dhs, early = feed_forward(
        first, residual, ends, swapped, small, gathered, ffn_places
    )

    wide_block = lambda device, section: 2 * device + section
    down_block = lambda device, section: section * count + device
    ffn_orders = (
        [bits[0], bits[1], SECTION] + bits[2:],
        [bits[0], SECTION, bits[2], bits[1]] + bits[3:],
    )
    attn_orders = (
        [bits[0], bits[1], bits[2], SECTION] + bits[3:],
        [bits[0], bits[2], bits[1], SECTION] + bits[3:],
    )
    groups = [(ffn_orders[0], wide_block), (ffn_orders[1], lambda d, s: down_block(d, s) + devices)]
    of_kind = lambda i, m: i // 2
    lefts = ffn_turned.reshape(2 * devices, half, L)
    sent, _ = weight_grad(
        me, lefts, count, ffn_pair, groups, 1, False, of_kind, [], "ffn_grad_sent"
    )
    do, delta, turned, inner_pair, out_low = inner_back(
        dhs, attended, small, attn_t, inner_pair, sent
    )
    moved = [swap_bit(s, *o[0]) for s, o in zip(sent, ffn_orders)]
    (low_a, high_a, low_b, high_b), _ = weight_grad(
        me, lefts, count, ffn_pair, groups, 1, False, of_kind, moved, "ffn_grad_kept", [do]
    )
    states = [(low_a, high_a), (low_b, high_b)]
    dq0, dk0, dv0, turned, _ = pair_back(
        0, first, doc_lengths, qkv, do, stats, delta, turned, [high_a, high_b]
    )
    dq1, dk1, dv1, turned, _ = pair_back(
        1, first, doc_lengths, qkv, do, stats, delta, turned
    )
    states = combine(states, [o[1] for o in ffn_orders], [dq1])
    groups = [(order, lambda d, s, g=g: 4 * d + 2 * s + g) for g, order in enumerate(attn_orders)]

    def last_quarter(step, me_ref):
        return jnp.where((step ^ (me_ref[0] >> (len(bits) - 2))) == 3, 1, 0)

    lefts = turned.reshape(2 * devices, half // 2, L)
    attn_sent, token = weight_grad(
        me, lefts, count, inner_pair, groups, 2, True, last_quarter, [],
        "attention_grad_sent", [s for _, s in states],
    )
    grads = (dq0, dk0, dv0, dq1, dk1, dv1)
    results, dx0, low, y_low = input_grad(
        0, 3, first, grads, ends, swapped, dhs, small, attn_t, results, out_low, [token], [y_low]
    )
    returned_x = [lax.ppermute(dx0, "section", [(1, 0)])]
    returned_y = lax.ppermute(y_low, "section", [(0, 1)])
    moved = [swap_bit(s, *o[0]) for s, o in zip(attn_sent, attn_orders)]
    states = combine(states, [o[2] for o in ffn_orders], [dx0])
    (low_a, high_a, low_b, high_b), token = weight_grad(
        me, lefts, count, inner_pair, groups, 2, True, last_quarter, moved,
        "attention_grad_kept", [dx0] + [s for _, s in states],
    )
    attn_states = [(low_a, high_a), (low_b, high_b)]
    states = combine(states, [o[3] for o in ffn_orders], [token])
    results, dx1, low = input_grad(
        3, 1, first, grads, ends, swapped, dhs, small, attn_t, results, low,
        [high_a, high_b] + [s for _, s in states],
    )
    returned_x.append(lax.ppermute(dx1, "section", [(1, 0)]))
    attn_states = combine(
        attn_states, [o[1] for o in attn_orders], [dx1, returned_x[0]]
    )
    for at in range(4, len(ffn_orders[0])):
        states = [reduce_step(s, o[at]) for s, o in zip(states, ffn_orders)]
    first_half, down_grad = states[0][0], states[1][0]
    attn_states = combine(
        attn_states, [o[2] for o in attn_orders],
        returned_x[1:] + [returned_y, first_half, down_grad],
    )
    attn_state = tuple(jnp.concatenate(both, axis=1) for both in zip(*attn_states))
    for pair in attn_orders[0][3:]:
        attn_state = reduce_step(attn_state, pair)
    attn_half = attn_state[0]
    results, token = place_results(first, returned_y, returned_x, results)
    late = owned_grads(attn_half, first_half, down_grad, low, early, [token])
    own_half = jnp.where(is_first, attn_half, first_half)
    other_half = swap_bit(jnp.where(is_first, first_half, attn_half), "section", 0)
    late = sum_everywhere(late)
    turned_wide = [a[0].T for a in (wide_master, wide_moment, wide_square)]
    norm, factor, *news = update_all(
        first, late, own_half, other_half, down_grad, turned_wide + [down_master, down_moment, down_square]
    )
    small_news = adamw(
        small_master, small_moment, small_square,
        late[:22].reshape(SMALL) * factor[0, 0], rate_small, 0.0,
    )
    return (
        results[None],
        *[a.T[None] for a in news[:3]],
        *news[3:6],
        *small_news,
        norm[0, 0],
    )


def solution(mesh):
    wide = P("section", None, "dp")
    down = P(("section", "dp"), None)
    ends = P("section", "dp", None)
    return jax.shard_map(
        shards,
        mesh=mesh,
        in_specs=(ends, P("dp", None), wide, wide, wide, down, down, down, P(), P(), P()),
        out_specs=(ends, wide, wide, wide, down, down, down, P(), P(), P(), P()),
        check_vma=False,
    )
```

```python
import functools

import jax
import jax.numpy as jnp
import numpy as np
from jax import lax
from jax.experimental import pallas as pl
from jax.experimental.pallas import tpu as pltpu
from jax.sharding import PartitionSpec as P

D = 768
FF = 3072
HEADS = 12
HEAD_DIM = 64
PAIRS = HEADS // 2
L = 1024
BLOCK = 256
TILES = L // BLOCK
STEP = 8
CHUNK = 512
WIDE_TILE = 512
FFN_TILE = 256
SMALL_AT = {}
offset = 0
for name, width in (
    ("g1", D), ("b1", D), ("bq", D), ("bv", D), ("gi", D), ("bi", D), ("bo", D), ("g2", D), ("b2", D),
    ("c1", FF), ("gh", FF), ("bh", FF), ("c2", D),
):
    SMALL_AT[name] = (offset, width)
    offset += width
SMALL = offset

eps_norm = 1e-05
clip_limit = 1.0
beta_one = 0.9
beta_two = 0.99
adam_eps = 1e-08
decay_weight = 0.1
rate_wide = 0.05
rate_down = 0.025
rate_small = 0.6
masked_score = -1e30

BOTH = ("section", "dp")
F32 = jnp.float32
BF16 = jnp.bfloat16
NN = ((1,), (0,))
NT = ((1,), (1,))
TN = ((0,), (0,))
VMEM_BYTES = 58 * 2**20


def dot(a, b, dims):
    return lax.dot_general(a, b, (dims, ((), ())), preferred_element_type=F32)


def small_row(small_ref, name, start=0, width=None):
    at, full = SMALL_AT[name]
    return small_ref[:, at + start : at + start + (full if width is None else width)]


def normalise(values):
    row_mean = jnp.mean(values, axis=-1, keepdims=True)
    centred = values - row_mean
    spread = jnp.mean(centred * centred, axis=-1, keepdims=True)
    inverse = lax.rsqrt(spread + eps_norm)
    return centred * inverse, inverse


def normalise_back(grad, gain, unit, inverse):
    scaled = grad * gain
    first = jnp.mean(scaled, axis=-1, keepdims=True)
    second = jnp.mean(scaled * unit, axis=-1, keepdims=True)
    return inverse * (scaled - first - unit * second)


def column_sum(values):
    return jnp.sum(values, axis=0, keepdims=True)


def document_ends(lengths_ref, first_ref):
    row = 1 - first_ref[0]
    ends = [lengths_ref[row, 0]]
    for i in (1, 2):
        ends.append(ends[-1] + lengths_ref[row, i])
    return ends


def visible_bias(ends, query_start, key_start, keys):
    key = key_start + lax.broadcasted_iota(jnp.int32, (keys, BLOCK), 0)
    query = query_start + lax.broadcasted_iota(jnp.int32, (1, BLOCK), 1)
    begin = jnp.zeros((1, BLOCK), jnp.int32)
    for end in ends:
        begin = jnp.where(query >= end, end, begin)
    return jnp.where((key >= begin) & (key <= query), 0.0, masked_score).astype(F32)


def halves(pair):
    lane = lax.broadcasted_iota(jnp.int32, pair.shape, 1)
    zero = jnp.zeros_like(pair)
    return jnp.where(lane < HEAD_DIM, pair, zero), jnp.where(lane < HEAD_DIM, zero, pair)


def first_key(tile):
    return max(0, tile - 2) * BLOCK


def attention_kernel(groups, first_ref, lengths_ref, me_ref, own_ref, swapped_ref, small_ref, *refs):
    slots, refs = refs[: len(groups)], refs[len(groups) :]
    qkv_ref, o_ref, stats_ref, hs_ref, pair_ref, held_ref, *refs = refs
    bias_ref, vt_ref, weights_ref, x_ref, a_ref, sem, x_sem, out_sem = refs

    @pl.when(first_ref[0] == 1)
    def _():
        pltpu.make_async_copy(own_ref.at[pl.ds(0, L)], x_ref, x_sem).start()

    @pl.when(first_ref[0] == 0)
    def _():
        pltpu.make_async_copy(swapped_ref, x_ref, x_sem).start()

    copies = []
    for at, (scale, shift, rows, apart) in enumerate(groups):
        for slot, bits in enumerate(apart):
            target = pl.multiple_of((me_ref[0] ^ bits) * scale + shift, 16)
            copies.append(
                pltpu.make_async_copy(
                    slots[at].at[slot], weights_ref.at[pl.ds(target, rows)], sem
                )
            )
    for copy in copies:
        copy.start()
    for copy in copies:
        copy.wait()
    hold = pltpu.make_async_copy(weights_ref, held_ref, out_sem.at[0])
    hold.start()
    pltpu.make_async_copy(swapped_ref, x_ref, x_sem).wait()

    def project(tile, carry):
        rows = pl.ds(pl.multiple_of(tile * WIDE_TILE, WIDE_TILE), WIDE_TILE)
        unit, _ = normalise(x_ref[rows, :].astype(F32))
        a = (unit * small_row(small_ref, "g1") + small_row(small_ref, "b1")).astype(BF16)
        a_ref[rows, :] = a
        q = (dot(a, weights_ref[:D, :], NT) + small_row(small_ref, "bq")).astype(BF16)
        qkv_ref[rows, :D] = q * jnp.asarray(0.125, BF16)
        qkv_ref[rows, D : 2 * D] = dot(a, weights_ref[D : 2 * D, :], NT).astype(BF16)
        v = (dot(a, weights_ref[2 * D : 3 * D, :], NT) + small_row(small_ref, "bv")).astype(BF16)
        qkv_ref[rows, 2 * D :] = v
        vt_ref[:, rows] = v.T
        return carry

    lax.fori_loop(0, L // WIDE_TILE, project, 0)
    hold_a = pltpu.make_async_copy(a_ref, pair_ref.at[0], out_sem.at[1])
    hold_a.start()
    ends = document_ends(lengths_ref, first_ref)

    for tile in range(TILES):
        start = first_key(tile)
        keys = (tile + 1) * BLOCK - start
        rows = slice(tile * BLOCK, (tile + 1) * BLOCK)
        window = slice(start, start + keys)
        bias_ref[:keys, :] = visible_bias(ends, tile * BLOCK, start, keys)

        def one_pair(pair, carry, rows=rows, window=window, keys=keys):
            at = pl.multiple_of(pair * 128, 128)
            q_parts = halves(qkv_ref[rows, pl.ds(at, 128)])
            k = qkv_ref[window, pl.ds(D + at, 128)]
            vt = vt_ref[pl.ds(at, 128), window]
            weights, tops = [], []
            for q_part in q_parts:
                scores = dot(k, q_part, NT) + bias_ref[:keys, :]
                top = jnp.max(scores, axis=0, keepdims=True)
                weights.append(jnp.exp(scores - top).astype(BF16))
                tops.append(top)
            ones = jnp.ones((16, keys), BF16)
            outs = []
            for i in range(2):
                left = jnp.concatenate([vt[i * HEAD_DIM : (i + 1) * HEAD_DIM], ones], axis=0)
                mixed = dot(left, weights[i], NN)
                total = mixed[HEAD_DIM : HEAD_DIM + 1, :]
                outs.append(mixed[:HEAD_DIM, :] / total)
                stats_ref[pair, i : i + 1, rows] = tops[i] + jnp.log(total)
            o_ref[rows, pl.ds(at, 128)] = jnp.concatenate(outs, axis=0).T
            return carry

        lax.fori_loop(0, PAIRS, one_pair, 0, unroll=2)

    def finish(tile, carry):
        rows = pl.ds(pl.multiple_of(tile * WIDE_TILE, WIDE_TILE), WIDE_TILE)
        unit, _ = normalise(o_ref[rows, :])
        u = (unit * small_row(small_ref, "gi") + small_row(small_ref, "bi")).astype(BF16)
        h = x_ref[rows, :].astype(F32) + dot(u, weights_ref[3 * D :, :], NT)
        hs_ref[rows, :] = (h + small_row(small_ref, "bo")).astype(BF16)
        return carry

    lax.fori_loop(0, L // WIDE_TILE, finish, 0)
    hold.wait()
    hold_a.wait()


def whole(memory_space=pltpu.VMEM):
    return pl.BlockSpec(memory_space=memory_space)


def beside(kernel, inputs, outputs, waits, carried):
    def body(*refs):
        passed = len(waits) + len(carried)
        after_inputs = refs[inputs + passed :]
        kernel(*refs[:inputs], *after_inputs[:outputs], *after_inputs[outputs + len(carried) :])

    return body


def shapes_of(arrays):
    return tuple(jax.ShapeDtypeStruct(a.shape, a.dtype) for a in arrays)


def attention_forward(first, lengths, me, ends_in, swapped, small, slots, groups):
    return pl.pallas_call(
        functools.partial(attention_kernel, groups),
        out_shape=(
            jax.ShapeDtypeStruct((L, 3 * D), BF16),
            jax.ShapeDtypeStruct((L, D), F32),
            jax.ShapeDtypeStruct((PAIRS, 2, L), F32),
            jax.ShapeDtypeStruct((L, D), BF16),
            jax.ShapeDtypeStruct((2, L, D), BF16),
            jax.ShapeDtypeStruct((FF, D), BF16),
        ),
        in_specs=[whole(pltpu.SMEM)] * 3 + [whole(pl.ANY)] * 2 + [whole()]
        + [whole(pl.ANY)] * len(slots),
        out_specs=(whole(),) * 4 + (whole(pl.ANY),) * 2,
        scratch_shapes=[
            pltpu.VMEM((3 * BLOCK, BLOCK), F32),
            pltpu.VMEM((D, L), BF16),
            pltpu.VMEM((FF, D), BF16),
            pltpu.VMEM((L, D), BF16),
            pltpu.VMEM((L, D), BF16),
            pltpu.SemaphoreType.DMA,
            pltpu.SemaphoreType.DMA,
            pltpu.SemaphoreType.DMA((2,)),
        ],
        compiler_params=pltpu.CompilerParams(vmem_limit_bytes=VMEM_BYTES),
        cost_estimate=pl.CostEstimate(flops=14 * 10**9, bytes_accessed=20 * 10**6, transcendentals=0),
        name="attention_forward",
    )(first, lengths, me, ends_in, swapped, small, *slots)


def gelu_parts(x):
    size = jnp.abs(x)
    bell = jnp.exp(x * x * -0.5)
    t = 1.0 / (1.0 + size * (0.3275911 * 0.5**0.5))
    tail = t * (0.5 * 0.254829592 + t * (0.5 * -0.284496736 + t * (
        0.5 * 1.421413741 + t * (0.5 * -1.453152027 + t * (0.5 * 1.061405429)))))
    tail = tail * bell
    phi = jnp.where(x > 0, 1.0 - tail, tail)
    return x * phi, phi + x * bell * 0.3989422804014327


def ffn_kernel(
    places, chosen_ref, hs_ref, lower_ref, swapped_ref, small_ref, slots_ref,
    y_ref, sent_ref, pair_ref, turned_ref, dhs_ref, wide_ref,
    g_ref, slope_ref, t_ref, held_ref, first_ref, second_ref, sems,
):
    first_rows, second_rows, rows = places

    def weight_copies(into_ref, rows_of, start, sem):
        return [
            pltpu.make_async_copy(
                slots_ref.at[block, pl.ds(start, rows)], into_ref.at[pl.ds(row, rows)], sem
            )
            for block, row in enumerate(rows_of)
        ]

    @pl.when(pl.program_id(0) == 0)
    def _():
        wide_ref[...] = jnp.zeros_like(wide_ref)
        copies = weight_copies(first_ref, first_rows, 0, sems.at[0])
        for copy in copies + weight_copies(second_ref, second_rows, rows, sems.at[1]):
            copy.start()
        for copy in copies:
            copy.wait()

    hs = hs_ref[...].astype(F32)
    unit, inverse = normalise(hs)
    e = (unit * small_row(small_ref, "g2") + small_row(small_ref, "b2")).astype(BF16)
    pair_ref[0] = e
    dy = jnp.where(chosen_ref[0] == 1, swapped_ref[...], lower_ref[...])
    pair_ref[1] = dy
    chunks = [slice(j, j + CHUNK) for j in range(0, FF, CHUNK)]

    total = jnp.zeros((FFN_TILE, 1), F32)
    for cut in chunks:
        f = dot(e, first_ref[cut, :], NT) + small_row(small_ref, "c1", cut.start, CHUNK)
        g, slope = gelu_parts(f)
        g_ref[:, cut] = g
        slope_ref[:, cut] = slope
        total = total + jnp.sum(g, axis=1, keepdims=True)
    mean = total / FF
    total = jnp.zeros((FFN_TILE, 1), F32)
    for cut in chunks:
        centred = g_ref[:, cut] - mean
        total = total + jnp.sum(centred * centred, axis=1, keepdims=True)
    inner_inverse = lax.rsqrt(total / FF + eps_norm)

    step = pl.program_id(0)
    columns = pl.ds(pl.multiple_of(step * FFN_TILE, FFN_TILE), FFN_TILE)
    flush = pltpu.make_async_copy(held_ref, turned_ref.at[:, :, columns], sems.at[2])

    @pl.when(step == 0)
    def _():
        for copy in weight_copies(second_ref, second_rows, rows, sems.at[1]):
            copy.wait()

    @pl.when(step > 0)
    def _():
        flush.wait()

    y = hs + small_row(small_ref, "c2")
    first_sum = jnp.zeros((FFN_TILE, 1), F32)
    second_sum = jnp.zeros((FFN_TILE, 1), F32)
    for cut in chunks:
        gain = small_row(small_ref, "gh", cut.start, CHUNK)
        ghat = (g_ref[:, cut] - mean) * inner_inverse
        g_ref[:, cut] = ghat
        n = (ghat * gain + small_row(small_ref, "bh", cut.start, CHUNK)).astype(BF16)
        held_ref[1, cut, :] = n.T
        y = y + dot(n, second_ref[cut, :], NN)
        dn = dot(dy, second_ref[cut, :], NT)
        wide_ref[0:1, cut] += column_sum(dn * ghat)
        wide_ref[1:2, cut] += column_sum(dn)
        scaled = dn * gain
        t_ref[:, cut] = scaled
        first_sum = first_sum + jnp.sum(scaled, axis=1, keepdims=True)
        second_sum = second_sum + jnp.sum(scaled * ghat, axis=1, keepdims=True)
    y_ref[...] = y
    sent_ref[...] = y.astype(BF16)
    first_sum = first_sum / FF
    second_sum = second_sum / FF

    de = jnp.zeros((FFN_TILE, D), F32)
    for cut in chunks:
        back = t_ref[:, cut] - first_sum - g_ref[:, cut] * second_sum
        df = (inner_inverse * back * slope_ref[:, cut]).astype(BF16)
        held_ref[0, cut, :] = df.T
        wide_ref[2:3, cut] += column_sum(df.astype(F32))
        de = de + dot(df, first_ref[cut, :], NN)
    flush.start()

    dyf = dy.astype(F32)
    wide_ref[3:4, :D] += column_sum(de * unit)
    wide_ref[3:4, D : 2 * D] += column_sum(de)
    wide_ref[3:4, 2 * D : 3 * D] += column_sum(dyf)
    dhp = normalise_back(de, small_row(small_ref, "g2"), unit, inverse)
    dhs_ref[...] = (dyf + dhp).astype(BF16)

    @pl.when(step == pl.num_programs(0) - 1)
    def _():
        flush.wait()


def feed_forward(chosen, hs, ends_in, swapped, small, slots, places):
    at = L // FFN_TILE
    tile = lambda shift=0: pl.BlockSpec((FFN_TILE, D), lambda i: (i + shift, 0))
    keep = lambda shape: pl.BlockSpec(shape, lambda i: (0, 0), pipeline_mode=pl.Buffered(1))
    return pl.pallas_call(
        functools.partial(ffn_kernel, places),
        grid=(at,),
        out_shape=(
            jax.ShapeDtypeStruct((2 * L, D), F32),
            jax.ShapeDtypeStruct((L, D), BF16),
            jax.ShapeDtypeStruct((2, L, D), BF16),
            jax.ShapeDtypeStruct((2, FF, L), BF16),
            jax.ShapeDtypeStruct((L, D), BF16),
            jax.ShapeDtypeStruct((4, FF), F32),
        ),
        in_specs=[whole(pltpu.SMEM), tile(), tile(at), tile(), keep((1, SMALL)), whole(pl.ANY)],
        out_specs=(
            tile(at), tile(),
            pl.BlockSpec((2, FFN_TILE, D), lambda i: (0, i, 0)),
            whole(pl.ANY),
            tile(),
            pl.BlockSpec((4, FF), lambda i: (0, 0)),
        ),
        scratch_shapes=[pltpu.VMEM((FFN_TILE, FF), F32)] * 3
        + [pltpu.VMEM((2, FF, FFN_TILE), BF16)]
        + [pltpu.VMEM((FF, D), BF16)] * 2
        + [pltpu.SemaphoreType.DMA((3,))],
        compiler_params=pltpu.CompilerParams(vmem_limit_bytes=VMEM_BYTES),
        cost_estimate=pl.CostEstimate(flops=40 * 10**9, bytes_accessed=30 * 10**6, transcendentals=0),
        name="feed_forward",
    )(chosen, hs, ends_in, swapped, small, slots)


TOKEN = jax.ShapeDtypeStruct((8, 128), F32)


def weight_grad_kernel(plan, me_ref, *refs):
    lefts, right_ref = refs[: plan["lefts"]], refs[plan["lefts"]]
    refs = refs[plan["lefts"] + 1 :]
    moved, outs, token_ref = refs[: plan["moved"]], refs[plan["moved"] : -1], refs[-1]
    rows = lefts[0].shape[1]
    blocks = [ref[0] for ref in lefts]
    token_ref[...] = jnp.zeros_like(token_ref)
    if rows % 16 == 0:
        value = dot(jnp.concatenate(blocks, axis=0), right_ref[0], NN)
        parts = [value[at * rows : (at + 1) * rows] for at in range(len(blocks))]
    else:
        parts = [dot(block, right_ref[0], NN) for block in blocks]
    split = plan["split"]
    step = pl.program_id(0) % 2**split
    kind = pl.program_id(0) // 2**split

    def store(group, parts):
        views = plan["views"][group]
        for at, part in enumerate(parts):
            place = tuple(int(p) for p in np.unravel_index(at, views))
            if not moved:
                outs[group][place] = part.astype(BF16)
                continue
            total = part + moved[group][place].astype(F32)
            low_ref, high_ref = outs[2 * group : 2 * group + 2]
            first_bit = plan["first"][group]
            if first_bit is None:
                if place[0] == 0:
                    low_ref[place[1:]] = total
                else:
                    high_ref[place[1:]] = total.astype(BF16)
                continue

            @pl.when((step >> first_bit) & 1 == 0)
            def _():
                low_ref[place[1:]] = total

            @pl.when((step >> first_bit) & 1 == 1)
            def _():
                high_ref[place[1:]] = total.astype(BF16)

    if plan["joint"]:
        count = len(parts) // 2
        for group in range(2):
            store(group, parts[group * count : (group + 1) * count])
    else:
        for group in range(2):

            @pl.when(kind == group)
            def _():
                store(group, parts)


def weight_grad(me, left, count, right, groups, split, joint, right_of, moved, name, waits=()):
    bits = count.bit_length() - 1
    rows = left.shape[1]
    steps = 2**split
    top = [("dp", bits - 1 - i) for i in range(split)]
    shift = bits - split
    in_specs, outs, out_specs, views, firsts, combos = [], [], [], [], [], []
    moved_specs = []

    def row_of(group, combo, step, me_ref):
        order, row_block = groups[group]
        free = [pair for pair in order[1:] if pair not in top]
        apart, across = (0 if moved else 1), 0
        for at, (axis, bit) in enumerate(free):
            on = (combo >> (len(free) - 1 - at)) & 1
            if axis == "dp":
                apart |= on << bit
            else:
                across = on
        return row_block((apart + (step << shift)) ^ me_ref[0], across ^ me_ref[1])

    def local_step(i, group):
        if joint:
            return i
        return jnp.clip(i - group * steps, 0, steps - 1)

    free_count = 2 ** (len(groups[0][0]) - 1 - split)
    if joint:
        for group in range(2):
            for combo in range(free_count):
                in_specs.append(
                    pl.BlockSpec(
                        (1, rows, L),
                        lambda i, m, g=group, c=combo: (row_of(g, c, i, m), 0, 0),
                    )
                )
    else:
        for combo in range(free_count):

            def place(i, m, c=combo):
                step = i % steps
                return jnp.where(i < steps, row_of(0, c, step, m), row_of(1, c, step, m)), 0, 0

            in_specs.append(pl.BlockSpec((1, rows, L), place))
    lefts = len(in_specs)
    in_specs.append(pl.BlockSpec((1, L, D), lambda i, m: (right_of(i, m), 0, 0)))

    for group, (order, _) in enumerate(groups):
        order = order[1:]

        def spots(i, m, pairs=order, group=group):
            step = local_step(i, group)
            return (*[(step >> (p[1] - shift)) & 1 if p in top else 0 for p in pairs], 0, 0)

        view = tuple(1 if pair in top else 2 for pair in order)
        views.append(view)
        firsts.append(order[0][1] - shift if order[0] in top else None)
        full = pl.BlockSpec((*view, rows, D), spots)
        if moved:
            moved_specs.append(full)
            half = pl.BlockSpec(
                (*view[1:], rows, D), lambda i, m, spots=spots: spots(i, m)[1:]
            )
            out_specs += [half, half]
            shape = (2,) * (len(order) - 1) + (rows, D)
            outs += [jax.ShapeDtypeStruct(shape, F32), jax.ShapeDtypeStruct(shape, BF16)]
        else:
            out_specs.append(full)
            outs.append(jax.ShapeDtypeStruct((2,) * len(order) + (rows, D), BF16))
    plan = dict(
        lefts=lefts, moved=len(moved), split=split, views=views, first=firsts, joint=joint
    )
    moved = [m.reshape((2,) * (len(groups[0][0]) - 1) + (rows, D)) for m in moved]
    inputs = len(in_specs) + len(moved) + 1
    *results, token = pl.pallas_call(
        beside(functools.partial(weight_grad_kernel, plan), inputs, len(outs) + 1, waits, ()),
        grid_spec=pltpu.PrefetchScalarGridSpec(
            num_scalar_prefetch=1,
            grid=(steps if joint else 2 * steps,),
            in_specs=in_specs + moved_specs + [whole(pl.ANY)] * len(waits),
            out_specs=tuple(out_specs) + (pl.BlockSpec((8, 128), lambda i, m: (0, 0)),),
        ),
        out_shape=tuple(outs) + (TOKEN,),
        compiler_params=pltpu.CompilerParams(vmem_limit_bytes=VMEM_BYTES),
        cost_estimate=pl.CostEstimate(flops=6 * 10**9, bytes_accessed=9 * 10**6, transcendentals=0),
        name=name,
    )(me, *[left] * lefts, right, *moved, *waits)
    return [r.reshape(-1, rows, D) for r in results], token


def inner_back_kernel(
    dhs_ref, o_ref, small_ref, weights_ref, pair_ref, do_ref, delta_ref, turned_ref, u_ref, low_ref
):
    @pl.when(pl.program_id(0) == 0)
    def _():
        low_ref[...] = jnp.zeros_like(low_ref)

    o = o_ref[...]
    unit, inverse = normalise(o)
    gain = small_row(small_ref, "gi")
    u_ref[0] = (unit * gain + small_row(small_ref, "bi")).astype(BF16)
    dhs = dhs_ref[...]
    turned_ref[0] = dhs.T
    du = dot(dhs, weights_ref[...], NN)
    low_ref[4:5, :] += column_sum(du * unit)
    low_ref[5:6, :] += column_sum(du)
    low_ref[6:7, :] += column_sum(dhs.astype(F32))
    do = normalise_back(du, gain, unit, inverse).astype(BF16)
    do_ref[...] = do
    product = (do.astype(F32) * o).T
    for head in range(HEADS):
        delta_ref[head // 2, head % 2 : head % 2 + 1, :] = column_sum(
            product[head * HEAD_DIM : (head + 1) * HEAD_DIM, :]
        )


def inner_back(dhs, o, small, weights, pair, waits=()):
    tile = lambda width: pl.BlockSpec((BLOCK, width), lambda i: (i, 0))
    return pl.pallas_call(
        beside(inner_back_kernel, 5, 5, waits, ()),
        grid=(TILES,),
        out_shape=(
            jax.ShapeDtypeStruct((L, D), BF16),
            jax.ShapeDtypeStruct((PAIRS, 2, L), F32),
            jax.ShapeDtypeStruct((4, D, L), BF16),
            jax.ShapeDtypeStruct((2, L, D), BF16),
            jax.ShapeDtypeStruct((8, D), F32),
        ),
        in_specs=[
            tile(D),
            tile(D),
            pl.BlockSpec((1, SMALL), lambda i: (0, 0), pipeline_mode=pl.Buffered(1)),
            pl.BlockSpec((D, D), lambda i: (3, 0), pipeline_mode=pl.Buffered(1)),
            whole(pl.ANY),
        ]
        + [whole(pl.ANY)] * len(waits),
        out_specs=(
            tile(D),
            pl.BlockSpec((PAIRS, 2, BLOCK), lambda i: (0, 0, i)),
            pl.BlockSpec((1, D, BLOCK), lambda i: (3, 0, i)),
            pl.BlockSpec((1, BLOCK, D), lambda i: (1, i, 0)),
            pl.BlockSpec((8, D), lambda i: (0, 0)),
        ),
        input_output_aliases={4: 3},
        compiler_params=pltpu.CompilerParams(vmem_limit_bytes=VMEM_BYTES),
        cost_estimate=pl.CostEstimate(flops=6 * 10**9, bytes_accessed=15 * 10**6, transcendentals=0),
        name="inner_back",
    )(dhs, o, small, weights, pair, *waits)


GROUP = 3


def pair_back_kernel(
    first_ref, lengths_ref, q_ref, k_ref, v_ref, do_ref, stats_ref, delta_ref, earlier_ref,
    dq_ref, dk_ref, dv_ref, turned_ref, token_ref, bias_ref, dk_sum, dv_sum,
):
    token_ref[...] = jnp.zeros_like(token_ref)

    @pl.when(pl.program_id(0) == 0)
    def _():
        ends = document_ends(lengths_ref, first_ref)
        for tile in range(TILES):
            start = first_key(tile)
            keys = (tile + 1) * BLOCK - start
            bias_ref[tile, :keys, :] = visible_bias(ends, tile * BLOCK, start, keys)

    dk_sum[...] = jnp.zeros_like(dk_sum)
    dv_sum[...] = jnp.zeros_like(dv_sum)
    for tile in range(TILES):
        start = first_key(tile)
        keys = (tile + 1) * BLOCK - start
        rows = slice(tile * BLOCK, (tile + 1) * BLOCK)
        window = slice(start, start + keys)
        q_parts = halves(q_ref[rows, :])
        do_parts = halves(do_ref[rows, :])
        k = k_ref[window, :]
        v = v_ref[window, :]
        kt = k.T
        dqs = []
        for i in range(2):
            scores = dot(k, q_parts[i], NT) + bias_ref[tile, :keys, :]
            probs = jnp.exp(scores - stats_ref[0, i : i + 1, rows])
            dprobs = dot(v, do_parts[i], NT)
            ds = (probs * (dprobs - delta_ref[0, i : i + 1, rows])).astype(BF16)
            dv_sum[window, :] += dot(probs.astype(BF16), do_parts[i], NN)
            dk_sum[window, :] += dot(ds, q_parts[i], NN)
            dqs.append(dot(kt[i * HEAD_DIM : (i + 1) * HEAD_DIM], ds, NN))
        dq = (jnp.concatenate(dqs, axis=0) * 0.125).astype(BF16)
        turned_ref[0, :, rows] = dq
        dq_ref[rows, :] = dq.T
    for part, sum_ref, out_ref in ((1, dk_sum, dk_ref), (2, dv_sum, dv_ref)):
        grad = sum_ref[...].astype(BF16)
        out_ref[...] = grad
        turned_ref[part] = grad.T


def pair_back(part, first_flag, lengths, qkv, do, stats, delta, turned, waits=()):
    first = part * GROUP
    column = lambda base: pl.BlockSpec((L, 128), lambda i: (0, base + first + i))
    rows = pl.BlockSpec((1, 2, L), lambda i: (first + i, 0, 0))
    out = pl.BlockSpec((L, 128), lambda i: (0, i))
    width = GROUP * 128
    return pl.pallas_call(
        beside(pair_back_kernel, 9, 5, waits, ()),
        grid=(GROUP,),
        out_shape=(jax.ShapeDtypeStruct((L, width), BF16),) * 3
        + (jax.ShapeDtypeStruct((4, D, L), BF16), TOKEN),
        in_specs=[
            whole(pltpu.SMEM), whole(pltpu.SMEM), column(0), column(PAIRS), column(2 * PAIRS), column(0), rows, rows,
            whole(pl.ANY),
        ]
        + [whole(pl.ANY)] * len(waits),
        out_specs=(out,) * 3 + (
            pl.BlockSpec((3, 128, L), lambda i: (0, first + i, 0)),
            pl.BlockSpec((8, 128), lambda i: (0, 0)),
        ),
        input_output_aliases={8: 3},
        scratch_shapes=[
            pltpu.VMEM((TILES, 3 * BLOCK, BLOCK), F32),
            pltpu.VMEM((L, 128), F32),
            pltpu.VMEM((L, 128), F32),
        ],
        compiler_params=pltpu.CompilerParams(vmem_limit_bytes=VMEM_BYTES),
        cost_estimate=pl.CostEstimate(flops=13 * 10**9, bytes_accessed=15 * 10**6, transcendentals=0),
        name="pair_back",
    )(first_flag, lengths, qkv, qkv, qkv, do, stats, delta, turned, *waits)


def input_grad_kernel(
    first_ref, dq0, dk0, dv0, dq1, dk1, dv1, own_ref, swapped_ref, dhs_ref, small_ref, weights_ref,
    results_ref, earlier_ref, dx_ref, sent_ref, low_ref,
):
    @pl.when(pl.program_id(0) == 0)
    def _():
        low_ref[...] = earlier_ref[...]

    x = jnp.where(first_ref[0] == 1, own_ref[...], swapped_ref[...])
    unit, inverse = normalise(x.astype(F32))
    gain = small_row(small_ref, "g1")
    grads = [ref[...] for ref in (dq0, dq1, dk0, dk1, dv0, dv1)]
    width = GROUP * 128
    da = dot(jnp.concatenate(grads, axis=1), weights_ref[...], NN)
    for at, grad in enumerate(grads):
        if at < 2 or at > 3:
            row = 2 if at < 2 else 3
            cut = slice((at % 2) * width, (at % 2 + 1) * width)
            low_ref[row : row + 1, cut] += column_sum(grad.astype(F32))
    low_ref[0:1, :] += column_sum(da * unit)
    low_ref[1:2, :] += column_sum(da)
    dx = normalise_back(da, gain, unit, inverse) + dhs_ref[...].astype(F32)
    dx_ref[...] = dx
    sent_ref[...] = dx.astype(BF16)


def input_grad(start, tiles, first, grads, ends_in, swapped, dhs, small, weights, results, earlier, waits=(), carried=()):
    tile = lambda width: pl.BlockSpec((BLOCK, width), lambda i: (i + start, 0))
    keep = lambda shape: pl.BlockSpec(shape, lambda i: (0, 0), pipeline_mode=pl.Buffered(1))
    return pl.pallas_call(
        beside(input_grad_kernel, 14, 3, waits, carried),
        grid=(tiles,),
        out_shape=(
            jax.ShapeDtypeStruct((2 * L, D), F32),
            jax.ShapeDtypeStruct((tiles * BLOCK, D), BF16),
            jax.ShapeDtypeStruct((8, D), F32),
        )
        + shapes_of(carried),
        in_specs=[whole(pltpu.SMEM)] + [tile(GROUP * 128)] * 6
        + [tile(D)] * 3 + [keep((1, SMALL)), keep((3 * D, D))]
        + [whole(pl.ANY), keep((8, D))]
        + [whole(pl.ANY)] * (len(waits) + len(carried)),
        out_specs=(
            tile(D),
            pl.BlockSpec((BLOCK, D), lambda i: (i, 0)),
            pl.BlockSpec((8, D), lambda i: (0, 0)),
        )
        + (whole(pl.ANY),) * len(carried),
        input_output_aliases={12: 0} | {14 + len(waits) + i: 3 + i for i in range(len(carried))},
        compiler_params=pltpu.CompilerParams(vmem_limit_bytes=VMEM_BYTES),
        cost_estimate=pl.CostEstimate(flops=4 * 10**9, bytes_accessed=10 * 10**6, transcendentals=0),
        name="input_grad",
    )(first, *grads, ends_in, swapped, dhs, small, weights, results, earlier, *waits, *carried)


def place_kernel(first_ref, y_ref, dx0_ref, dx1_ref, results_ref, out_ref, token_ref):
    token_ref[...] = jnp.zeros_like(token_ref)
    is_dx = first_ref[0] == 1
    step = pl.program_id(0)

    @pl.when(step == 0)
    def _():
        out_ref[...] = jnp.where(is_dx, dx0_ref[:WIDE_TILE, :], y_ref[...]).astype(F32)

    @pl.when(step == 1)
    def _():
        dx = jnp.concatenate([dx0_ref[WIDE_TILE:, :], dx1_ref[...]], axis=0)
        out_ref[...] = jnp.where(is_dx, dx, y_ref[...]).astype(F32)


def place_results(first, y, dx, results):
    tile = pl.BlockSpec((WIDE_TILE, D), lambda i, f: (i, 0))
    return pl.pallas_call(
        place_kernel,
        grid_spec=pltpu.PrefetchScalarGridSpec(
            num_scalar_prefetch=1,
            grid=(L // WIDE_TILE,),
            in_specs=[tile] + [pl.BlockSpec(d.shape, lambda i, f: (0, 0)) for d in dx]
            + [whole(pl.ANY)],
            out_specs=(
                pl.BlockSpec((WIDE_TILE, D), lambda i, f: (i + f[0] * (L // WIDE_TILE), 0)),
                pl.BlockSpec((8, 128), lambda i, f: (0, 0)),
            ),
        ),
        out_shape=(jax.ShapeDtypeStruct((2 * L, D), F32), TOKEN),
        input_output_aliases={4: 0},
        cost_estimate=pl.CostEstimate(flops=10**6, bytes_accessed=8 * 10**6, transcendentals=0),
        name="place_results",
    )(first, y, *dx, results)


def combine_kernel(groups, *refs):
    inputs, outputs = refs[: 4 * groups], refs[4 * groups :]
    for g in range(groups):
        low, high, low_in, high_in = inputs[4 * g : 4 * g + 4]
        kept_ref, sent_ref = outputs[2 * g : 2 * g + 2]
        kept_ref[...] = low[...] + low_in[...].astype(F32)
        sent_ref[...] = (high[...] + high_in[...].astype(F32)).astype(BF16)


def combine(states, bits, waits=()):
    moved = [swap_bit(sent, *bit) for (_, sent), bit in zip(states, bits)]
    half = states[0][0].shape[0] // 2
    steps = min(half, 2)
    block = (half // steps,) + states[0][0].shape[1:]
    operands, in_specs, out_shape, out_specs = [], [], [], []
    lower = pl.BlockSpec(block, lambda i: (i, 0, 0))
    upper = pl.BlockSpec(block, lambda i: (i + steps, 0, 0))
    for (kept, _), other in zip(states, moved):
        operands += [kept, kept, other, other]
        in_specs += [lower, upper, lower, upper]
        shape = (half,) + kept.shape[1:]
        out_shape += [jax.ShapeDtypeStruct(shape, F32), jax.ShapeDtypeStruct(shape, BF16)]
        out_specs += [lower, lower]
    outs = pl.pallas_call(
        beside(
            functools.partial(combine_kernel, len(states)), len(operands), len(out_shape), waits, ()
        ),
        grid=(steps,),
        in_specs=in_specs + [whole(pl.ANY)] * len(waits),
        out_specs=tuple(out_specs),
        out_shape=tuple(out_shape),
        compiler_params=pltpu.CompilerParams(vmem_limit_bytes=VMEM_BYTES),
        cost_estimate=pl.CostEstimate(flops=10**6, bytes_accessed=8 * 10**6, transcendentals=0),
        name="combine",
    )(*operands, *waits)
    return [(outs[2 * g], outs[2 * g + 1]) for g in range(len(states))]


def owned_kernel(attn_ref, first_ref, down_ref, low_ref, early_ref, late_ref):
    total = jnp.zeros((1, 1), F32)
    for ref in (attn_ref, first_ref, down_ref):
        total = total + jnp.sum(column_sum(ref[...] * ref[...]), axis=1, keepdims=True)
    late_ref[...] = jnp.zeros_like(late_ref)
    late_ref[:7, :] = low_ref[:7, :]
    order = [(3, 0), (3, 1)] + [(row, part) for row in (2, 0, 1) for part in range(4)] + [(3, 2)]
    for at, (row, part) in enumerate(order):
        late_ref[7 + at : 8 + at, :] = early_ref[row : row + 1, part * D : (part + 1) * D]
    late_ref[22:23, :] = jnp.broadcast_to(total, (1, D))


def owned_grads(attn, first, down, low, early, waits):
    return pl.pallas_call(
        beside(owned_kernel, 5, 1, waits, ()),
        in_specs=[whole()] * 5 + [whole(pl.ANY)] * len(waits),
        out_specs=whole(),
        out_shape=jax.ShapeDtypeStruct((24, D), F32),
        name="owned_grads",
    )(attn, first, down, low, early, *waits)


def update_kernel(first_ref, late_ref, own_ref, other_ref, down_ref, *refs):
    states, norm_ref, factor_ref, outs = refs[:6], refs[6], refs[7], refs[8:]
    grads = late_ref[:22, :]
    norm = jnp.sqrt(late_ref[22:23, 0:1] + jnp.sum(column_sum(grads * grads), axis=1, keepdims=True))
    factor = clip_limit / jnp.maximum(norm, clip_limit)
    norm_ref[...] = norm
    factor_ref[...] = factor
    half = own_ref.shape[0]
    upper = jnp.where(first_ref[0] == 1, own_ref[...], other_ref[...])
    lower = jnp.where(first_ref[0] == 1, other_ref[...], own_ref[...])
    jobs = (
        (0, slice(0, half), upper, rate_wide),
        (0, slice(half, 2 * half), lower, rate_wide),
        (1, slice(0, half), down_ref[...], rate_down),
    )
    for kind, rows, grad, rate in jobs:
        master, moment, square = [ref[rows, :] for ref in states[3 * kind : 3 * kind + 3]]
        news = adamw(master, moment, square, grad * factor, rate, decay_weight)
        for new, out_ref in zip(news, outs[3 * kind : 3 * kind + 3]):
            out_ref[rows, :] = new


def update_all(first, late, own, other, down, states):
    scalar = jax.ShapeDtypeStruct((1, 1), F32)
    return pl.pallas_call(
        update_kernel,
        in_specs=[whole(pltpu.SMEM)] + [whole()] * 10,
        out_specs=(whole(),) * 8,
        out_shape=(scalar, scalar) + shapes_of(states),
        compiler_params=pltpu.CompilerParams(vmem_limit_bytes=VMEM_BYTES),
        name="update_all",
    )(first, late, own, other, down, *states)


SECTION = ("section", 0)


def swap_bit(value, axis, bit):
    mask = 2**bit
    return lax.ppermute(value, axis, [(i, i ^ mask) for i in range(lax.axis_size(axis))])


def swap_mask(value, mask):
    pairs = [(i, i ^ mask) for i in range(2 * lax.axis_size("dp"))]
    return lax.ppermute(value, BOTH, pairs)


def sum_everywhere(value):
    size = lax.axis_size("dp")
    masks = [1, size] + [2**b for b in range(1, size.bit_length() - 1)]
    while masks:
        if len(masks) % 2 == 1:
            value = value + swap_mask(value, masks.pop(0))
            continue
        one, two = masks.pop(0), masks.pop(0)
        across = [swap_mask(value, mask) for mask in (one, two, one | two)]
        value = (value + across[0]) + (across[1] + across[2])
    return value


def axis_bits():
    return [("dp", b) for b in range(lax.axis_size("dp").bit_length() - 1)]


def plane_patterns(order):
    slot = np.arange(2 ** len(order), dtype=np.int32)
    apart = np.zeros_like(slot)
    for at, (_, bit) in enumerate(order):
        apart |= ((slot >> at) & 1) << bit
    return tuple(int(a) for a in apart)


def gather_steps(own, order):
    held = own
    for axis, bit in order:
        held = jnp.concatenate([held, swap_bit(held, axis, bit)], axis=0)
    return held


def reduce_step(state, bit):
    kept, sent = state
    moved = swap_bit(sent, *bit).astype(F32)
    half = kept.shape[0] // 2
    if half == 0:
        return kept[0] + moved[0], None
    return kept[:half] + moved[:half], (kept[half:] + moved[half:]).astype(BF16)


def after(values, *others):
    return lax.optimization_barrier((values, others))[0]


def adamw(master, moment, square, clipped, step_rate, decay):
    moment_new = beta_one * moment + (1.0 - beta_one) * clipped
    square_new = beta_two * square + (1.0 - beta_two) * clipped * clipped
    moment_hat = moment_new / (1.0 - beta_one**STEP)
    square_hat = square_new / (1.0 - beta_two**STEP)
    master_new = master - step_rate * (
        moment_hat / (jnp.sqrt(square_hat) + adam_eps) + decay * master
    )
    return (moment_new, square_new, master_new)


def shards(
    layer_ends,
    doc_lengths,
    wide_master,
    wide_moment,
    wide_square,
    down_master,
    down_moment,
    down_square,
    small_master,
    small_moment,
    small_square,
):
    is_first = lax.axis_index("section") == 0
    count = lax.axis_size("dp")
    devices = 2 * count
    wide_rows = FF // count
    half_rows = wide_rows // 2
    small = small_master.reshape(1, SMALL)
    bits = axis_bits()
    reduce_orders = (bits, [bits[0], bits[2], bits[1]] + bits[3:])
    gather_orders = tuple(order[::-1] for order in reduce_orders)
    device = np.arange(count)
    half = half_rows

    own = wide_master[0].T.astype(BF16)
    other = swap_bit(own, "section", 0)
    attn_own = jnp.where(is_first, own, other)
    first_own = jnp.where(is_first, other[:half], own[half:])
    gathered = lax.all_gather(
        jnp.concatenate([first_own, down_master.astype(BF16)], axis=0), BOTH, axis=0, tiled=False
    )

    first = is_first.astype(jnp.int32)[None]
    me = jnp.stack([lax.axis_index("dp"), lax.axis_index("section")]).astype(jnp.int32)
    ends = layer_ends[0]
    to_swap = after(jnp.where(is_first, ends[L:], ends[:L]), other)
    swapped = swap_bit(to_swap, "section", 0)

    shared = 0
    while gather_orders[0][shared] == gather_orders[1][shared]:
        shared += 1
    held = gather_steps(attn_own[None], gather_orders[0][:shared])
    parts = [
        gather_steps(held[:, g * half : (g + 1) * half], gather_orders[g][shared:-1])
        for g in range(2)
    ]
    parts[1] = after(parts[1], swapped)
    slots, groups = [], []
    for g, order in enumerate(gather_orders):
        patterns = plane_patterns(order[:-1])
        for part, bit in ((parts[g], 0), (swap_bit(parts[g], *order[-1]), 1)):
            slots.append(part)
            groups.append((wide_rows, g * half, half, tuple(p ^ bit for p in patterns)))
    block = np.arange(devices)
    first_rows = (block % count) * wide_rows + (block // count) * half
    ffn_places = (tuple(int(r) for r in first_rows), tuple(int(b) * half for b in block), half)
    if half % 16 != 0:
        whole_attn = jnp.zeros((FF, D), BF16)
        for part, (scale, shift, _, apart) in zip(slots, groups):
            for slot, bits_apart in enumerate(apart):
                row = (lax.axis_index("dp") ^ bits_apart) * scale + shift
                whole_attn = lax.dynamic_update_slice(whole_attn, part[slot], (row, 0))
        slots, groups = [whole_attn[None]], [(0, 0, FF, (0,))]
        first_all = gathered[:, :half].reshape(2, count, half, D).transpose(1, 0, 2, 3)
        second_all = gathered[:, half:].reshape(FF, D)
        gathered = jnp.concatenate([first_all.reshape(FF, D), second_all], axis=0)[None]
        ffn_places = ((0,), (0,), FF)

    qkv, attended, stats, residual, inner_pair, attn_t = attention_forward(
        first, doc_lengths, me, ends, swapped, small, slots, tuple(groups)
    )
    results, y_low, ffn_pair, ffn_turned, dhs, early = feed_forward(
        first, residual, ends, swapped, small, gathered, ffn_places
    )

    wide_block = lambda device, section: 2 * device + section
    down_block = lambda device, section: section * count + device
    ffn_orders = (
        [bits[0], bits[1], SECTION] + bits[2:],
        [bits[0], SECTION, bits[2], bits[1]] + bits[3:],
    )
    attn_orders = (
        [bits[0], bits[1], bits[2], SECTION] + bits[3:],
        [bits[0], bits[2], bits[1], SECTION] + bits[3:],
    )
    groups = [(ffn_orders[0], wide_block), (ffn_orders[1], lambda d, s: down_block(d, s) + devices)]
    of_kind = lambda i, m: i // 2
    lefts = ffn_turned.reshape(2 * devices, half, L)
    sent, _ = weight_grad(
        me, lefts, count, ffn_pair, groups, 1, False, of_kind, [], "ffn_grad_sent"
    )
    do, delta, turned, inner_pair, out_low = inner_back(
        dhs, attended, small, attn_t, inner_pair, sent
    )
    moved = [swap_bit(s, *o[0]) for s, o in zip(sent, ffn_orders)]
    (low_a, high_a, low_b, high_b), _ = weight_grad(
        me, lefts, count, ffn_pair, groups, 1, False, of_kind, moved, "ffn_grad_kept", [do]
    )
    states = [(low_a, high_a), (low_b, high_b)]
    dq0, dk0, dv0, turned, _ = pair_back(
        0, first, doc_lengths, qkv, do, stats, delta, turned, [high_a, high_b]
    )
    dq1, dk1, dv1, turned, _ = pair_back(
        1, first, doc_lengths, qkv, do, stats, delta, turned
    )
    states = combine(states, [o[1] for o in ffn_orders], [dq1])
    groups = [(order, lambda d, s, g=g: 4 * d + 2 * s + g) for g, order in enumerate(attn_orders)]

    def last_quarter(step, me_ref):
        return jnp.where((step ^ (me_ref[0] >> (len(bits) - 2))) == 3, 1, 0)

    lefts = turned.reshape(2 * devices, half // 2, L)
    attn_sent, token = weight_grad(
        me, lefts, count, inner_pair, groups, 2, True, last_quarter, [],
        "attention_grad_sent", [s for _, s in states],
    )
    grads = (dq0, dk0, dv0, dq1, dk1, dv1)
    results, dx0, low, y_low = input_grad(
        0, 3, first, grads, ends, swapped, dhs, small, attn_t, results, out_low, [token], [y_low]
    )
    returned_x = [lax.ppermute(dx0, "section", [(1, 0)])]
    returned_y = lax.ppermute(y_low, "section", [(0, 1)])
    moved = [swap_bit(s, *o[0]) for s, o in zip(attn_sent, attn_orders)]
    states = combine(states, [o[2] for o in ffn_orders], [dx0])
    (low_a, high_a, low_b, high_b), token = weight_grad(
        me, lefts, count, inner_pair, groups, 2, True, last_quarter, moved,
        "attention_grad_kept", [dx0] + [s for _, s in states],
    )
    attn_states = [(low_a, high_a), (low_b, high_b)]
    states = combine(states, [o[3] for o in ffn_orders], [token])
    results, dx1, low = input_grad(
        3, 1, first, grads, ends, swapped, dhs, small, attn_t, results, low,
        [high_a, high_b] + [s for _, s in states],
    )
    returned_x.append(lax.ppermute(dx1, "section", [(1, 0)]))
    attn_states = combine(
        attn_states, [o[1] for o in attn_orders], [dx1, returned_x[0]]
    )
    for at in range(4, len(ffn_orders[0])):
        states = [reduce_step(s, o[at]) for s, o in zip(states, ffn_orders)]
    first_half, down_grad = states[0][0], states[1][0]
    attn_states = combine(
        attn_states, [o[2] for o in attn_orders],
        returned_x[1:] + [returned_y, first_half, down_grad],
    )
    attn_state = tuple(jnp.concatenate(both, axis=1) for both in zip(*attn_states))
    for pair in attn_orders[0][3:]:
        attn_state = reduce_step(attn_state, pair)
    attn_half = attn_state[0]
    results, token = place_results(first, returned_y, returned_x, results)
    late = owned_grads(attn_half, first_half, down_grad, low, early, [token])
    own_half = jnp.where(is_first, attn_half, first_half)
    other_half = swap_bit(jnp.where(is_first, first_half, attn_half), "section", 0)
    late = sum_everywhere(late)
    turned_wide = [a[0].T for a in (wide_master, wide_moment, wide_square)]
    norm, factor, *news = update_all(
        first, late, own_half, other_half, down_grad, turned_wide + [down_master, down_moment, down_square]
    )
    small_news = adamw(
        small_master, small_moment, small_square,
        late[:22].reshape(SMALL) * factor[0, 0], rate_small, 0.0,
    )
    return (
        results[None],
        *[a.T[None] for a in news[:3]],
        *news[3:6],
        *small_news,
        norm[0, 0],
    )


def solution(mesh):
    wide = P("section", None, "dp")
    down = P(("section", "dp"), None)
    ends = P("section", "dp", None)
    return jax.shard_map(
        shards,
        mesh=mesh,
        in_specs=(ends, P("dp", None), wide, wide, wide, down, down, down, P(), P(), P()),
        out_specs=(ends, wide, wide, wide, down, down, down, P(), P(), P(), P()),
        check_vma=False,
    )
```
